32 devices in a mesh: member: 2 (over x), lat: 8 (over z, y), lon: 2 (over core).
Axes of the slice: x: 2, y: 2, z: 4, core: 2. Of those that a mesh axis runs over, the one named last changes fastest.
Arguments:
- tokens: bfloat16 [128, 192, 1024], P(('member', 'lat'), 'lon'), parts along dimension 0, may hold values from -6 to 6
- ln_gain: float32 [1024], replicated, may hold values from 0.5 to 1.5
- w_query: bfloat16 [1024, 1024], replicated, may hold values from -3 to 3
- w_keyval: bfloat16 [1024, 2048], replicated, may hold values from -3 to 3
- w_out: bfloat16 [1024, 1024], replicated, may hold values from -0.1875 to 0.1875
- w_dec: bfloat16 [1024, 512], replicated, may hold values from -0.1875 to 0.1875
- nudge: float32 [32], replicated, may hold values from 0.2 to 1
- state: float32 [32, 512, 768], P(None, ('member', 'lat'), 'lon'), parts along dimension 1, may hold values from -6 to 6
Outputs:
- advanced: float32 [32, 512, 768], P(None, ('member', 'lat', 'lon')), parts along dimension 1
The draws below stay inside these ranges and needn't reach their ends.
There are 2 independent parts, one for each index of `member`. The reference program is written for one: setup_inputs(seed, part) draws one part's arguments, and reference() takes and returns one part's arrays. A program takes and returns all parts, laid end to end along the dimension named above; an argument that names none is the same for every part. Nothing has to cross between parts.
All inputs are finite; a program needn't handle non-finite values.
Results may differ from the reference program's by a relative error of at most 0.003.
Values may be sent and summed in bfloat16 or wider, within the bound.
No kernel may reach another device: no remote copies, remote signals or barrier semaphores. Data moves between devices by JAX's collectives and lax.ppermute only.
A program may use at most 128 MiB of HBM per device.

```python
import math
import jax
import jax.numpy as jnp
from jax import lax

D = 1024
HEADS = 16
WIN = 8
PATCH = 4
VARS = 4
LEV = 8
LON_PIX = 768
KEEP = 256
CH = 32
NTR = 64
NTC = 192
NLAT_PIX = 256


def paired_weights(key):
    base_key = jax.random.fold_in(key, 1234)
    key_keys, key_query = jax.random.split(base_key, 2)
    keyval_raw = jax.random.normal(key_keys, (D, 2 * D), jnp.float32) / math.sqrt(D)
    query_raw = jax.random.normal(key_query, (D, D), jnp.float32) / math.sqrt(D)
    return (jnp.clip(query_raw, -3.0, 3.0), jnp.clip(keyval_raw, -3.0, 3.0))


def draw_w_query(key, part):
    return paired_weights(key)[0].astype(jnp.bfloat16)


def draw_w_keyval(key, part):
    return paired_weights(key)[1].astype(jnp.bfloat16)


def block_scale(key, dims, pieces, least, largest):
    def one(axis_at, parts):
        heights = jax.random.uniform(jax.random.fold_in(jax.random.fold_in(key, 6), axis_at), (parts,), jnp.float32, least / len(pieces), largest / len(pieces))
        return jnp.repeat(jnp.exp(heights), dims[axis_at] // parts).reshape((-1,) + (1,) * (len(dims) - axis_at - 1))

    gain = one(*pieces[0])
    for cut in pieces[1:]:
        gain = gain * one(*cut)
    return gain


def normal_values(own_key, shape, deviation, limit, cuts=(), held_as=jnp.bfloat16):
    result = jax.random.normal(own_key, shape, jnp.float32) * deviation
    if len(cuts) > 0:
        result = block_scale(own_key, shape, cuts, -0.22, 0.18) * result
    return jnp.clip(result, min=-limit, max=limit).astype(held_as)


def setup_inputs(seed: int = 0, part: int = 0) -> dict:
    splits = jax.random.split(jax.random.key(seed), 9)
    part_keys = jax.random.split(jax.random.fold_in(splits[8], part), 9)
    return {
        "tokens": normal_values(part_keys[0], (NTR, NTC, D), 1.0, 6.0, ((0, 8), (1, 2))),
        "ln_gain": jnp.clip(1.0 + 0.1 * jax.random.normal(splits[1], (D,), jnp.float32), 0.5, 1.5),
        "w_query": draw_w_query(jax.random.fold_in(splits[8], 71), part),
        "w_keyval": draw_w_keyval(jax.random.fold_in(splits[8], 71), part),
        "w_out": normal_values(splits[4], (D, D), D ** -0.5, 0.1875),
        "w_dec": normal_values(splits[5], (D, CH * PATCH * PATCH), D ** -0.5, 0.1875),
        "nudge": jnp.clip(jnp.exp(jax.random.uniform(splits[6], (CH,), jnp.float32, math.log(0.2), math.log(1.0))), 0.2, 1.0),
        "state": normal_values(part_keys[7], (CH, NLAT_PIX, LON_PIX), 1.0, 6.0, ((1, 8), (2, 2)), jnp.float32),
    }


time_step = 0.1
diffusion = 0.5
epsilon = 1e-05

def layer_norm(inputs, gain_vector):
    centred = inputs - lax.optimization_barrier(jnp.mean(inputs, axis=-1, keepdims=True))
    variance = lax.optimization_barrier(jnp.mean(centred * centred, axis=-1, keepdims=True))
    return (centred * lax.rsqrt(variance + epsilon) * gain_vector).astype(jnp.bfloat16)

def to_windows(tensor, row_blocks, col_blocks):
    features = tensor.shape[-1]
    shaped = tensor.reshape(row_blocks, WIN, col_blocks, WIN, features)
    return shaped.transpose(0, 2, 1, 3, 4).reshape(row_blocks * col_blocks, WIN * WIN, features)

def from_windows(tensor, row_blocks, col_blocks):
    features = tensor.shape[-1]
    shaped = tensor.reshape(row_blocks, col_blocks, WIN, WIN, features)
    return shaped.transpose(0, 2, 1, 3, 4).reshape(row_blocks * WIN, col_blocks * WIN, features)

def window_attention(queries, keys_win, values_win, key_valid):
    windows_count, window_cells, model_width = queries.shape
    head_size = model_width // HEADS
    query_heads = queries.astype(jnp.float32).reshape(windows_count, window_cells, HEADS, head_size)
    key_heads = keys_win.astype(jnp.float32).reshape(windows_count, window_cells, HEADS, head_size)
    value_heads = values_win.astype(jnp.float32).reshape(windows_count, window_cells, HEADS, head_size)
    scores = jnp.einsum('wqhd,wkhd->whqk', query_heads, key_heads) / math.sqrt(head_size)
    scores = jnp.where(key_valid[:, None, None, :], scores, -1e+30)
    peak_score = lax.optimization_barrier(jnp.max(scores, axis=-1, keepdims=True))
    weights = jnp.exp(scores - peak_score)
    weights = (weights / lax.optimization_barrier(jnp.sum(weights, axis=-1, keepdims=True))).astype(jnp.bfloat16)
    weights = lax.optimization_barrier(weights).astype(jnp.float32)
    mixed_out = jnp.einsum('whqk,wkhd->wqhd', weights, value_heads)
    return mixed_out.astype(jnp.bfloat16).reshape(windows_count, window_cells, model_width)

def zonal_basis(length, kept_waves):
    columns = jnp.arange(length, dtype=jnp.int32)
    wave_index = jnp.arange(kept_waves, dtype=jnp.int32)
    winding = columns[:, None] * wave_index[None, :] % length
    phases = winding.astype(jnp.float32) * (2.0 * math.pi / length)
    basis_table = jnp.concatenate([jnp.cos(phases), jnp.sin(phases)], axis=1)
    factor = jnp.where(wave_index == 0, 1.0, 2.0).astype(jnp.float32) / length
    return (basis_table, jnp.concatenate([factor, factor]))

def tendency(padded):
    centre = padded[:, 1:-1, 1:-1]
    east_cell = padded[:, 1:-1, 2:]
    west_cell = padded[:, 1:-1, :-2]
    north_cell = padded[:, 2:, 1:-1]
    south_cell = padded[:, :-2, 1:-1]
    field_shape = (VARS, LEV) + centre.shape[1:]
    wind_u = centre[:LEV][None]
    wind_v = centre[LEV:2 * LEV][None]
    advection = wind_u * (east_cell - west_cell).reshape(field_shape) * 0.5
    advection = advection + wind_v * (north_cell - south_cell).reshape(field_shape) * 0.5
    spread_term = diffusion * (east_cell + west_cell + north_cell + south_cell - 4.0 * centre)
    return spread_term - advection.reshape(centre.shape)

def extend_full(field):
    padded_rows = jnp.pad(field, ((0, 0), (1, 1), (0, 0)))
    return jnp.concatenate([padded_rows[..., -1:], padded_rows, padded_rows[..., :1]], axis=2)

def reference(tokens, ln_gain, w_query, w_keyval, w_out, w_dec, nudge, state):
    rows_all, cols_all, model_width = tokens.shape
    half_win = WIN // 2
    padded = jnp.pad(tokens, ((half_win, half_win), (0, 0), (0, 0)))
    padded = jnp.roll(padded, half_win, axis=1)
    inside = jnp.pad(jnp.ones((rows_all,), jnp.int32), (half_win, half_win))
    col_blocks = cols_all // WIN

    def one_band(band_index):
        row_start = (band_index * WIN).astype(jnp.int32)
        token_band = lax.dynamic_slice_in_dim(padded, row_start, WIN, 0)
        row_keep = lax.dynamic_slice_in_dim(inside, row_start, WIN, 0)
        normed = layer_norm(token_band.astype(jnp.float32), ln_gain)
        flat_rows = normed.reshape(WIN * cols_all, model_width)
        queries = jnp.dot(flat_rows, w_query, preferred_element_type=jnp.float32).astype(jnp.bfloat16)
        keyval = jnp.dot(flat_rows, w_keyval, preferred_element_type=jnp.float32).astype(jnp.bfloat16)
        queries = queries.reshape(WIN, cols_all, model_width)
        keyval = keyval.reshape(WIN, cols_all, 2 * model_width)
        keep_grid = jnp.broadcast_to(row_keep[:, None, None], (WIN, cols_all, 1))
        key_valid = to_windows(keep_grid, 1, col_blocks)[..., 0] > 0
        keyval_win = to_windows(keyval, 1, col_blocks)
        outputs = window_attention(to_windows(queries, 1, col_blocks), keyval_win[..., :model_width], keyval_win[..., model_width:], key_valid)
        return from_windows(outputs, 1, col_blocks)
    all_bands = lax.map(one_band, jnp.arange(rows_all // WIN + 1, dtype=jnp.int32))
    attended = all_bands.reshape(rows_all + WIN, cols_all, model_width)[half_win:half_win + rows_all]
    attended = jnp.roll(attended, -half_win, axis=1)
    update = jnp.dot(attended.reshape(-1, model_width), w_out, preferred_element_type=jnp.float32)
    layer_out = (tokens.astype(jnp.float32).reshape(-1, model_width) + update).astype(jnp.bfloat16)
    decoded = jnp.dot(layer_out, w_dec, preferred_element_type=jnp.float32)
    decoded = decoded.reshape(rows_all, cols_all, VARS * LEV, PATCH, PATCH).transpose(2, 0, 3, 1, 4)
    decoded = decoded.reshape(VARS * LEV, rows_all * PATCH, cols_all * PATCH)
    basis_table, factor = zonal_basis(LON_PIX, KEEP)
    difference = (decoded - state).reshape(-1, LON_PIX)
    coefficients = jnp.dot(difference, basis_table, precision=lax.Precision.HIGHEST, preferred_element_type=jnp.float32)
    filtered = jnp.dot(coefficients * factor, basis_table.T, precision=lax.Precision.HIGHEST, preferred_element_type=jnp.float32)
    nudged = state + nudge[:, None, None] * filtered.reshape(state.shape)
    first_section = nudged + time_step * tendency(extend_full(nudged))
    return 0.5 * (nudged + first_section + time_step * tendency(extend_full(first_section)))
```

```python
import functools
import math

import jax
import jax.numpy as jnp
import ml_dtypes
import numpy as np
from jax import lax
from jax.experimental import pallas as pl
from jax.experimental.pallas import tpu as pltpu
from jax.sharding import PartitionSpec as P

HEADS = 16
WIN = 8
PATCH = 4
VARS = 4
LEV = 8
KEEP = 256

time_step = 0.1
diffusion = 0.5
epsilon = 1e-05
HALF = WIN // 2
GROUP = 4
MIB = 1 << 20
F32 = jnp.float32
BF16 = jnp.bfloat16


def zonal_filter(length, kept_waves):
    lag = np.arange(length, dtype=np.float64)
    waves = np.arange(1, kept_waves, dtype=np.float64)
    kernel = 1.0 + 2.0 * np.cos(2.0 * np.pi / length * lag[:, None] * waves[None, :]).sum(1)
    at = (np.arange(length)[:, None] - np.arange(length)[None, :]) % length
    return (kernel / length)[at]


def split_high_low(matrix):
    high = matrix.astype(ml_dtypes.bfloat16)
    low = (matrix - high.astype(np.float64)).astype(ml_dtypes.bfloat16)
    return high, low


def decoded_order(total_cols, parts):
    cols = total_cols // parts
    group_cols = GROUP * WIN
    rows = []
    for part in range(parts):
        lanes = []
        for group in range(cols // group_cols):
            for b in range(PATCH):
                for place in range(group_cols):
                    col = part * cols + group * group_cols + place
                    if place % WIN < HALF:
                        col += WIN
                    lanes.append((col % total_cols) * PATCH + b)
        rows.append(lanes)
    return np.array(rows)


def dot(a, b):
    return lax.dot_general(a, b, (((1,), (0,)), ((), ())), preferred_element_type=F32)


def dot_nt(a, b):
    return lax.dot_general(a, b, (((1,), (1,)), ((), ())), preferred_element_type=F32)


def window_tokens(load, load_next, cols, emit):
    lead = lax.broadcasted_iota(jnp.int32, (2 * WIN, 1), 0) % WIN < HALF
    pairs = cols // (2 * WIN)
    for pair in range(pairs):
        for duo in range(HALF // 2):
            rows = []
            for r in (2 * duo, 2 * duo + 1):
                here = load(r, pair * 2 * WIN).astype(F32)
                if pair + 1 < pairs:
                    after = load(r, (pair + 1) * 2 * WIN).astype(F32)[:WIN]
                else:
                    after = load_next(r).astype(F32)
                shifted = jnp.concatenate([here[WIN:], after], axis=0)
                rows.append(jnp.where(lead, shifted, here))
            for side in range(2):
                part = slice(side * WIN, (side + 1) * WIN)
                emit(2 * pair + side, duo, jnp.concatenate([rows[0][part], rows[1][part]], axis=0))


def normalise(block, gain):
    centred = block - jnp.mean(block, axis=-1, keepdims=True)
    variance = jnp.mean(centred * centred, axis=-1, keepdims=True)
    return (centred * lax.rsqrt(variance + epsilon) * gain).astype(BF16)


def place_tokens(load, load_next, cols, gain, raw_ref, normed_ref):
    def emit(window, duo, block):
        at = window * WIN * HALF + duo * 2 * WIN
        raw_ref[at : at + 2 * WIN, :] = block.astype(BF16)
        normed_ref[at : at + 2 * WIN, :] = normalise(block, gain)

    window_tokens(load, load_next, cols, emit)


def project(normed_ref, wq_ref, wkv_ref, qkv_ref):
    width = wq_ref.shape[0]
    normed = normed_ref[...]
    qkv_ref[:, :width] = dot(normed, wq_ref[...]).astype(BF16)
    qkv_ref[:, width : 2 * width] = dot(normed, wkv_ref[:, :width]).astype(BF16)
    qkv_ref[:, 2 * width :] = dot(normed, wkv_ref[:, width:]).astype(BF16)


def own_kernel(where_ref, tok_ref, next_ref, gain_ref, wq_ref, wkv_ref, raw_ref, qkv_ref, normed_ref):
    first = HALF * where_ref[0]
    place_tokens(
        lambda r, c: tok_ref[first + r, c : c + 2 * WIN, :],
        lambda r: next_ref[r],
        tok_ref.shape[1],
        gain_ref[...],
        raw_ref,
        normed_ref,
    )
    project(normed_ref, wq_ref, wkv_ref, qkv_ref)


def main_kernel(
    where_ref,
    x_ref,
    next_ref,
    gain_ref,
    raw_own_ref,
    qkv_own_ref,
    wq_ref,
    wkv_ref,
    wout_ref,
    wdec_ref,
    keep_ref,
    send_ref,
    raw_ref,
    normed_ref,
    qkv_ref,
    prob_ref,
    att_ref,
):
    cols, width = x_ref.shape[1:]
    head_size = width // HEADS
    half_cells = HALF * WIN
    cells = 2 * half_cells
    lanes = 4 * head_size
    place_tokens(
        lambda r, c: x_ref[r, c : c + 2 * WIN, :],
        lambda r: next_ref[r],
        cols,
        gain_ref[...],
        raw_ref,
        normed_ref,
    )
    project(normed_ref, wq_ref, wkv_ref, qkv_ref)

    def iota(shape, dim):
        return lax.broadcasted_iota(jnp.int32, shape, dim)

    blocks = (iota((lanes, lanes), 0) // head_size == iota((lanes, lanes), 1) // head_size).astype(F32).astype(BF16)
    split_rows = iota((cells, 2 * cells), 0) // half_cells != iota((cells, 2 * cells), 1) % cells // half_cells
    bias = jnp.where(split_rows & (where_ref[1] > 0), -1e30, 0.0)
    first_head = iota((cells, 2 * cells), 1) < cells
    scale = 1.0 / math.sqrt(head_size)
    token_rows = GROUP * WIN

    def one_group(group, _):
        for quad in range(HEADS // 4):
            at = quad * lanes

            def part(window, offset):
                rows = pl.ds(pl.multiple_of((group * GROUP + window) * half_cells, half_cells), half_cells)
                columns = slice(offset + at, offset + at + lanes)
                return jnp.concatenate([qkv_own_ref[rows, columns], qkv_ref[rows, columns]], axis=0)

            for window in range(GROUP):
                keys = jnp.concatenate([part(window, width)] * 4, axis=0) * blocks
                scores = dot_nt(part(window, 0), keys)
                for side in range(2):
                    two = scores[:, side * 2 * cells : (side + 1) * 2 * cells] + bias
                    left = jnp.max(jnp.where(first_head, two, -jnp.inf), axis=-1, keepdims=True)
                    right = jnp.max(jnp.where(first_head, -jnp.inf, two), axis=-1, keepdims=True)
                    peak = jnp.where(first_head, left, right)
                    prob_ref[window * cells : (window + 1) * cells, side * 2 * cells : (side + 1) * 2 * cells] = jnp.exp(
                        (two - peak) * scale
                    ).astype(BF16)
            sums = dot(prob_ref[...], blocks)
            for window in range(GROUP):
                values = jnp.concatenate([part(window, 2 * width)] * 4, axis=0) * blocks
                rows = slice(window * cells, (window + 1) * cells)
                att_ref[rows, at : at + lanes] = (dot(prob_ref[rows, :], values) / sums[rows]).astype(BF16)
        update = dot(att_ref[...], wout_ref[...])
        pieces = []
        for half in range(2):
            for r in range(HALF):
                for window in range(GROUP):
                    inside = half * half_cells + r * WIN
                    pieces.append((window, inside))
        raws = []
        for window in range(GROUP):
            rows = pl.ds(pl.multiple_of((group * GROUP + window) * half_cells, half_cells), half_cells)
            raws.append(
                jnp.concatenate([raw_own_ref[rows, :].astype(F32), raw_ref[rows, :].astype(F32)], axis=0)
            )
        layer_out = jnp.concatenate(
            [
                raws[w][i : i + WIN] + update[w * cells + i : w * cells + i + WIN]
                for w, i in pieces
            ],
            axis=0,
        ).astype(BF16)
        decoded = dot_nt(wdec_ref[...], layer_out)
        band = decoded.shape[0] // PATCH
        lane_part = iota((band, HALF * token_rows), 1) // token_rows
        out_lanes = pl.ds(pl.multiple_of(group * (PATCH * token_rows), PATCH * token_rows), PATCH * token_rows)
        for half, out_ref in ((0, keep_ref), (1, send_ref)):
            from_b = [
                decoded[b * band : (b + 1) * band, half * HALF * token_rows : (half + 1) * HALF * token_rows]
                for b in range(PATCH)
            ]
            for r in range(HALF):
                total = None
                for b in range(PATCH):
                    moved = from_b[b]
                    if b != r:
                        moved = pltpu.roll(moved, (b - r) % PATCH * token_rows, axis=1)
                    total = moved if total is None else jnp.where(lane_part == b, moved, total)
                out_ref[r * band : (r + 1) * band, out_lanes] = total.astype(BF16)
        return 0

    lax.fori_loop(0, cols // token_rows, one_group, 0)


def state_kernel(where_ref, state_ref, got_ref, nudge_ref, high_ref, low_ref, out_ref, whole_ref):
    lon = where_ref[0]
    channels, own_rows, cols = got_ref.shape
    own_lanes = pl.ds(pl.multiple_of(lon * cols, 128), cols)
    got_lanes = pl.ds(pl.multiple_of((1 - lon) * cols, 128), cols)
    for y in range(0, own_rows, 8):
        own_part = pl.ds(pl.multiple_of(lon * own_rows + y, 8), 8)
        for ch in range(0, channels, 8):
            own = jnp.swapaxes(state_ref[ch : ch + 8, own_part, :], 0, 1)
            got = jnp.swapaxes(got_ref[ch : ch + 8, y : y + 8, :], 0, 1)
            for i in range(8):
                rows = slice((y + i) * channels + ch, (y + i) * channels + ch + 8)
                whole_ref[rows, own_lanes] = own[i]
                whole_ref[rows, got_lanes] = got[i]
    step = nudge_ref.shape[0]
    for at in range(0, out_ref.shape[0], step):
        field = whole_ref[at : at + step, :]
        high = field.astype(BF16)
        low = (field - high.astype(F32)).astype(BF16)
        smooth = dot(high, high_ref[...]) + (dot(high, low_ref[...]) + dot(low, high_ref[...]))
        out_ref[at : at + step, :] = field - nudge_ref[...] * smooth


def filter_kernel(where_ref, base_ref, keep_ref, got_ref, nudge_ref, high_ref, low_ref, out_ref, lon_ref, lat_ref):
    lon = where_ref[0]
    keep, got = keep_ref[...], got_ref[...]
    smooth = dot(keep, high_ref[lon]) + dot(got, high_ref[1 - lon])
    smooth = smooth + (dot(keep, low_ref[lon]) + dot(got, low_ref[1 - lon]))
    step = nudge_ref.shape[0]
    total = out_ref.shape[0]
    for at in range(0, total, step):
        out_ref[at : at + step, :] = base_ref[at : at + step, :] + nudge_ref[...] * smooth[at : at + step]
    edge = lon_ref.shape[0]
    inner = pl.ds(pl.multiple_of((1 - lon) * (total - edge), edge), edge)
    outer = pl.ds(pl.multiple_of(lon * (total - edge), edge), edge)
    lon_ref[...] = out_ref[inner, :].astype(BF16)
    lat_ref[...] = out_ref[outer, :].astype(BF16)


def advance_kernel(where_ref, field_ref, lon_ref, lat_ref, out_ref, ext_ref, first_ref, last_ref):
    total, length = field_ref.shape
    edge = lon_ref.shape[0]
    channels = edge // 2
    rows = total // channels
    is_top = where_ref[0] == 0
    pole = where_ref[1] > 0
    from_lon, from_lat = lon_ref[...].astype(F32), lat_ref[...].astype(F32)
    ext_ref[:edge, :] = jnp.where(is_top, from_lat, from_lon)
    ext_ref[edge : edge + total, :] = field_ref[...]
    ext_ref[edge + total :, :] = jnp.where(is_top, from_lon, from_lat)

    def sections(ref, row, use):
        def tile(y, var):
            return ref[pl.ds(pl.multiple_of(y * channels + var * LEV, LEV), LEV), :]

        wind_u, wind_v = tile(row + 1, 0), tile(row + 1, 1)
        push_u, push_v = (0.5 * time_step) * wind_u, (0.5 * time_step) * wind_v
        calm = diffusion * time_step
        east, west, north, south = calm - push_u, calm + push_u, calm - push_v, calm + push_v
        for var in range(VARS):
            centre = tile(row + 1, var)
            step = east * pltpu.roll(centre, length - 1, axis=1) + west * pltpu.roll(centre, 1, axis=1)
            step = step + (north * tile(row + 2, var) + south * tile(row, var))
            use(row, var, centre, step - (4.0 * calm) * centre)

    def put_first(row, var, centre, step):
        at = pl.ds(pl.multiple_of(row * channels + var * LEV, LEV), LEV)
        first_ref[at, :] = centre + step

    def put_out(row, var, centre, step):
        nudged = ext_ref[pl.ds(pl.multiple_of((row + 2) * channels + var * LEV, LEV), LEV), :]
        at = pl.ds(pl.multiple_of(row * channels + var * LEV, LEV), LEV)
        last_ref[at, :] = 0.5 * (nudged + centre + step)

    def first_row(row, _):
        sections(ext_ref, row, put_first)
        return 0

    lax.fori_loop(0, rows + 2, first_row, 0)

    @pl.when(pole & is_top)
    def _():
        first_ref[:channels, :] = jnp.zeros((channels, length), F32)

    @pl.when(pole & jnp.logical_not(is_top))
    def _():
        first_ref[(rows + 1) * channels :, :] = jnp.zeros((channels, length), F32)

    def second_row(row, _):
        sections(first_ref, row, put_out)
        return 0

    lax.fori_loop(0, rows, second_row, 0)
    for y in range(0, rows, 8):
        for ch in range(0, channels, 8):
            block = [last_ref[(y + i) * channels + ch : (y + i) * channels + ch + 8, :][None] for i in range(8)]
            out_ref[ch : ch + 8, y : y + 8, :] = jnp.swapaxes(jnp.concatenate(block, axis=0), 0, 1)


def call(kernel, out_shape, n_in, scratch=(), vmem=56):
    vmem_spec = pl.BlockSpec(memory_space=pltpu.VMEM)
    many = isinstance(out_shape, (tuple, list))
    return pl.pallas_call(
        kernel,
        out_shape=out_shape,
        in_specs=[pl.BlockSpec(memory_space=pltpu.SMEM)] + [vmem_spec] * n_in,
        out_specs=[vmem_spec] * len(out_shape) if many else vmem_spec,
        scratch_shapes=list(scratch),
        compiler_params=pltpu.CompilerParams(vmem_limit_bytes=vmem * MIB),
    )


def body(tokens, ln_gain, w_query, w_keyval, w_out, w_dec, nudge, state):
    tok_rows, tok_cols, width = tokens.shape
    channels, state_rows, state_cols = state.shape
    n_lat, n_lon = lax.axis_size("lat"), lax.axis_size("lon")
    lat, lon = lax.axis_index("lat"), lax.axis_index("lon")
    total_cols = tok_cols * n_lon
    length = state_cols * n_lon
    band_rows = state_rows // n_lon
    both = ("lat", "lon")
    tokens_half = tok_cols * HALF
    decoded_lanes = tok_cols * PATCH
    band = band_rows * channels

    pole = ((lat == 0) & (lon == 0)) | ((lat == n_lat - 1) & (lon == 1))
    where = jnp.stack([lon, pole.astype(jnp.int32)]).astype(jnp.int32)

    def at(row, col):
        return row * n_lon + col

    last = n_lat - 1
    swap = [(0, 1), (1, 0)]
    shift = [(at(i, 0), at(i + 1, 0)) for i in range(last)] + [(at(last, 0), at(last, 1))]
    shift += [(at(i, 1), at(i - 1, 1)) for i in range(1, n_lat)] + [(at(0, 1), at(0, 0))]
    meet = [(at(i, 1), at(i + 1, 0)) for i in range(last)] + [(at(i + 1, 0), at(i, 1)) for i in range(last)]
    meet_all = meet + [(at(0, 0), at(0, 0)), (at(last, 1), at(last, 1))]

    give = lax.dynamic_slice_in_dim(tokens, HALF * (1 - lon), HALF, 0)
    own_first = lax.dynamic_slice(tokens, (HALF * lon, 0, 0), (HALF, WIN, width))
    got_tokens = lax.ppermute(give, both, shift)
    own_next = lax.ppermute(give[:, :WIN], "lon", swap)
    got_next = lax.ppermute(own_first, both, meet_all)
    give_state = lax.dynamic_slice_in_dim(state, band_rows * (1 - lon), band_rows, 1)
    got_state = lax.ppermute(give_state, "lon", swap)

    gain = ln_gain[None, :]
    nudge_rows = jnp.tile(nudge[:, None], (PATCH, 1))
    matrix = zonal_filter(length, KEEP)
    high, low = (jnp.asarray(m) for m in split_high_low(matrix))
    order = decoded_order(total_cols, n_lon)
    dec_high, dec_low = (jnp.asarray(m) for m in split_high_low(matrix[order]))
    w_dec_t = w_dec.reshape(width, channels, PATCH, PATCH).transpose(3, 2, 1, 0).reshape(-1, width)

    raw_own, qkv_own = call(
        own_kernel,
        (
            jax.ShapeDtypeStruct((tokens_half, width), BF16),
            jax.ShapeDtypeStruct((tokens_half, 3 * width), BF16),
        ),
        5,
        [pltpu.VMEM((tokens_half, width), BF16)],
    )(where, tokens, own_next, gain, w_query, w_keyval)

    base = call(
        state_kernel,
        jax.ShapeDtypeStruct((band, length), F32),
        5,
        [pltpu.VMEM((band, length), F32)],
    )(where, state, got_state, nudge_rows, high, low)

    decoded_shape = jax.ShapeDtypeStruct((band, decoded_lanes), BF16)
    window_cells = GROUP * WIN * WIN
    keep, send = call(
        main_kernel,
        (decoded_shape, decoded_shape),
        9,
        [
            pltpu.VMEM((tokens_half, width), BF16),
            pltpu.VMEM((tokens_half, width), BF16),
            pltpu.VMEM((tokens_half, 3 * width), BF16),
            pltpu.VMEM((window_cells, 4 * width // HEADS), BF16),
            pltpu.VMEM((window_cells, width), BF16),
        ],
    )(where, got_tokens, got_next, gain, raw_own, qkv_own, w_query, w_keyval, w_out, w_dec_t)

    got = lax.ppermute(send, both, meet_all)

    edge = jax.ShapeDtypeStruct((2 * channels, length), BF16)
    nudged, to_lon, to_lat = call(
        filter_kernel,
        (jax.ShapeDtypeStruct((band, length), F32), edge, edge),
        6,
    )(where, base, keep, got, nudge_rows, dec_high, dec_low)

    from_lat = lax.ppermute(to_lat, both, meet)
    from_lon = lax.ppermute(to_lon, "lon", swap)

    return call(
        advance_kernel,
        jax.ShapeDtypeStruct((channels, band_rows, length), F32),
        3,
        [
            pltpu.VMEM((band + 4 * channels, length), F32),
            pltpu.VMEM((band + 2 * channels, length), F32),
            pltpu.VMEM((band, length), F32),
        ],
    )(where, nudged, from_lon, from_lat)


def solution(mesh):
    in_specs = (
        P(("member", "lat"), "lon", None),
        P(),
        P(),
        P(),
        P(),
        P(),
        P(),
        P(None, ("member", "lat"), "lon"),
    )
    out_specs = P(None, ("member", "lat", "lon"), None)
    return jax.shard_map(body, mesh=mesh, in_specs=in_specs, out_specs=out_specs, check_vma=False)
```

```python
import functools
import math

import jax
import jax.numpy as jnp
import ml_dtypes
import numpy as np
from jax import lax
from jax.experimental import pallas as pl
from jax.experimental.pallas import tpu as pltpu
from jax.sharding import PartitionSpec as P

HEADS = 16
WIN = 8
PATCH = 4
VARS = 4
LEV = 8
KEEP = 256

time_step = 0.1
diffusion = 0.5
epsilon = 1e-05
HALF = WIN // 2
GROUP = 4
MIB = 1 << 20
F32 = jnp.float32
BF16 = jnp.bfloat16


def zonal_filter(length, kept_waves):
    lag = np.arange(length, dtype=np.float64)
    waves = np.arange(1, kept_waves, dtype=np.float64)
    kernel = 1.0 + 2.0 * np.cos(2.0 * np.pi / length * lag[:, None] * waves[None, :]).sum(1)
    at = (np.arange(length)[:, None] - np.arange(length)[None, :]) % length
    return (kernel / length)[at]


def split_high_low(matrix):
    high = matrix.astype(ml_dtypes.bfloat16)
    low = (matrix - high.astype(np.float64)).astype(ml_dtypes.bfloat16)
    return high, low


def decoded_order(total_cols, parts):
    cols = total_cols // parts
    group_cols = GROUP * WIN
    rows = []
    for part in range(parts):
        lanes = []
        for group in range(cols // group_cols):
            for b in range(PATCH):
                for place in range(group_cols):
                    col = part * cols + group * group_cols + place
                    if place % WIN < HALF:
                        col += WIN
                    lanes.append((col % total_cols) * PATCH + b)
        rows.append(lanes)
    return np.array(rows)


def place():
    lat, lon = lax.axis_index("lat"), lax.axis_index("lon")
    return lon, ((lat == 0) & (lon == 0)) | ((lat == lax.axis_size("lat") - 1) & (lon == 1))


def nudge_column(nudge_ref, rows):
    channels = nudge_ref.shape[1]
    picked = lax.broadcasted_iota(jnp.int32, (rows, channels), 0) % channels == lax.broadcasted_iota(
        jnp.int32, (rows, channels), 1
    )
    return jnp.sum(jnp.where(picked, nudge_ref[...], 0.0), axis=1, keepdims=True)


def dot(a, b):
    return lax.dot_general(a, b, (((1,), (0,)), ((), ())), preferred_element_type=F32)


def dot_nt(a, b):
    return lax.dot_general(a, b, (((1,), (1,)), ((), ())), preferred_element_type=F32)


def window_tokens(load, load_next, cols, emit):
    lead = lax.broadcasted_iota(jnp.int32, (2 * WIN, 1), 0) % WIN < HALF
    pairs = cols // (2 * WIN)
    for pair in range(pairs):
        for duo in range(HALF // 2):
            rows = []
            for r in (2 * duo, 2 * duo + 1):
                here = load(r, pair * 2 * WIN).astype(F32)
                if pair + 1 < pairs:
                    after = load(r, (pair + 1) * 2 * WIN).astype(F32)[:WIN]
                else:
                    after = load_next(r).astype(F32)
                shifted = jnp.concatenate([here[WIN:], after], axis=0)
                rows.append(jnp.where(lead, shifted, here))
            for side in range(2):
                part = slice(side * WIN, (side + 1) * WIN)
                emit(2 * pair + side, duo, jnp.concatenate([rows[0][part], rows[1][part]], axis=0))


def normalise(block, gain):
    centred = block - jnp.mean(block, axis=-1, keepdims=True)
    variance = jnp.mean(centred * centred, axis=-1, keepdims=True)
    return (centred * lax.rsqrt(variance + epsilon) * gain).astype(BF16)


def place_tokens(load, load_next, cols, gain, raw_ref, normed_ref):
    def emit(window, duo, block):
        at = window * WIN * HALF + duo * 2 * WIN
        raw_ref[at : at + 2 * WIN, :] = block.astype(BF16)
        normed_ref[at : at + 2 * WIN, :] = normalise(block, gain)

    window_tokens(load, load_next, cols, emit)


def project(normed_ref, wq_ref, wkv_ref, qkv_ref):
    width = wq_ref.shape[0]
    normed = normed_ref[...]
    qkv_ref[:, :width] = dot(normed, wq_ref[...]).astype(BF16)
    qkv_ref[:, width : 2 * width] = dot(normed, wkv_ref[:, :width]).astype(BF16)
    qkv_ref[:, 2 * width :] = dot(normed, wkv_ref[:, width:]).astype(BF16)


def own_kernel(tok_ref, next_ref, gain_ref, wq_ref, wkv_ref, raw_ref, qkv_ref, normed_ref):
    first = HALF * place()[0]
    place_tokens(
        lambda r, c: tok_ref[first + r, c : c + 2 * WIN, :],
        lambda r: next_ref[r],
        tok_ref.shape[1],
        gain_ref[...],
        raw_ref,
        normed_ref,
    )
    project(normed_ref, wq_ref, wkv_ref, qkv_ref)


def main_kernel(
    x_ref,
    next_ref,
    gain_ref,
    raw_own_ref,
    qkv_own_ref,
    wq_ref,
    wkv_ref,
    wout_ref,
    wdec_ref,
    keep_ref,
    send_ref,
    raw_ref,
    normed_ref,
    qkv_ref,
    prob_ref,
    att_ref,
):
    cols, width = x_ref.shape[1:]
    head_size = width // HEADS
    half_cells = HALF * WIN
    cells = 2 * half_cells
    lanes = 4 * head_size
    place_tokens(
        lambda r, c: x_ref[r, c : c + 2 * WIN, :],
        lambda r: next_ref[r],
        cols,
        gain_ref[...],
        raw_ref,
        normed_ref,
    )
    project(normed_ref, wq_ref, wkv_ref, qkv_ref)

    def iota(shape, dim):
        return lax.broadcasted_iota(jnp.int32, shape, dim)

    blocks = (iota((lanes, lanes), 0) // head_size == iota((lanes, lanes), 1) // head_size).astype(F32).astype(BF16)
    split_rows = iota((cells, 2 * cells), 0) // half_cells != iota((cells, 2 * cells), 1) % cells // half_cells
    bias = jnp.where(split_rows & place()[1], -1e30, 0.0)
    first_head = iota((cells, 2 * cells), 1) < cells
    scale = 1.0 / math.sqrt(head_size)
    token_rows = GROUP * WIN

    def one_group(group, _):
        for quad in range(HEADS // 4):
            at = quad * lanes

            def part(window, offset):
                rows = pl.ds(pl.multiple_of((group * GROUP + window) * half_cells, half_cells), half_cells)
                columns = slice(offset + at, offset + at + lanes)
                return jnp.concatenate([qkv_own_ref[rows, columns], qkv_ref[rows, columns]], axis=0)

            for window in range(GROUP):
                keys = jnp.concatenate([part(window, width)] * 4, axis=0) * blocks
                scores = dot_nt(part(window, 0), keys)
                for side in range(2):
                    two = scores[:, side * 2 * cells : (side + 1) * 2 * cells] + bias
                    left = jnp.max(jnp.where(first_head, two, -jnp.inf), axis=-1, keepdims=True)
                    right = jnp.max(jnp.where(first_head, -jnp.inf, two), axis=-1, keepdims=True)
                    peak = jnp.where(first_head, left, right)
                    prob_ref[window * cells : (window + 1) * cells, side * 2 * cells : (side + 1) * 2 * cells] = jnp.exp(
                        (two - peak) * scale
                    ).astype(BF16)
            sums = dot(prob_ref[...], blocks)
            for window in range(GROUP):
                values = jnp.concatenate([part(window, 2 * width)] * 4, axis=0) * blocks
                rows = slice(window * cells, (window + 1) * cells)
                att_ref[rows, at : at + lanes] = (dot(prob_ref[rows, :], values) / sums[rows]).astype(BF16)
        update = dot(att_ref[...], wout_ref[...])
        pieces = []
        for half in range(2):
            for r in range(HALF):
                for window in range(GROUP):
                    inside = half * half_cells + r * WIN
                    pieces.append((window, inside))
        raws = []
        for window in range(GROUP):
            rows = pl.ds(pl.multiple_of((group * GROUP + window) * half_cells, half_cells), half_cells)
            raws.append(
                jnp.concatenate([raw_own_ref[rows, :].astype(F32), raw_ref[rows, :].astype(F32)], axis=0)
            )
        layer_out = jnp.concatenate(
            [
                raws[w][i : i + WIN] + update[w * cells + i : w * cells + i + WIN]
                for w, i in pieces
            ],
            axis=0,
        ).astype(BF16)
        decoded = dot_nt(wdec_ref[...], layer_out)
        band = decoded.shape[0] // PATCH
        lane_part = iota((band, HALF * token_rows), 1) // token_rows
        out_lanes = pl.ds(pl.multiple_of(group * (PATCH * token_rows), PATCH * token_rows), PATCH * token_rows)
        for half, out_ref in ((0, keep_ref), (1, send_ref)):
            from_b = [
                decoded[b * band : (b + 1) * band, half * HALF * token_rows : (half + 1) * HALF * token_rows]
                for b in range(PATCH)
            ]
            for r in range(HALF):
                total = None
                for b in range(PATCH):
                    moved = from_b[b]
                    if b != r:
                        moved = pltpu.roll(moved, (b - r) % PATCH * token_rows, axis=1)
                    total = moved if total is None else jnp.where(lane_part == b, moved, total)
                out_ref[r * band : (r + 1) * band, out_lanes] = total.astype(BF16)
        return 0

    lax.fori_loop(0, cols // token_rows, one_group, 0)


def state_kernel(state_ref, got_ref, nudge_ref, high_ref, low_ref, out_ref, whole_ref):
    lon = place()[0]
    channels, own_rows, cols = got_ref.shape
    own_lanes = pl.ds(pl.multiple_of(lon * cols, 128), cols)
    got_lanes = pl.ds(pl.multiple_of((1 - lon) * cols, 128), cols)
    for y in range(0, own_rows, 8):
        own_part = pl.ds(pl.multiple_of(lon * own_rows + y, 8), 8)
        for ch in range(0, channels, 8):
            own = jnp.swapaxes(state_ref[ch : ch + 8, own_part, :], 0, 1)
            got = jnp.swapaxes(got_ref[ch : ch + 8, y : y + 8, :], 0, 1)
            for i in range(8):
                rows = slice((y + i) * channels + ch, (y + i) * channels + ch + 8)
                whole_ref[rows, own_lanes] = own[i]
                whole_ref[rows, got_lanes] = got[i]
    step = PATCH * channels
    strength = nudge_column(nudge_ref, step)
    for at in range(0, out_ref.shape[0], step):
        field = whole_ref[at : at + step, :]
        high = field.astype(BF16)
        low = (field - high.astype(F32)).astype(BF16)
        smooth = dot(high, high_ref[...]) + (dot(high, low_ref[...]) + dot(low, high_ref[...]))
        out_ref[at : at + step, :] = field - strength * smooth


def filter_kernel(base_ref, keep_ref, got_ref, nudge_ref, high_ref, low_ref, out_ref, lon_ref, lat_ref):
    lon = place()[0]
    keep, got = keep_ref[...], got_ref[...]
    smooth = dot(keep, high_ref[lon]) + dot(got, high_ref[1 - lon])
    smooth = smooth + (dot(keep, low_ref[lon]) + dot(got, low_ref[1 - lon]))
    step = PATCH * nudge_ref.shape[1]
    strength = nudge_column(nudge_ref, step)
    total = out_ref.shape[0]
    for at in range(0, total, step):
        out_ref[at : at + step, :] = base_ref[at : at + step, :] + strength * smooth[at : at + step]
    edge = lon_ref.shape[0]
    inner = pl.ds(pl.multiple_of((1 - lon) * (total - edge), edge), edge)
    outer = pl.ds(pl.multiple_of(lon * (total - edge), edge), edge)
    lon_ref[...] = out_ref[inner, :].astype(BF16)
    lat_ref[...] = out_ref[outer, :].astype(BF16)


def advance_kernel(field_ref, lon_ref, lat_ref, out_ref, ext_ref, first_ref, last_ref):
    total, length = field_ref.shape
    edge = lon_ref.shape[0]
    channels = edge // 2
    rows = total // channels
    lon, pole = place()
    is_top = lon == 0
    from_lon, from_lat = lon_ref[...].astype(F32), lat_ref[...].astype(F32)
    ext_ref[:edge, :] = jnp.where(is_top, from_lat, from_lon)
    ext_ref[edge : edge + total, :] = field_ref[...]
    ext_ref[edge + total :, :] = jnp.where(is_top, from_lon, from_lat)

    def sections(ref, row, use):
        def tile(y, var):
            return ref[pl.ds(pl.multiple_of(y * channels + var * LEV, LEV), LEV), :]

        wind_u, wind_v = tile(row + 1, 0), tile(row + 1, 1)
        push_u, push_v = (0.5 * time_step) * wind_u, (0.5 * time_step) * wind_v
        calm = diffusion * time_step
        east, west, north, south = calm - push_u, calm + push_u, calm - push_v, calm + push_v
        for var in range(VARS):
            centre = tile(row + 1, var)
            step = east * pltpu.roll(centre, length - 1, axis=1) + west * pltpu.roll(centre, 1, axis=1)
            step = step + (north * tile(row + 2, var) + south * tile(row, var))
            use(row, var, centre, step - (4.0 * calm) * centre)

    def put_first(row, var, centre, step):
        at = pl.ds(pl.multiple_of(row * channels + var * LEV, LEV), LEV)
        first_ref[at, :] = centre + step

    def put_out(row, var, centre, step):
        nudged = ext_ref[pl.ds(pl.multiple_of((row + 2) * channels + var * LEV, LEV), LEV), :]
        at = pl.ds(pl.multiple_of(row * channels + var * LEV, LEV), LEV)
        last_ref[at, :] = 0.5 * (nudged + centre + step)

    def first_row(row, _):
        sections(ext_ref, row, put_first)
        return 0

    lax.fori_loop(0, rows + 2, first_row, 0)

    @pl.when(pole & is_top)
    def _():
        first_ref[:channels, :] = jnp.zeros((channels, length), F32)

    @pl.when(pole & jnp.logical_not(is_top))
    def _():
        first_ref[(rows + 1) * channels :, :] = jnp.zeros((channels, length), F32)

    def second_row(row, _):
        sections(first_ref, row, put_out)
        return 0

    lax.fori_loop(0, rows, second_row, 0)
    for y in range(0, rows, 8):
        for ch in range(0, channels, 8):
            block = [last_ref[(y + i) * channels + ch : (y + i) * channels + ch + 8, :][None] for i in range(8)]
            out_ref[ch : ch + 8, y : y + 8, :] = jnp.swapaxes(jnp.concatenate(block, axis=0), 0, 1)


def call(kernel, out_shape, n_in, scratch=(), vmem=24):
    vmem_spec = pl.BlockSpec(memory_space=pltpu.VMEM)
    many = isinstance(out_shape, (tuple, list))
    return pl.pallas_call(
        kernel,
        out_shape=out_shape,
        in_specs=[vmem_spec] * n_in,
        out_specs=[vmem_spec] * len(out_shape) if many else vmem_spec,
        scratch_shapes=list(scratch),
        compiler_params=pltpu.CompilerParams(vmem_limit_bytes=vmem * MIB),
    )


def body(tokens, ln_gain, w_query, w_keyval, w_out, w_dec, nudge, state):
    tok_rows, tok_cols, width = tokens.shape
    channels, state_rows, state_cols = state.shape
    n_lat, n_lon = lax.axis_size("lat"), lax.axis_size("lon")
    lon = lax.axis_index("lon")
    total_cols = tok_cols * n_lon
    length = state_cols * n_lon
    band_rows = state_rows // n_lon
    both = ("lat", "lon")
    tokens_half = tok_cols * HALF
    decoded_lanes = tok_cols * PATCH
    band = band_rows * channels


    def at(row, col):
        return row * n_lon + col

    last = n_lat - 1
    swap = [(0, 1), (1, 0)]
    shift = [(at(i, 0), at(i + 1, 0)) for i in range(last)] + [(at(last, 0), at(last, 1))]
    shift += [(at(i, 1), at(i - 1, 1)) for i in range(1, n_lat)] + [(at(0, 1), at(0, 0))]
    meet = [(at(i, 1), at(i + 1, 0)) for i in range(last)] + [(at(i + 1, 0), at(i, 1)) for i in range(last)]
    meet_all = meet + [(at(0, 0), at(0, 0)), (at(last, 1), at(last, 1))]

    give = lax.dynamic_slice_in_dim(tokens, HALF * (1 - lon), HALF, 0)
    own_first = lax.dynamic_slice(tokens, (HALF * lon, 0, 0), (HALF, WIN, width))
    got_tokens = lax.ppermute(give, both, shift)
    own_next = lax.ppermute(give[:, :WIN], "lon", swap)
    got_next = lax.ppermute(own_first, both, meet_all)
    give_state = lax.dynamic_slice_in_dim(state, band_rows * (1 - lon), band_rows, 1)
    got_state = lax.ppermute(give_state, "lon", swap)

    gain = ln_gain[None, :]
    nudge_row = nudge[None, :]
    matrix = zonal_filter(length, KEEP)
    high, low = (jnp.asarray(m) for m in split_high_low(matrix))
    order = decoded_order(total_cols, n_lon)
    dec_high, dec_low = (jnp.asarray(m) for m in split_high_low(matrix[order]))
    w_dec_t = w_dec.reshape(width, channels, PATCH, PATCH).transpose(3, 2, 1, 0).reshape(-1, width)

    raw_own, qkv_own = call(
        own_kernel,
        (
            jax.ShapeDtypeStruct((tokens_half, width), BF16),
            jax.ShapeDtypeStruct((tokens_half, 3 * width), BF16),
        ),
        5,
        [pltpu.VMEM((tokens_half, width), BF16)],
    )(tokens, own_next, gain, w_query, w_keyval)

    base = call(
        state_kernel,
        jax.ShapeDtypeStruct((band, length), F32),
        5,
        [pltpu.VMEM((band, length), F32)],
    )(state, got_state, nudge_row, high, low)

    decoded_shape = jax.ShapeDtypeStruct((band, decoded_lanes), BF16)
    window_cells = GROUP * WIN * WIN
    keep, send = call(
        main_kernel,
        (decoded_shape, decoded_shape),
        9,
        [
            pltpu.VMEM((tokens_half, width), BF16),
            pltpu.VMEM((tokens_half, width), BF16),
            pltpu.VMEM((tokens_half, 3 * width), BF16),
            pltpu.VMEM((window_cells, 4 * width // HEADS), BF16),
            pltpu.VMEM((window_cells, width), BF16),
        ],
    )(got_tokens, got_next, gain, raw_own, qkv_own, w_query, w_keyval, w_out, w_dec_t)

    got = lax.ppermute(send, both, meet_all)

    edge = jax.ShapeDtypeStruct((2 * channels, length), BF16)
    nudged, to_lon, to_lat = call(
        filter_kernel,
        (jax.ShapeDtypeStruct((band, length), F32), edge, edge),
        6,
    )(base, keep, got, nudge_row, dec_high, dec_low)

    from_lat = lax.ppermute(to_lat, both, meet)
    from_lon = lax.ppermute(to_lon, "lon", swap)

    return call(
        advance_kernel,
        jax.ShapeDtypeStruct((channels, band_rows, length), F32),
        3,
        [
            pltpu.VMEM((band + 4 * channels, length), F32),
            pltpu.VMEM((band + 2 * channels, length), F32),
            pltpu.VMEM((band, length), F32),
        ],
    )(nudged, from_lon, from_lat)


def solution(mesh):
    in_specs = (
        P(("member", "lat"), "lon", None),
        P(),
        P(),
        P(),
        P(),
        P(),
        P(),
        P(None, ("member", "lat"), "lon"),
    )
    out_specs = P(None, ("member", "lat", "lon"), None)
    return jax.shard_map(body, mesh=mesh, in_specs=in_specs, out_specs=out_specs, check_vma=False)
```

```python
import functools
import math

import jax
import jax.numpy as jnp
import ml_dtypes
import numpy as np
from jax import lax
from jax.experimental import pallas as pl
from jax.experimental.pallas import tpu as pltpu
from jax.sharding import PartitionSpec as P

HEADS = 16
WIN = 8
PATCH = 4
VARS = 4
LEV = 8
KEEP = 256

time_step = 0.1
diffusion = 0.5
epsilon = 1e-05
HALF = WIN // 2
GROUP = 4
MIB = 1 << 20
F32 = jnp.float32
BF16 = jnp.bfloat16


def zonal_filter(length, kept_waves):
    lag = np.arange(length, dtype=np.float64)
    waves = np.arange(1, kept_waves, dtype=np.float64)
    kernel = 1.0 + 2.0 * np.cos(2.0 * np.pi / length * lag[:, None] * waves[None, :]).sum(1)
    at = (np.arange(length)[:, None] - np.arange(length)[None, :]) % length
    return (kernel / length)[at]


def split_high_low(matrix):
    high = matrix.astype(ml_dtypes.bfloat16)
    low = (matrix - high.astype(np.float64)).astype(ml_dtypes.bfloat16)
    return high, low


def decoded_order(total_cols, parts):
    cols = total_cols // parts
    group_cols = GROUP * WIN
    rows = []
    for part in range(parts):
        lanes = []
        for group in range(cols // group_cols):
            for b in range(PATCH):
                for place in range(group_cols):
                    col = part * cols + group * group_cols + place
                    if place % WIN < HALF:
                        col += WIN
                    lanes.append((col % total_cols) * PATCH + b)
        rows.append(lanes)
    return np.array(rows)


def place():
    lat, lon = lax.axis_index("lat"), lax.axis_index("lon")
    return lon, ((lat == 0) & (lon == 0)) | ((lat == lax.axis_size("lat") - 1) & (lon == 1))


def nudge_column(nudge_ref, rows):
    channels = nudge_ref.shape[1]
    picked = lax.broadcasted_iota(jnp.int32, (rows, channels), 0) % channels == lax.broadcasted_iota(
        jnp.int32, (rows, channels), 1
    )
    return jnp.sum(jnp.where(picked, nudge_ref[...], 0.0), axis=1, keepdims=True)


def dot(a, b):
    return lax.dot_general(a, b, (((1,), (0,)), ((), ())), preferred_element_type=F32)


def dot_nt(a, b):
    return lax.dot_general(a, b, (((1,), (1,)), ((), ())), preferred_element_type=F32)


def window_tokens(load, first, cols, emit):
    lead = lax.broadcasted_iota(jnp.int32, (2 * WIN, 1), 0) % WIN < HALF
    for pair in range(cols // (2 * WIN)):
        col = first + pair * 2 * WIN
        for r in range(HALF):
            here = load(r, col, 2 * WIN).astype(F32)
            after = load(r, col + 2 * WIN, WIN).astype(F32)
            emit(pair, r, jnp.where(lead, jnp.concatenate([here[WIN:], after], axis=0), here))


def normalise(block, gain):
    centred = block - jnp.mean(block, axis=-1, keepdims=True)
    variance = jnp.mean(centred * centred, axis=-1, keepdims=True)
    return centred * lax.rsqrt(variance + epsilon) * gain


def place_tokens(load, first, cols, gain, raw_ref, normed_ref):
    held = {}

    def emit(pair, r, block):
        group, inside = divmod(pair * 2, GROUP)
        at = (group * HALF + r) * GROUP * WIN + inside * WIN
        raw_ref[at : at + 2 * WIN, :] = block.astype(BF16)
        held[r % 2] = normalise(block, gain)
        if r % 2:
            for side in range(2):
                part = slice(side * WIN, (side + 1) * WIN)
                at = (2 * pair + side) * WIN * HALF + (r - 1) * WIN
                both = jnp.concatenate([held[0][part], held[1][part]], axis=0)
                normed_ref[at : at + 2 * WIN, :] = both.astype(BF16)

    window_tokens(load, first, cols, emit)


def project(normed_ref, wq_ref, wkv_ref, qkv_ref, copies=()):
    width = wq_ref.shape[0]
    normed = normed_ref[...]
    for i in range(3):
        if copies:
            copies[i].wait()
        weights = wq_ref[...] if i == 0 else wkv_ref[:, (i - 1) * width : i * width]
        qkv_ref[:, i * width : (i + 1) * width] = dot(normed, weights).astype(BF16)


def run_copies(sems, pairs):
    copies = [pltpu.make_async_copy(source, target, sems.at[i]) for i, (source, target) in enumerate(pairs)]
    for copy in copies:
        copy.start()
    return copies


def pack_kernel(pieces, tok_ref, state_ref, *refs):
    *give_refs, edge_ref, give_state_ref, sems = refs
    lon = place()[0]
    rows = give_state_ref.shape[1]
    pairs = []
    for give_ref, (start, size) in zip(give_refs, pieces):
        pairs.append((tok_ref.at[pl.ds(HALF * (1 - lon), HALF), pl.ds(start, size), :], give_ref))
    pairs.append((tok_ref.at[:, pl.ds(0, edge_ref.shape[1]), :], edge_ref))
    pairs.append((state_ref.at[:, pl.ds(pl.multiple_of(rows * (1 - lon), 8), rows), :], give_state_ref))
    for copy in run_copies(sems, pairs):
        copy.wait()


def own_kernel(
    tok_hbm,
    edge_ref,
    gain_ref,
    wq_hbm,
    wkv_hbm,
    wout_hbm,
    wdec_hbm,
    qkv_ref,
    wdec_t_ref,
    wmix_t_ref,
    decoded_ref,
    wq_ref,
    wkv_ref,
    tok_ref,
    raw_ref,
    normed_ref,
    wdec_ref,
    wout_ref,
    sems,
):
    lon = place()[0]
    cols = tok_ref.shape[1]
    width = wq_ref.shape[0]
    keys, values = pl.ds(0, width), pl.ds(width, width)
    own_rows = pl.ds(HALF * lon, HALF)
    copies = run_copies(
        sems,
        [
            (tok_hbm.at[own_rows], tok_ref),
            (wq_hbm, wq_ref),
            (wkv_hbm.at[:, keys], wkv_ref.at[:, keys]),
            (wkv_hbm.at[:, values], wkv_ref.at[:, values]),
            (wdec_hbm, wdec_ref),
            (wout_hbm, wout_ref),
        ],
    )

    def load(r, c, size):
        if c == cols:
            return edge_ref[HALF * lon + r, :size, :]
        return tok_ref[r, c : c + size, :]

    copies[0].wait()
    place_tokens(load, 0, cols, gain_ref[...], raw_ref, normed_ref)
    project(normed_ref, wq_ref, wkv_ref, qkv_ref, copies[1:4])
    outs = wdec_ref.shape[1]
    band = outs // PATCH
    channels = band // PATCH
    row = lax.broadcasted_iota(jnp.int32, (outs, 1), 0)
    source = (row % channels) * PATCH * PATCH + (row % band // channels) * PATCH + row // band
    pick = (lax.broadcasted_iota(jnp.int32, (outs, outs), 1) == source).astype(F32).astype(BF16)
    copies[4].wait()
    wdec_t_ref[...] = dot_nt(pick, wdec_ref[...]).astype(BF16)
    decoded_ref[...] = dot_nt(wdec_t_ref[...], raw_ref[...])
    copies[5].wait()
    wmix_t_ref[...] = dot_nt(wdec_t_ref[...], wout_ref[...]).astype(BF16)


def main_kernel(first, starts, *refs):
    x_refs, refs = refs[: len(starts)], refs[len(starts) :]
    gain_ref, qkv_own_ref, decoded_own_ref, wq_ref, wkv_ref, wmix_ref, wdec_ref, *refs = refs
    keep_ref, send_ref, raw_ref, normed_ref, qkv_ref, att_ref, decoded_ref = refs
    width = raw_ref.shape[1]
    head_size = width // HEADS
    half_cells = HALF * WIN
    cells = 2 * half_cells
    lanes = 4 * head_size
    quads = HEADS // 4
    cols = raw_ref.shape[0] // HALF
    base = first * HALF
    group_cols = GROUP * WIN
    group_half = GROUP * half_cells

    def load(r, c, size):
        which = max(i for i in range(len(starts)) if starts[i] <= c)
        return x_refs[which][r, c - starts[which] : c - starts[which] + size, :]

    def iota(shape, dim):
        return lax.broadcasted_iota(jnp.int32, shape, dim)

    blocks = (iota((lanes, lanes), 0) // head_size == iota((lanes, lanes), 1) // head_size).astype(F32).astype(BF16)
    split_rows = iota((cells, 2 * cells), 0) // half_cells != iota((cells, 2 * cells), 1) % cells // half_cells
    bias = jnp.where(split_rows & place()[1], -1e30, 0.0)
    first_head = iota((cells, 2 * cells), 1) < cells
    scale = 1.0 / (math.sqrt(head_size) * math.log(2.0))

    def project_quad(quad):
        normed = normed_ref[...]
        at = quad * lanes
        for offset, weights in (
            (0, wq_ref[:, at : at + lanes]),
            (width, wkv_ref[:, at : at + lanes]),
            (2 * width, wkv_ref[:, width + at : width + at + lanes]),
        ):
            qkv_ref[:, offset + at : offset + at + lanes] = dot(normed, weights).astype(BF16)

    def part(window, quad, offset):
        columns = slice(offset + quad * lanes, offset + (quad + 1) * lanes)
        got = slice(window * half_cells, (window + 1) * half_cells)
        own = slice(base + got.start, base + got.stop)
        return jnp.concatenate([qkv_own_ref[own, columns], qkv_ref[got, columns]], axis=0)

    def score(window, quad):
        keys = jnp.concatenate([part(window, quad, width)] * 4, axis=0) * blocks
        return dot_nt(part(window, quad, 0), keys)

    def weigh(scores):
        outs = []
        for side in range(2):
            two = scores[:, side * 2 * cells : (side + 1) * 2 * cells] + bias
            left = jnp.max(jnp.where(first_head, two, -jnp.inf), axis=-1, keepdims=True)
            right = jnp.max(jnp.where(first_head, -jnp.inf, two), axis=-1, keepdims=True)
            peak = jnp.where(first_head, left, right)
            outs.append(jnp.exp2((two - peak) * scale).astype(BF16))
        return jnp.concatenate(outs, axis=1)

    def mix(group, quad, weights):
        sums = dot(jnp.concatenate(weights, axis=0), blocks)
        mixed = []
        for i in range(GROUP):
            values = jnp.concatenate([part(group * GROUP + i, quad, 2 * width)] * 4, axis=0) * blocks
            mixed.append(dot(weights[i], values) / sums[i * cells : (i + 1) * cells])
        tiles = [mixed[i][at : at + WIN] for at in range(0, cells, WIN) for i in range(GROUP)]
        rows = slice(group * 2 * group_half, (group + 1) * 2 * group_half)
        att_ref[rows, quad * lanes : (quad + 1) * lanes] = jnp.concatenate(tiles, axis=0).astype(BF16)

    def decode(group):
        rows = slice(group * 2 * group_half, (group + 1) * 2 * group_half)
        decoded = dot_nt(wmix_ref[...], att_ref[rows, :])
        got = slice(group * group_half, (group + 1) * group_half)
        own = slice(base + got.start, base + got.stop)
        band = decoded.shape[0] // PATCH
        out_lanes = slice(group * group_cols * PATCH, (group + 1) * group_cols * PATCH)
        lane_part = iota((band, group_half), 1) // group_cols
        for half, more, out_ref in ((0, decoded_own_ref[:, own], keep_ref), (1, decoded_ref[:, got], send_ref)):
            total = decoded[:, half * group_half : (half + 1) * group_half] + more
            from_b = [total[b * band : (b + 1) * band] for b in range(PATCH)]
            for r in range(HALF):
                placed = None
                for b in range(PATCH):
                    moved = from_b[b]
                    if b != r:
                        moved = pltpu.roll(moved, (b - r) % PATCH * group_cols, axis=1)
                    placed = moved if placed is None else jnp.where(lane_part == b, moved, placed)
                out_ref[r * band : (r + 1) * band, out_lanes] = placed.astype(BF16)

    place_tokens(load, first, cols, gain_ref[...], raw_ref, normed_ref)
    project_quad(0)
    units = [(group, quad) for group in range(cols // group_cols) for quad in range(quads)]
    weights = None
    for i in range(len(units) + 1):
        if i < len(units):
            group, quad = units[i]
            scores = [score(group * GROUP + w, quad) for w in range(GROUP)]
            if group == 0 and quad + 1 < quads:
                project_quad(quad + 1)
            if i == quads - 1:
                decoded_ref[...] = dot_nt(wdec_ref[...], raw_ref[...])
        if i > 0:
            mix(*units[i - 1], weights)
            if units[i - 1][1] == quads - 1:
                decode(units[i - 1][0])
        if i < len(units):
            weights = [weigh(x) for x in scores]

    lon = place()[0]
    total_rows = keep_ref.shape[0]
    edge = send_ref.shape[0] - total_rows
    near = pl.ds(pl.multiple_of(lon * (total_rows - edge), edge), edge)
    send_ref[total_rows:, :] = keep_ref[near, :]


def unfiltered(field, high_ref, low_ref, strength):
    high = field.astype(BF16)
    low = (field - high.astype(F32)).astype(BF16)
    smooth = dot(high, high_ref[...]) + (dot(high, low_ref[...]) + dot(low, high_ref[...]))
    return field - strength * smooth


def state_kernel(state_ref, got_ref, nudge_ref, high_ref, low_ref, out_ref, edge_ref, whole_ref):
    lon = place()[0]
    channels, own_rows, cols = got_ref.shape
    own_lanes = pl.ds(pl.multiple_of(lon * cols, 128), cols)
    got_lanes = pl.ds(pl.multiple_of((1 - lon) * cols, 128), cols)
    for y in range(0, own_rows, 8):
        own_part = pl.ds(pl.multiple_of(lon * own_rows + y, 8), 8)
        for ch in range(0, channels, 8):
            own = jnp.swapaxes(state_ref[ch : ch + 8, own_part, :], 0, 1)
            got = jnp.swapaxes(got_ref[ch : ch + 8, y : y + 8, :], 0, 1)
            for i in range(8):
                rows = slice((y + i) * channels + ch, (y + i) * channels + ch + 8)
                whole_ref[rows, own_lanes] = own[i]
                whole_ref[rows, got_lanes] = got[i]
    step = PATCH * channels
    strength = nudge_column(nudge_ref, step)
    for at in range(0, out_ref.shape[0], step):
        out_ref[at : at + step, :] = unfiltered(whole_ref[at : at + step, :], high_ref, low_ref, strength)
    edge = edge_ref.shape[0]
    near = pl.ds(pl.multiple_of(lon * (out_ref.shape[0] - edge), edge), edge)
    edge_ref[...] = out_ref[near, :].astype(BF16)


def filter_rows(dec, first, high_ref, low_ref):
    rows = pl.ds(pl.multiple_of(first, 128), dec.shape[1])
    return dot(dec, high_ref[rows, :]) + dot(dec, low_ref[rows, :])


def early_kernel(chunks, base_ref, base_edge_ref, nudge_ref, high_ref, low_ref, *refs):
    keep_refs, send_refs, got_refs, out_ref = refs[:chunks], refs[chunks : 2 * chunks], refs[2 * chunks : -1], refs[-1]
    lon = place()[0]
    total = base_ref.shape[0]
    edge = base_edge_ref.shape[0]
    far = pl.ds(pl.multiple_of((1 - lon) * (total - edge), edge), edge)
    own = [jnp.concatenate([keep[...], send[far, :]], axis=0) for keep, send in zip(keep_refs, send_refs)]
    decoded = jnp.concatenate(own + [got[...] for got in got_refs], axis=1)
    smooth = filter_rows(decoded, lon * (high_ref.shape[0] // 3), high_ref, low_ref)
    step = PATCH * nudge_ref.shape[1]
    strength = nudge_column(nudge_ref, step)
    for at in range(0, total, step):
        out_ref[at : at + step, :] = base_ref[at : at + step, :] + strength * smooth[at : at + step]
    out_ref[total:, :] = base_edge_ref[...].astype(F32) + strength[:edge] * smooth[total:]


def late_kernel(early_ref, got_ref, nudge_ref, high_ref, low_ref, out_ref, near_ref, lat_ref):
    lon = place()[0]
    total = out_ref.shape[0]
    edge = lat_ref.shape[0]
    part = high_ref.shape[0] // 3
    smooth = filter_rows(got_ref[...], lon * part + 2 * part - got_ref.shape[1], high_ref, low_ref)
    step = PATCH * nudge_ref.shape[1]
    strength = nudge_column(nudge_ref, step)
    for at in range(0, total, step):
        out_ref[at : at + step, :] = early_ref[at : at + step, :] + strength * smooth[at : at + step]
    lat_ref[...] = early_ref[total:, :] + strength[:edge] * smooth[total:]
    far = pl.ds(pl.multiple_of((1 - lon) * (total - edge), edge), edge)
    near_ref[...] = out_ref[far, :].astype(BF16)


def row_tile(ref, row, var):
    at = row * (VARS * LEV) + var * LEV
    return pl.ds(at if isinstance(at, int) else pl.multiple_of(at, LEV), LEV)


def tendency_row(south, centre, north, use):
    push_u, push_v = (0.5 * time_step) * centre(0), (0.5 * time_step) * centre(1)
    calm = diffusion * time_step
    to_east, to_west, to_north, to_south = calm - push_u, calm + push_u, calm - push_v, calm + push_v
    for var in range(VARS):
        field = centre(var)
        length = field.shape[1]
        step = to_east * pltpu.roll(field, length - 1, axis=1) + to_west * pltpu.roll(field, 1, axis=1)
        step = step + (to_north * north(var) + to_south * south(var))
        use(var, field, step - (4.0 * calm) * field)


def inner_kernel(field_ref, first_ref, last_ref):
    rows = field_ref.shape[0] // (VARS * LEV)

    def reader(ref, row):
        return lambda var: ref[row_tile(ref, row, var), :]

    def section(ref, row, use):
        tendency_row(reader(ref, row - 1), reader(ref, row), reader(ref, row + 1), use)

    def first_row(row, _):
        def put(var, field, step):
            first_ref[row_tile(first_ref, row, var), :] = field + step

        section(field_ref, row, put)
        return 0

    def last_row(row, _):
        def put(var, field, step):
            nudged = field_ref[row_tile(field_ref, row, var), :]
            last_ref[row_tile(last_ref, row, var), :] = 0.5 * (nudged + field + step)

        section(first_ref, row, put)
        return 0

    lax.fori_loop(1, rows - 1, first_row, 0)
    lax.fori_loop(2, rows - 2, last_row, 0)


def outer_kernel(field_ref, first_ref, last_ref, lon_ref, lat_ref, out_ref, ext_ref, edge_ref):
    channels, rows, length = out_ref.shape
    lon, pole = place()
    is_top = lon == 0
    from_lon = lon_ref[...].astype(F32)
    from_lat = jnp.where(pole, 0.0, lat_ref[...])
    edge = from_lon.shape[0]
    ext_ref[:edge, :] = jnp.where(is_top, from_lat, from_lon)
    ext_ref[edge:, :] = jnp.where(is_top, from_lon, from_lat)

    def field(row):
        def read(var):
            if row < 0:
                return ext_ref[row_tile(ext_ref, row + 2, var), :]
            if row >= rows:
                return ext_ref[row_tile(ext_ref, row - rows + 2, var), :]
            return field_ref[row_tile(field_ref, row, var), :]

        return read

    def first(row):
        def read(var):
            if row < 1:
                return edge_ref[row_tile(edge_ref, row + 1, var), :]
            if row >= rows - 1:
                return edge_ref[row_tile(edge_ref, row - rows + 3, var), :]
            return first_ref[row_tile(first_ref, row, var), :]

        return read

    outside = jnp.where(pole, 0.0, 1.0)
    for row in (-1, 0, rows - 1, rows):
        keep = None
        if row < 0:
            keep = jnp.where(is_top, outside, 1.0)
        if row >= rows:
            keep = jnp.where(is_top, 1.0, outside)

        def put(var, value, step):
            total = value + step
            at = row + 1 if row < 1 else row - rows + 3
            edge_ref[row_tile(edge_ref, at, var), :] = total if keep is None else total * keep

        tendency_row(field(row - 1), field(row), field(row + 1), put)
    outer = {}
    for row in (0, 1, rows - 2, rows - 1):

        def put(var, value, step):
            outer[row, var] = 0.5 * (field(row)(var) + value + step)

        tendency_row(first(row - 1), first(row), first(row + 1), put)
    for y in range(0, rows, 8):
        for var in range(VARS):
            block = []
            for row in range(y, y + 8):
                tile = outer[row, var] if (row, var) in outer else last_ref[row_tile(last_ref, row, var), :]
                block.append(tile[None])
            out_ref[var * LEV : (var + 1) * LEV, y : y + 8, :] = jnp.swapaxes(jnp.concatenate(block, axis=0), 0, 1)


def work(micros):
    return pl.CostEstimate(flops=int(micros * 1e9), bytes_accessed=int(micros * 1e6), transcendentals=0)


def call(kernel, out_shape, n_in, scratch=(), vmem=24, micros=1.0):
    vmem_spec = pl.BlockSpec(memory_space=pltpu.VMEM)
    many = isinstance(out_shape, (tuple, list))
    return pl.pallas_call(
        kernel,
        out_shape=out_shape,
        in_specs=[vmem_spec] * n_in,
        out_specs=[vmem_spec] * len(out_shape) if many else vmem_spec,
        scratch_shapes=list(scratch),
        cost_estimate=work(micros),
        compiler_params=pltpu.CompilerParams(vmem_limit_bytes=vmem * MIB),
    )


def body(tokens, ln_gain, w_query, w_keyval, w_out, w_dec, nudge, state):
    tok_rows, tok_cols, width = tokens.shape
    channels, state_rows, state_cols = state.shape
    n_lat, n_lon = lax.axis_size("lat"), lax.axis_size("lon")
    lon = lax.axis_index("lon")
    total_cols = tok_cols * n_lon
    length = state_cols * n_lon
    band_rows = state_rows // n_lon
    both = ("lat", "lon")
    tokens_half = tok_cols * HALF
    band = band_rows * channels


    def at(row, col):
        return row * n_lon + col

    last = n_lat - 1
    swap = [(0, 1), (1, 0)]
    shift = [(at(i, 0), at(i + 1, 0)) for i in range(last)] + [(at(last, 0), at(last, 1))]
    shift += [(at(i, 1), at(i - 1, 1)) for i in range(1, n_lat)] + [(at(0, 1), at(0, 0))]
    meet = [(at(i, 1), at(i + 1, 0)) for i in range(last)] + [(at(i + 1, 0), at(i, 1)) for i in range(last)]
    meet_all = meet + [(at(0, 0), at(0, 0)), (at(last, 1), at(last, 1))]

    step = GROUP * WIN
    split = max(tok_cols - step, step)
    chunks = [(0, split)] + ([(split, step)] if split < tok_cols else [])
    cuts = [0] + [split + 2 * WIN] * (len(chunks) - 1) + [tok_cols]
    pieces = [(cuts[i], cuts[i + 1] - cuts[i]) for i in range(len(chunks))]

    hbm, vmem = pl.BlockSpec(memory_space=pltpu.HBM), pl.BlockSpec(memory_space=pltpu.VMEM)
    in_hbm = functools.partial(pltpu.with_memory_space_constraint, memory_space=pltpu.HBM)
    shapes = [pltpu.VMEM((HALF, size, width), BF16) for _, size in pieces]
    shapes.append(pltpu.VMEM((tok_rows, 2 * WIN, width), BF16))
    shapes.append(pltpu.VMEM((channels, band_rows, state_cols), F32))
    *give, give_edge, give_state = pl.pallas_call(
        functools.partial(pack_kernel, pieces),
        out_shape=shapes,
        in_specs=[hbm, hbm],
        out_specs=[vmem] * len(shapes),
        scratch_shapes=[pltpu.SemaphoreType.DMA((len(shapes),))],
        compiler_params=pltpu.CompilerParams(vmem_limit_bytes=8 * MIB),
    )(in_hbm(tokens), in_hbm(state))
    edge_tokens = lax.ppermute(give_edge, "lon", swap)
    their_edge = lax.dynamic_slice(edge_tokens, (HALF * (1 - lon), 0, 0), (HALF, WIN, width))
    give[-1] = jnp.concatenate([give[-1], their_edge], axis=1)
    got_tokens = [lax.ppermute(give[0], both, shift)]
    got_state = lax.ppermute(give_state, "lon", swap)

    gain = ln_gain[None, :]
    nudge_row = nudge[None, :]
    matrix = zonal_filter(length, KEEP)
    high, low = (jnp.asarray(m) for m in split_high_low(matrix))
    order = decoded_order(total_cols, n_lon)
    order = np.concatenate([order[0], order[1], order[0]])
    dec_high, dec_low = (jnp.asarray(m) for m in split_high_low(matrix[order]))

    n_out = w_dec.shape[1]
    qkv_own, w_dec_t, w_mix_t, decoded_own, *weights = pl.pallas_call(
        own_kernel,
        out_shape=[
            pltpu.VMEM((tokens_half, 3 * width), BF16),
            pltpu.VMEM((n_out, width), BF16),
            pltpu.VMEM((n_out, width), BF16),
            pltpu.VMEM((n_out, tokens_half), F32),
            pltpu.VMEM(w_query.shape, BF16),
            pltpu.VMEM(w_keyval.shape, BF16),
        ],
        in_specs=[hbm, vmem, vmem, hbm, hbm, hbm, hbm],
        out_specs=[vmem] * 6,
        scratch_shapes=[
            pltpu.VMEM((HALF, tok_cols, width), BF16),
            pltpu.VMEM((tokens_half, width), BF16),
            pltpu.VMEM((tokens_half, width), BF16),
            pltpu.VMEM(w_dec.shape, BF16),
            pltpu.VMEM(w_out.shape, BF16),
            pltpu.SemaphoreType.DMA((6,)),
        ],
        cost_estimate=work(7.5),
        compiler_params=pltpu.CompilerParams(vmem_limit_bytes=32 * MIB),
    )(in_hbm(tokens), edge_tokens, gain, in_hbm(w_query), in_hbm(w_keyval), in_hbm(w_out), in_hbm(w_dec))

    edge_rows = 2 * channels
    got_state, qkv_own = lax.optimization_barrier((got_state, qkv_own))
    base, base_edge = call(
        state_kernel,
        (pltpu.VMEM((band, length), F32), pltpu.VMEM((edge_rows, length), BF16)),
        5,
        [pltpu.VMEM((band, length), F32)],
        micros=2.7,
    )(state, got_state, nudge_row, high, low)
    got_base_edge = lax.ppermute(base_edge, both, meet)
    gain, base, *give[1:] = lax.optimization_barrier((gain, base, *give[1:]))
    got_tokens += [lax.ppermute(part, both, shift) for part in give[1:]]

    keep, send, got = [], [], []
    for i, (first, cols) in enumerate(chunks):
        kept, sent = call(
            functools.partial(main_kernel, first, cuts[: i + 1]),
            (pltpu.VMEM((band, cols * PATCH), BF16), pltpu.VMEM((band + edge_rows, cols * PATCH), BF16)),
            7 + i + 1,
            [
                pltpu.VMEM((cols * HALF, width), BF16),
                pltpu.VMEM((cols * HALF, width), BF16),
                pltpu.VMEM((cols * HALF, 3 * width), BF16),
                pltpu.VMEM((cols * WIN, width), BF16),
                pltpu.VMEM((n_out, cols * HALF), F32),
            ],
            micros=3.0 * (cols // step),
        )(*got_tokens[: i + 1], gain, qkv_own, decoded_own, *weights, w_mix_t, w_dec_t)
        gain, kept = lax.optimization_barrier((gain, kept))
        if i == 0:
            gain, got_base_edge = lax.optimization_barrier((gain, got_base_edge))
        keep.append(kept)
        send.append(sent)
        got.append(lax.ppermute(sent, both, meet_all))

    early = call(
        functools.partial(early_kernel, len(chunks)),
        pltpu.VMEM((band + edge_rows, length), F32),
        5 + 3 * len(chunks) - 1,
        micros=1.6,
    )(base, got_base_edge, nudge_row, dec_high, dec_low, *keep, *send, *got[:-1])
    nudged, to_lon, from_lat = call(
        late_kernel,
        (
            pltpu.VMEM((band, length), F32),
            pltpu.VMEM((edge_rows, length), BF16),
            pltpu.VMEM((edge_rows, length), F32),
        ),
        5,
    )(early, got[-1], nudge_row, dec_high, dec_low)
    from_lon = lax.ppermute(to_lon, "lon", swap)

    field = pltpu.VMEM((band, length), F32)
    first, last_rows = call(inner_kernel, (field, field), 1, micros=4.0)(nudged)
    return call(
        outer_kernel,
        jax.ShapeDtypeStruct((channels, band_rows, length), F32),
        5,
        [pltpu.VMEM((2 * edge_rows, length), F32), pltpu.VMEM((2 * edge_rows, length), F32)],
        micros=2.2,
    )(nudged, first, last_rows, from_lon, from_lat)


def solution(mesh):
    in_specs = (
        P(("member", "lat"), "lon", None),
        P(),
        P(),
        P(),
        P(),
        P(),
        P(),
        P(None, ("member", "lat"), "lon"),
    )
    out_specs = P(None, ("member", "lat", "lon"), None)
    return jax.shard_map(body, mesh=mesh, in_specs=in_specs, out_specs=out_specs, check_vma=False)
```

```python
import functools
import math

import jax
import jax.numpy as jnp
import ml_dtypes
import numpy as np
from jax import lax
from jax.experimental import pallas as pl
from jax.experimental.pallas import tpu as pltpu
from jax.sharding import PartitionSpec as P

HEADS = 16
WIN = 8
PATCH = 4
VARS = 4
LEV = 8
KEEP = 256

time_step = 0.1
diffusion = 0.5
epsilon = 1e-05
HALF = WIN // 2
GROUP = 4
MIB = 1 << 20
F32 = jnp.float32
BF16 = jnp.bfloat16


def zonal_filter(length, kept_waves):
    lag = np.arange(length, dtype=np.float64)
    waves = np.arange(1, kept_waves, dtype=np.float64)
    kernel = 1.0 + 2.0 * np.cos(2.0 * np.pi / length * lag[:, None] * waves[None, :]).sum(1)
    at = (np.arange(length)[:, None] - np.arange(length)[None, :]) % length
    return (kernel / length)[at]


def split_high_low(matrix):
    high = matrix.astype(ml_dtypes.bfloat16)
    low = (matrix - high.astype(np.float64)).astype(ml_dtypes.bfloat16)
    return high, low


def decoded_order(total_cols, parts):
    cols = total_cols // parts
    group_cols = GROUP * WIN
    rows = []
    for part in range(parts):
        lanes = []
        for group in range(cols // group_cols):
            for b in range(PATCH):
                for place in range(group_cols):
                    col = part * cols + group * group_cols + place
                    if place % WIN < HALF:
                        col += WIN
                    lanes.append((col % total_cols) * PATCH + b)
        rows.append(lanes)
    return np.array(rows)


def place():
    lat, lon = lax.axis_index("lat"), lax.axis_index("lon")
    return lon, ((lat == 0) & (lon == 0)) | ((lat == lax.axis_size("lat") - 1) & (lon == 1))


def nudge_column(nudge_ref, rows):
    channels = nudge_ref.shape[1]
    picked = lax.broadcasted_iota(jnp.int32, (rows, channels), 0) % channels == lax.broadcasted_iota(
        jnp.int32, (rows, channels), 1
    )
    return jnp.sum(jnp.where(picked, nudge_ref[...], 0.0), axis=1, keepdims=True)


def dot(a, b):
    return lax.dot_general(a, b, (((1,), (0,)), ((), ())), preferred_element_type=F32)


def dot_nt(a, b):
    return lax.dot_general(a, b, (((1,), (1,)), ((), ())), preferred_element_type=F32)


def window_tokens(load, first, cols, emit):
    lead = lax.broadcasted_iota(jnp.int32, (2 * WIN, 1), 0) % WIN < HALF
    for pair in range(cols // (2 * WIN)):
        col = first + pair * 2 * WIN
        for r in range(HALF):
            here = load(r, col, 2 * WIN)
            after = load(r, col + 2 * WIN, WIN)
            emit(pair, r, jnp.where(lead, jnp.concatenate([here[WIN:], after], axis=0), here))


def normalise(block, gain):
    centred = block - jnp.mean(block, axis=-1, keepdims=True)
    variance = jnp.mean(centred * centred, axis=-1, keepdims=True)
    return centred * lax.rsqrt(variance + epsilon) * gain


def place_tokens(load, first, cols, gain, raw_ref, normed_ref):
    held = {}

    def emit(pair, r, block):
        group, inside = divmod(pair * 2, GROUP)
        at = (group * HALF + r) * GROUP * WIN + inside * WIN
        raw_ref[at : at + 2 * WIN, :] = block.astype(BF16)
        held[r % 2] = normalise(block, gain)
        if r % 2:
            for side in range(2):
                part = slice(side * WIN, (side + 1) * WIN)
                at = (2 * pair + side) * WIN * HALF + (r - 1) * WIN
                both = jnp.concatenate([held[0][part], held[1][part]], axis=0)
                normed_ref[at : at + 2 * WIN, :] = both.astype(BF16)

    window_tokens(load, first, cols, emit)


def project(normed_ref, wq_ref, wkv_ref, qkv_ref, copies=()):
    width = wq_ref.shape[0]
    normed = normed_ref[...]
    for i in range(3):
        if copies:
            copies[i].wait()
        weights = wq_ref[...] if i == 0 else wkv_ref[:, (i - 1) * width : i * width]
        qkv_ref[:, i * width : (i + 1) * width] = dot(normed, weights).astype(BF16)


def run_copies(sems, pairs):
    copies = [pltpu.make_async_copy(source, target, sems.at[i]) for i, (source, target) in enumerate(pairs)]
    for copy in copies:
        copy.start()
    return copies


def pack_kernel(tok_ref, state_ref, give_ref, more_ref, edge_ref, give_state_ref, whole_ref, sems):
    lon = place()[0]
    rows = give_state_ref.shape[1]
    give_rows = pl.ds(HALF * (1 - lon), HALF)
    more = more_ref.shape[1]
    pairs = [
        (tok_ref.at[give_rows, pl.ds(0, whole_ref.shape[1]), :], whole_ref),
        (tok_ref.at[give_rows, pl.ds(tok_ref.shape[1] - more, more), :], more_ref),
        (tok_ref.at[:, pl.ds(0, edge_ref.shape[1]), :], edge_ref),
        (state_ref.at[:, pl.ds(pl.multiple_of(rows * (1 - lon), 8), rows), :], give_state_ref),
    ]
    copies = run_copies(sems, pairs)
    copies[0].wait()
    give_ref[...] = whole_ref[:, : give_ref.shape[1], :]
    for copy in copies[1:]:
        copy.wait()


def edge_blocks(rows, width):
    places = []
    for block in range(rows * width[0] // (16 * 128)):
        lane, row = divmod(block, rows // 16)
        to_row, to_lane = divmod(block, width[1] // 128)
        places.append(
            (
                (slice(row * 16, row * 16 + 16), slice(lane * 128, lane * 128 + 128)),
                (slice(to_row * 16, to_row * 16 + 16), slice(to_lane * 128, to_lane * 128 + 128)),
            )
        )
    return places


def last_piece_kernel(cols, more_ref, edge_ref, base_edge_ref, out_ref):
    lon = place()[0]
    for r in range(HALF):
        own = more_ref[r].astype(F32)[more_ref.shape[1] - cols + WIN :]
        after = edge_ref[HALF * (1 - lon) + r, :WIN, :].astype(F32)
        out_ref[r * cols : (r + 1) * cols, :] = jnp.concatenate([own, after], axis=0).astype(BF16)
    for (rows, lanes), (to_rows, to_lanes) in edge_blocks(base_edge_ref.shape[0], (base_edge_ref.shape[1], out_ref.shape[1])):
        at = slice(HALF * cols + to_rows.start, HALF * cols + to_rows.stop)
        out_ref[at, to_lanes] = base_edge_ref[rows, lanes]


def own_kernel(
    tok_hbm,
    edge_ref,
    gain_ref,
    wq_hbm,
    wkv_hbm,
    wout_hbm,
    wdec_hbm,
    state_hbm,
    high_hbm,
    low_hbm,
    qkv_ref,
    wdec_t_ref,
    wmix_t_ref,
    decoded_ref,
    wq_ref,
    wkv_ref,
    state_ref,
    high_ref,
    low_ref,
    tok_ref,
    raw_ref,
    normed_ref,
    wdec_ref,
    wout_ref,
    sems,
):
    lon = place()[0]
    cols = tok_ref.shape[1]
    width = wq_ref.shape[0]
    keys, values = pl.ds(0, width), pl.ds(width, width)
    own_rows = pl.ds(HALF * lon, HALF)
    state_rows = pl.ds(pl.multiple_of(state_ref.shape[1] * lon, 8), state_ref.shape[1])
    copies = run_copies(
        sems,
        [
            (tok_hbm.at[own_rows], tok_ref),
            (wq_hbm, wq_ref),
            (wkv_hbm.at[:, keys], wkv_ref.at[:, keys]),
            (wkv_hbm.at[:, values], wkv_ref.at[:, values]),
            (wdec_hbm, wdec_ref),
            (wout_hbm, wout_ref),
            (state_hbm.at[:, state_rows, :], state_ref),
            (high_hbm, high_ref),
            (low_hbm, low_ref),
        ],
    )

    def load(r, c, size):
        if c == cols:
            return edge_ref[HALF * lon + r, :size, :].astype(F32)
        return tok_ref[r, c : c + size, :].astype(F32)

    copies[0].wait()
    place_tokens(load, 0, cols, gain_ref[...], raw_ref, normed_ref)
    project(normed_ref, wq_ref, wkv_ref, qkv_ref, copies[1:4])
    outs = wdec_ref.shape[1]
    band = outs // PATCH
    channels = band // PATCH
    row = lax.broadcasted_iota(jnp.int32, (outs, 1), 0)
    source = (row % channels) * PATCH * PATCH + (row % band // channels) * PATCH + row // band
    pick = (lax.broadcasted_iota(jnp.int32, (outs, outs), 1) == source).astype(F32).astype(BF16)
    copies[4].wait()
    wdec_t_ref[...] = dot_nt(pick, wdec_ref[...]).astype(BF16)
    decoded_ref[...] = dot_nt(wdec_t_ref[...], raw_ref[...])
    copies[5].wait()
    wmix_t_ref[...] = dot_nt(wdec_t_ref[...], wout_ref[...]).astype(BF16)
    for copy in copies[6:]:
        copy.wait()


def main_kernel(first, starts, *refs):
    x_refs, refs = refs[: len(starts)], refs[len(starts) :]
    gain_ref, qkv_own_ref, decoded_own_ref, wq_ref, wkv_ref, wmix_ref, wdec_ref, *refs = refs
    keep_ref, send_ref, raw_ref, normed_ref, qkv_ref, att_ref, decoded_ref = refs
    width = raw_ref.shape[1]
    head_size = width // HEADS
    half_cells = HALF * WIN
    cells = 2 * half_cells
    lanes = 4 * head_size
    quads = HEADS // 4
    cols = raw_ref.shape[0] // HALF
    base = first * HALF
    group_cols = GROUP * WIN
    group_half = GROUP * half_cells

    def load(r, c, size):
        which = max(i for i in range(len(starts)) if starts[i] <= c)
        at = c - starts[which]
        if which:
            at += r * group_cols
            return x_refs[which][at : at + size, :].astype(F32)
        if at + size > x_refs[which].shape[1]:
            return jnp.concatenate([load(r, c, size // 2), load(r, c + size // 2, size // 2)], axis=0)
        return x_refs[which][r, at : at + size, :].astype(F32)

    def iota(shape, dim):
        return lax.broadcasted_iota(jnp.int32, shape, dim)

    blocks = (iota((lanes, lanes), 0) // head_size == iota((lanes, lanes), 1) // head_size).astype(F32).astype(BF16)
    split_rows = iota((cells, 2 * cells), 0) // half_cells != iota((cells, 2 * cells), 1) % cells // half_cells
    bias = jnp.where(split_rows & place()[1], -1e30, 0.0)
    first_head = iota((cells, 2 * cells), 1) < cells
    scale = 1.0 / (math.sqrt(head_size) * math.log(2.0))

    def project_quad(quad):
        normed = normed_ref[...]
        at = quad * lanes
        for offset, weights in (
            (0, wq_ref[:, at : at + lanes]),
            (width, wkv_ref[:, at : at + lanes]),
            (2 * width, wkv_ref[:, width + at : width + at + lanes]),
        ):
            qkv_ref[:, offset + at : offset + at + lanes] = dot(normed, weights).astype(BF16)

    def part(window, quad, offset):
        columns = slice(offset + quad * lanes, offset + (quad + 1) * lanes)
        got = slice(window * half_cells, (window + 1) * half_cells)
        own = slice(base + got.start, base + got.stop)
        return jnp.concatenate([qkv_own_ref[own, columns], qkv_ref[got, columns]], axis=0)

    def score(window, quad):
        keys = jnp.concatenate([part(window, quad, width)] * 4, axis=0) * blocks
        return dot_nt(part(window, quad, 0), keys)

    def weigh(scores):
        outs = []
        for side in range(2):
            two = scores[:, side * 2 * cells : (side + 1) * 2 * cells] + bias
            left = jnp.max(jnp.where(first_head, two, -jnp.inf), axis=-1, keepdims=True)
            right = jnp.max(jnp.where(first_head, -jnp.inf, two), axis=-1, keepdims=True)
            peak = jnp.where(first_head, left, right)
            outs.append(jnp.exp2((two - peak) * scale).astype(BF16))
        return jnp.concatenate(outs, axis=1)

    def mix(group, quad, weights):
        sums = dot(jnp.concatenate(weights, axis=0), blocks)
        mixed = []
        for i in range(GROUP):
            values = jnp.concatenate([part(group * GROUP + i, quad, 2 * width)] * 4, axis=0) * blocks
            mixed.append(dot(weights[i], values) / sums[i * cells : (i + 1) * cells])
        tiles = [mixed[i][at : at + WIN] for at in range(0, cells, WIN) for i in range(GROUP)]
        rows = slice(group * 2 * group_half, (group + 1) * 2 * group_half)
        att_ref[rows, quad * lanes : (quad + 1) * lanes] = jnp.concatenate(tiles, axis=0).astype(BF16)

    def decode(group):
        rows = slice(group * 2 * group_half, (group + 1) * 2 * group_half)
        decoded = dot_nt(wmix_ref[...], att_ref[rows, :])
        got = slice(group * group_half, (group + 1) * group_half)
        own = slice(base + got.start, base + got.stop)
        band = decoded.shape[0] // PATCH
        out_lanes = slice(group * group_cols * PATCH, (group + 1) * group_cols * PATCH)
        lane_part = iota((band, group_half), 1) // group_cols
        for half, more, out_ref in ((0, decoded_own_ref[:, own], keep_ref), (1, decoded_ref[:, got], send_ref)):
            total = decoded[:, half * group_half : (half + 1) * group_half] + more
            from_b = [total[b * band : (b + 1) * band] for b in range(PATCH)]
            for r in range(HALF):
                placed = None
                for b in range(PATCH):
                    moved = from_b[b]
                    if b != r:
                        moved = pltpu.roll(moved, (b - r) % PATCH * group_cols, axis=1)
                    placed = moved if placed is None else jnp.where(lane_part == b, moved, placed)
                out_ref[r * band : (r + 1) * band, out_lanes] = placed.astype(BF16)

    place_tokens(load, first, cols, gain_ref[...], raw_ref, normed_ref)
    project_quad(0)
    units = [(group, quad) for group in range(cols // group_cols) for quad in range(quads)]
    weights = None
    for i in range(len(units) + 1):
        if i < len(units):
            group, quad = units[i]
            scores = [score(group * GROUP + w, quad) for w in range(GROUP)]
            if group == 0 and quad + 1 < quads:
                project_quad(quad + 1)
            if i == quads - 1:
                decoded_ref[...] = dot_nt(wdec_ref[...], raw_ref[...])
        if i > 0:
            mix(*units[i - 1], weights)
            if units[i - 1][1] == quads - 1:
                decode(units[i - 1][0])
        if i < len(units):
            weights = [weigh(x) for x in scores]

    lon = place()[0]
    total_rows = keep_ref.shape[0]
    edge = send_ref.shape[0] - total_rows
    near = pl.ds(pl.multiple_of(lon * (total_rows - edge), edge), edge)
    send_ref[total_rows:, :] = keep_ref[near, :]


def unfiltered(field, high_ref, low_ref, strength):
    high = field.astype(BF16)
    low = (field - high.astype(F32)).astype(BF16)
    smooth = dot(high, high_ref[...]) + (dot(high, low_ref[...]) + dot(low, high_ref[...]))
    return field - strength * smooth


def state_kernel(state_ref, got_ref, nudge_ref, high_ref, low_ref, out_ref, edge_ref, whole_ref):
    lon = place()[0]
    channels, own_rows, cols = got_ref.shape
    own_lanes = pl.ds(pl.multiple_of(lon * cols, 128), cols)
    got_lanes = pl.ds(pl.multiple_of((1 - lon) * cols, 128), cols)
    for y in range(0, own_rows, 8):
        for ch in range(0, channels, 8):
            own = jnp.swapaxes(state_ref[ch : ch + 8, y : y + 8, :], 0, 1)
            got = jnp.swapaxes(got_ref[ch : ch + 8, y : y + 8, :], 0, 1)
            for i in range(8):
                rows = slice((y + i) * channels + ch, (y + i) * channels + ch + 8)
                whole_ref[rows, own_lanes] = own[i]
                whole_ref[rows, got_lanes] = got[i]
    step = PATCH * channels
    strength = nudge_column(nudge_ref, step)
    for at in range(0, out_ref.shape[0], step):
        out_ref[at : at + step, :] = unfiltered(whole_ref[at : at + step, :], high_ref, low_ref, strength)
    edge = edge_ref.shape[0]
    near = pl.ds(pl.multiple_of(lon * (out_ref.shape[0] - edge), edge), edge)
    edge_ref[...] = out_ref[near, :].astype(BF16)


def filter_rows(dec, first, high_ref, low_ref):
    rows = pl.ds(pl.multiple_of(first, 128), dec.shape[1])
    return dot(dec, high_ref[rows, :]) + dot(dec, low_ref[rows, :])


def early_kernel(base_ref, piece_ref, nudge_ref, high_ref, low_ref, *refs):
    *refs, out_ref = refs
    keep_refs, send_refs = refs[: len(refs) // 2], refs[len(refs) // 2 :]
    lon = place()[0]
    total = base_ref.shape[0]
    edge = out_ref.shape[0] - total
    far = pl.ds(pl.multiple_of((1 - lon) * (total - edge), edge), edge)
    own = [jnp.concatenate([keep[...], send[far, :]], axis=0) for keep, send in zip(keep_refs, send_refs)]
    decoded = jnp.concatenate(own, axis=1)
    smooth = filter_rows(decoded, lon * (high_ref.shape[0] // 3), high_ref, low_ref)
    step = PATCH * nudge_ref.shape[1]
    strength = nudge_column(nudge_ref, step)
    for at in range(0, total, step):
        out_ref[at : at + step, :] = base_ref[at : at + step, :] + strength * smooth[at : at + step]
    length, width = out_ref.shape[1], piece_ref.shape[1]
    first = piece_ref.shape[0] - edge * length // width
    for (rows, lanes), (at_rows, at_lanes) in edge_blocks(edge, (length, width)):
        base_edge = piece_ref[first + at_rows.start : first + at_rows.stop, at_lanes].astype(F32)
        term = strength[rows] * smooth[total + rows.start : total + rows.stop, lanes]
        out_ref[total + rows.start : total + rows.stop, lanes] = base_edge + term


def add_kernel(skip, early_ref, got_ref, nudge_ref, high_ref, low_ref, out_ref):
    smooth = filter_rows(got_ref[...], place()[0] * (high_ref.shape[0] // 3) + high_ref.shape[0] // 3 + skip, high_ref, low_ref)
    step = PATCH * nudge_ref.shape[1]
    strength = nudge_column(nudge_ref, step)
    for at in range(0, out_ref.shape[0], step):
        rows = slice(at, min(at + step, out_ref.shape[0]))
        out_ref[rows, :] = early_ref[rows, :] + strength[: rows.stop - at] * smooth[rows]


def last_rows(high_ref, got_ref):
    part = high_ref.shape[0] // 3
    return place()[0] * part + 2 * part - got_ref.shape[1]


def near_kernel(early_ref, got_ref, nudge_ref, high_ref, low_ref, near_ref):
    lon = place()[0]
    edge = near_ref.shape[0]
    total = early_ref.shape[0] - edge
    far = pl.ds(pl.multiple_of((1 - lon) * (total - edge), edge), edge)
    smooth = filter_rows(got_ref[far, :], last_rows(high_ref, got_ref), high_ref, low_ref)
    near_ref[...] = (early_ref[far, :] + nudge_column(nudge_ref, edge) * smooth).astype(BF16)


def row_tile(ref, row, var):
    at = row * (VARS * LEV) + var * LEV
    return pl.ds(at if isinstance(at, int) else pl.multiple_of(at, LEV), LEV)


def tendency_row(south, centre, north, use, only=range(VARS)):
    push_u, push_v = (0.5 * time_step) * centre(0), (0.5 * time_step) * centre(1)
    calm = diffusion * time_step
    to_east, to_west, to_north, to_south = calm - push_u, calm + push_u, calm - push_v, calm + push_v
    for var in only:
        field = centre(var)
        length = field.shape[1]
        step = to_east * pltpu.roll(field, length - 1, axis=1) + to_west * pltpu.roll(field, 1, axis=1)
        step = step + (to_north * north(var) + to_south * south(var))
        use(var, field, step - (4.0 * calm) * field)


def inner_kernel(early_ref, got_ref, nudge_ref, high_ref, low_ref, field_ref, lat_ref, first_ref, last_ref):
    total = field_ref.shape[0]
    edge = lat_ref.shape[0]
    rows = total // (VARS * LEV)
    smooth = filter_rows(got_ref[...], last_rows(high_ref, got_ref), high_ref, low_ref)
    step = PATCH * nudge_ref.shape[1]
    strength = nudge_column(nudge_ref, step)
    for at in range(0, total, step):
        field_ref[at : at + step, :] = early_ref[at : at + step, :] + strength * smooth[at : at + step]
    lat_ref[...] = early_ref[total:, :] + strength[:edge] * smooth[total:]

    def reader(ref, row):
        return lambda var: ref[row_tile(ref, row, var), :]

    def section(ref, row, use):
        tendency_row(reader(ref, row - 1), reader(ref, row), reader(ref, row + 1), use)

    for row in range(1, rows - 1):

        def put_first(var, field, step):
            first_ref[row_tile(first_ref, row, var), :] = field + step

        section(field_ref, row, put_first)
    for row in range(2, rows - 2):

        def put_last(var, field, step):
            nudged = field_ref[row_tile(field_ref, row, var), :]
            last_ref[row_tile(last_ref, row, var), :] = 0.5 * (nudged + field + step)

        section(first_ref, row, put_last)


def outer_kernel(field_ref, first_ref, last_ref, lon_ref, lat_ref, out_hbm, ext_ref, edge_ref, out_ref, sems):
    channels, rows, length = out_ref.shape
    lon, pole = place()
    is_top = lon == 0
    from_lon = lon_ref[...].astype(F32)
    from_lat = jnp.where(pole, 0.0, lat_ref[...])
    edge = from_lon.shape[0]
    ext_ref[:edge, :] = jnp.where(is_top, from_lat, from_lon)
    ext_ref[edge:, :] = jnp.where(is_top, from_lon, from_lat)

    def field(row):
        def read(var):
            if row < 0:
                return ext_ref[row_tile(ext_ref, row + 2, var), :]
            if row >= rows:
                return ext_ref[row_tile(ext_ref, row - rows + 2, var), :]
            return field_ref[row_tile(field_ref, row, var), :]

        return read

    def first(row):
        def read(var):
            if row < 1:
                return edge_ref[row_tile(edge_ref, row + 1, var), :]
            if row >= rows - 1:
                return edge_ref[row_tile(edge_ref, row - rows + 3, var), :]
            return first_ref[row_tile(first_ref, row, var), :]

        return read

    outside = jnp.where(pole, 0.0, 1.0)
    for row in (-1, 0, rows - 1, rows):
        keep = None
        if row < 0:
            keep = jnp.where(is_top, outside, 1.0)
        if row >= rows:
            keep = jnp.where(is_top, 1.0, outside)

        def put(var, value, step):
            total = value + step
            at = row + 1 if row < 1 else row - rows + 3
            edge_ref[row_tile(edge_ref, at, var), :] = total if keep is None else total * keep

        tendency_row(field(row - 1), field(row), field(row + 1), put)
    copies = []
    for var in range(VARS):
        levels = slice(var * LEV, (var + 1) * LEV)
        outer = {}
        for row in (0, 1, rows - 2, rows - 1):

            def put(var, value, step):
                outer[row, var] = 0.5 * (field(row)(var) + value + step)

            tendency_row(first(row - 1), first(row), first(row + 1), put, [var])
        for y in range(0, rows, 8):
            block = []
            for row in range(y, y + 8):
                tile = outer[row, var] if (row, var) in outer else last_ref[row_tile(last_ref, row, var), :]
                block.append(tile[None])
            out_ref[levels, y : y + 8, :] = jnp.swapaxes(jnp.concatenate(block, axis=0), 0, 1)
        part = pl.ds(var * LEV, LEV)
        copies.append(pltpu.make_async_copy(out_ref.at[part], out_hbm.at[part], sems.at[var]))
        copies[-1].start()
    for copy in copies:
        copy.wait()


def work(micros):
    return pl.CostEstimate(flops=int(micros * 1e9), bytes_accessed=int(micros * 1e6), transcendentals=0)


def call(kernel, out_shape, n_in, scratch=(), vmem=24, micros=1.0):
    vmem_spec = pl.BlockSpec(memory_space=pltpu.VMEM)
    many = isinstance(out_shape, (tuple, list))
    return pl.pallas_call(
        kernel,
        out_shape=out_shape,
        in_specs=[vmem_spec] * n_in,
        out_specs=[vmem_spec] * len(out_shape) if many else vmem_spec,
        scratch_shapes=list(scratch),
        cost_estimate=work(micros),
        compiler_params=pltpu.CompilerParams(vmem_limit_bytes=vmem * MIB),
    )


def body(tokens, ln_gain, w_query, w_keyval, w_out, w_dec, nudge, state):
    tok_rows, tok_cols, width = tokens.shape
    channels, state_rows, state_cols = state.shape
    n_lat, n_lon = lax.axis_size("lat"), lax.axis_size("lon")
    lon = lax.axis_index("lon")
    total_cols = tok_cols * n_lon
    length = state_cols * n_lon
    band_rows = state_rows // n_lon
    both = ("lat", "lon")
    tokens_half = tok_cols * HALF
    band = band_rows * channels


    def at(row, col):
        return row * n_lon + col

    last = n_lat - 1
    swap = [(0, 1), (1, 0)]
    shift = [(at(i, 0), at(i + 1, 0)) for i in range(last)] + [(at(last, 0), at(last, 1))]
    shift += [(at(i, 1), at(i - 1, 1)) for i in range(1, n_lat)] + [(at(0, 1), at(0, 0))]
    meet = [(at(i, 1), at(i + 1, 0)) for i in range(last)] + [(at(i + 1, 0), at(i, 1)) for i in range(last)]
    meet_all = meet + [(at(0, 0), at(0, 0)), (at(last, 1), at(last, 1))]

    step = GROUP * WIN
    split = max(tok_cols - step, step)
    chunks = [(0, split)] + ([(split, step)] if split < tok_cols else [])
    cuts = [0] + [split + WIN] * (len(chunks) - 1) + [tok_cols]

    hbm, vmem = pl.BlockSpec(memory_space=pltpu.HBM), pl.BlockSpec(memory_space=pltpu.VMEM)
    in_hbm = functools.partial(pltpu.with_memory_space_constraint, memory_space=pltpu.HBM)
    give, more, give_edge, give_state = pl.pallas_call(
        pack_kernel,
        out_shape=[
            pltpu.VMEM((HALF, cuts[1], width), BF16),
            pltpu.VMEM((HALF, step, width), BF16),
            pltpu.VMEM((tok_rows, 2 * WIN, width), BF16),
            pltpu.VMEM((channels, band_rows, state_cols), F32),
        ],
        in_specs=[hbm, hbm],
        out_specs=[vmem] * 4,
        scratch_shapes=[
            pltpu.VMEM((HALF, split + 2 * WIN, width), BF16),
            pltpu.SemaphoreType.DMA((4,)),
        ],
        compiler_params=pltpu.CompilerParams(vmem_limit_bytes=12 * MIB),
    )(in_hbm(tokens), in_hbm(state))
    edge_tokens = lax.ppermute(give_edge, "lon", swap)
    got_tokens = [lax.ppermute(give, both, shift)]
    got_state = lax.ppermute(give_state, "lon", swap)

    gain = ln_gain[None, :]
    nudge_row = nudge[None, :]
    matrix = zonal_filter(length, KEEP)
    high, low = (jnp.asarray(m) for m in split_high_low(matrix))
    order = decoded_order(total_cols, n_lon)
    order = np.concatenate([order[0], order[1], order[0]])
    dec_high, dec_low = (jnp.asarray(m) for m in split_high_low(matrix[order]))

    n_out = w_dec.shape[1]
    qkv_own, w_dec_t, w_mix_t, decoded_own, *weights, own_state, high, low = pl.pallas_call(
        own_kernel,
        out_shape=[
            pltpu.VMEM((tokens_half, 3 * width), BF16),
            pltpu.VMEM((n_out, width), BF16),
            pltpu.VMEM((n_out, width), BF16),
            pltpu.VMEM((n_out, tokens_half), F32),
            pltpu.VMEM(w_query.shape, BF16),
            pltpu.VMEM(w_keyval.shape, BF16),
            pltpu.VMEM((channels, band_rows, state_cols), F32),
            pltpu.VMEM((length, length), BF16),
            pltpu.VMEM((length, length), BF16),
        ],
        in_specs=[hbm, vmem, vmem] + [hbm] * 7,
        out_specs=[vmem] * 9,
        scratch_shapes=[
            pltpu.VMEM((HALF, tok_cols, width), BF16),
            pltpu.VMEM((tokens_half, width), BF16),
            pltpu.VMEM((tokens_half, width), BF16),
            pltpu.VMEM(w_dec.shape, BF16),
            pltpu.VMEM(w_out.shape, BF16),
            pltpu.SemaphoreType.DMA((9,)),
        ],
        cost_estimate=work(7.5),
        compiler_params=pltpu.CompilerParams(vmem_limit_bytes=32 * MIB),
    )(in_hbm(tokens), edge_tokens, gain, in_hbm(w_query), in_hbm(w_keyval), in_hbm(w_out), in_hbm(w_dec), in_hbm(state), in_hbm(high), in_hbm(low))

    edge_rows = 2 * channels
    got_state, qkv_own = lax.optimization_barrier((got_state, qkv_own))
    base, base_edge = call(
        state_kernel,
        (pltpu.VMEM((band, length), F32), pltpu.VMEM((edge_rows, length), BF16)),
        5,
        [pltpu.VMEM((band, length), F32)],
        micros=2.7,
    )(own_state, got_state, nudge_row, high, low)
    their_base_edge = lax.ppermute(base_edge, "lon", swap)
    last_cols = tok_cols - cuts[1] + WIN
    last_rows = HALF * last_cols + edge_rows * length // width
    last_piece = call(functools.partial(last_piece_kernel, last_cols), pltpu.VMEM((last_rows, width), BF16), 3, vmem=12)(
        more, edge_tokens, their_base_edge
    )
    got_tokens.append(lax.ppermute(last_piece, both, shift))
    gain, last_piece = lax.optimization_barrier((gain, last_piece))

    keep, send, got = [], [], []
    for i, (first, cols) in enumerate(chunks):
        kept, sent = call(
            functools.partial(main_kernel, first, cuts[: i + 1]),
            (pltpu.VMEM((band, cols * PATCH), BF16), pltpu.VMEM((band + edge_rows, cols * PATCH), BF16)),
            7 + i + 1,
            [
                pltpu.VMEM((cols * HALF, width), BF16),
                pltpu.VMEM((cols * HALF, width), BF16),
                pltpu.VMEM((cols * HALF, 3 * width), BF16),
                pltpu.VMEM((cols * WIN, width), BF16),
                pltpu.VMEM((n_out, cols * HALF), F32),
            ],
            micros=3.0 * (cols // step),
        )(*got_tokens[: i + 1], gain, qkv_own, decoded_own, *weights, w_mix_t, w_dec_t)
        gain, kept = lax.optimization_barrier((gain, kept))
        keep.append(kept)
        send.append(sent)
        got.append(lax.ppermute(sent, both, meet_all))

    sums = pltpu.VMEM((band + edge_rows, length), F32)
    early = call(early_kernel, sums, 5 + 2 * len(chunks), micros=1.2)(
        base, got_tokens[-1], nudge_row, dec_high, dec_low, *keep, *send
    )
    skip = 0
    for part in got[:-1]:
        early = call(functools.partial(add_kernel, skip), sums, 5)(early, part, nudge_row, dec_high, dec_low)
        skip += part.shape[1]
    late = (early, got[-1], nudge_row, dec_high, dec_low)
    to_lon = call(near_kernel, pltpu.VMEM((edge_rows, length), BF16), 5)(*late)
    from_lon = lax.ppermute(to_lon, "lon", swap)

    field = pltpu.VMEM((band, length), F32)
    edge = pltpu.VMEM((edge_rows, length), F32)
    nudged, from_lat, first, last_inner = call(inner_kernel, (field, edge, field, field), 5, micros=2.0)(*late)
    result = (channels, band_rows, length)
    return pl.pallas_call(
        outer_kernel,
        out_shape=jax.ShapeDtypeStruct(result, F32),
        in_specs=[vmem] * 5,
        out_specs=hbm,
        scratch_shapes=[
            pltpu.VMEM((2 * edge_rows, length), F32),
            pltpu.VMEM((2 * edge_rows, length), F32),
            pltpu.VMEM(result, F32),
            pltpu.SemaphoreType.DMA((VARS,)),
        ],
        cost_estimate=work(1.5),
        compiler_params=pltpu.CompilerParams(vmem_limit_bytes=24 * MIB),
    )(nudged, first, last_inner, from_lon, from_lat)


def solution(mesh):
    in_specs = (
        P(("member", "lat"), "lon", None),
        P(),
        P(),
        P(),
        P(),
        P(),
        P(),
        P(None, ("member", "lat"), "lon"),
    )
    out_specs = P(None, ("member", "lat", "lon"), None)
    return jax.shard_map(body, mesh=mesh, in_specs=in_specs, out_specs=out_specs, check_vma=False)
```

```python
import functools
import math

import jax
import jax.numpy as jnp
import ml_dtypes
import numpy as np
from jax import lax
from jax.experimental import pallas as pl
from jax.experimental.pallas import tpu as pltpu
from jax.sharding import PartitionSpec as P

HEADS = 16
WIN = 8
PATCH = 4
VARS = 4
LEV = 8
KEEP = 256

time_step = 0.1
diffusion = 0.5
epsilon = 1e-05
HALF = WIN // 2
GROUP = 4
MIB = 1 << 20
F32 = jnp.float32
BF16 = jnp.bfloat16


def zonal_filter(length, kept_waves):
    lag = np.arange(length, dtype=np.float64)
    waves = np.arange(1, kept_waves, dtype=np.float64)
    kernel = 1.0 + 2.0 * np.cos(2.0 * np.pi / length * lag[:, None] * waves[None, :]).sum(1)
    at = (np.arange(length)[:, None] - np.arange(length)[None, :]) % length
    return (kernel / length)[at]


def split_high_low(matrix):
    high = matrix.astype(ml_dtypes.bfloat16)
    low = (matrix - high.astype(np.float64)).astype(ml_dtypes.bfloat16)
    return high, low


def decoded_order(total_cols, parts):
    cols = total_cols // parts
    group_cols = GROUP * WIN
    rows = []
    for part in range(parts):
        lanes = []
        for group in range(cols // group_cols):
            for b in range(PATCH):
                for place in range(group_cols):
                    col = part * cols + group * group_cols + place
                    if place % WIN < HALF:
                        col += WIN
                    lanes.append((col % total_cols) * PATCH + b)
        rows.append(lanes)
    return np.array(rows)


def place():
    lat, lon = lax.axis_index("lat"), lax.axis_index("lon")
    return lon, ((lat == 0) & (lon == 0)) | ((lat == lax.axis_size("lat") - 1) & (lon == 1))


def nudge_column(nudge_ref, rows):
    channels = nudge_ref.shape[1]
    picked = lax.broadcasted_iota(jnp.int32, (rows, channels), 0) % channels == lax.broadcasted_iota(
        jnp.int32, (rows, channels), 1
    )
    return jnp.sum(jnp.where(picked, nudge_ref[...], 0.0), axis=1, keepdims=True)


def dot(a, b):
    return lax.dot_general(a, b, (((1,), (0,)), ((), ())), preferred_element_type=F32)


def dot_nt(a, b):
    return lax.dot_general(a, b, (((1,), (1,)), ((), ())), preferred_element_type=F32)


def window_columns(here, after):
    lead = lax.broadcasted_iota(jnp.int32, (2 * WIN, 1), 0) % WIN < HALF
    here, after = here.astype(F32), after.astype(F32)
    return jnp.where(lead, jnp.concatenate([here[WIN:], after], axis=0), here)


def normalise(block, gain):
    centred = block - jnp.mean(block, axis=-1, keepdims=True)
    variance = jnp.mean(centred * centred, axis=-1, keepdims=True)
    return centred * lax.rsqrt(variance + epsilon) * gain


def place_tokens(load, cols, gain, raw_ref, normed_ref):
    held = {}

    def emit(pair, r, block):
        group, inside = divmod(pair * 2, GROUP)
        at = (group * HALF + r) * GROUP * WIN + inside * WIN
        raw_ref[at : at + 2 * WIN, :] = block.astype(BF16)
        held[r % 2] = normalise(block, gain)
        if r % 2:
            for side in range(2):
                part = slice(side * WIN, (side + 1) * WIN)
                at = (2 * pair + side) * WIN * HALF + (r - 1) * WIN
                both = jnp.concatenate([held[0][part], held[1][part]], axis=0)
                normed_ref[at : at + 2 * WIN, :] = both.astype(BF16)

    for pair in range(cols // (2 * WIN)):
        for r in range(HALF):
            emit(pair, r, load(pair, r))


def project(normed_ref, wq_ref, wkv_ref, qkv_ref, copies=()):
    width = wq_ref.shape[0]
    normed = normed_ref[...]
    for i in range(3):
        if copies:
            copies[i].wait()
        weights = wq_ref[...] if i == 0 else wkv_ref[:, (i - 1) * width : i * width]
        qkv_ref[:, i * width : (i + 1) * width] = dot(normed, weights).astype(BF16)


def run_copies(sems, pairs):
    copies = [pltpu.make_async_copy(source, target, sems.at[i]) for i, (source, target) in enumerate(pairs)]
    for copy in copies:
        copy.start()
    return copies


def pack_kernel(tok_ref, state_ref, give_ref, more_ref, edge_ref, give_state_ref, whole_ref, sems):
    lon = place()[0]
    rows = give_state_ref.shape[1]
    give_rows = pl.ds(HALF * (1 - lon), HALF)
    more = more_ref.shape[1]
    pairs = [
        (tok_ref.at[give_rows, pl.ds(0, whole_ref.shape[1]), :], whole_ref),
        (tok_ref.at[give_rows, pl.ds(tok_ref.shape[1] - more, more), :], more_ref),
        (tok_ref.at[:, pl.ds(0, edge_ref.shape[1]), :], edge_ref),
        (state_ref.at[:, pl.ds(pl.multiple_of(rows * (1 - lon), 8), rows), :], give_state_ref),
    ]
    copies = run_copies(sems, pairs)
    copies[0].wait()
    for r in range(HALF):
        for at in range(0, give_ref.shape[1], 2 * WIN):
            after = whole_ref[r, at + 2 * WIN : at + 3 * WIN, :]
            columns = window_columns(whole_ref[r, at : at + 2 * WIN, :], after)
            give_ref[r, at : at + 2 * WIN, :] = columns.astype(BF16)
    for copy in copies[1:]:
        copy.wait()


def edge_blocks(rows, width):
    places = []
    for block in range(rows * width[0] // (16 * 128)):
        lane, row = divmod(block, rows // 16)
        to_row, to_lane = divmod(block, width[1] // 128)
        places.append(
            (
                (slice(row * 16, row * 16 + 16), slice(lane * 128, lane * 128 + 128)),
                (slice(to_row * 16, to_row * 16 + 16), slice(to_lane * 128, to_lane * 128 + 128)),
            )
        )
    return places


def last_piece_kernel(more_ref, edge_ref, base_edge_ref, out_ref):
    lon = place()[0]
    cols = more_ref.shape[1]
    for r in range(HALF):
        for at in range(0, cols, 2 * WIN):
            if at + 2 * WIN < cols:
                after = more_ref[r, at + 2 * WIN : at + 3 * WIN, :]
            else:
                after = edge_ref[HALF * (1 - lon) + r, :WIN, :]
            columns = window_columns(more_ref[r, at : at + 2 * WIN, :], after)
            out_ref[r * cols + at : r * cols + at + 2 * WIN, :] = columns.astype(BF16)
    widths = (base_edge_ref.shape[1], out_ref.shape[1])
    for (rows, lanes), (to_rows, to_lanes) in edge_blocks(base_edge_ref.shape[0], widths):
        at = slice(HALF * cols + to_rows.start, HALF * cols + to_rows.stop)
        out_ref[at, to_lanes] = base_edge_ref[rows, lanes]


def own_kernel(
    tok_hbm,
    edge_ref,
    gain_ref,
    wq_hbm,
    wkv_hbm,
    wout_hbm,
    wdec_hbm,
    state_hbm,
    high_hbm,
    low_hbm,
    qkv_ref,
    wdec_t_ref,
    wmix_t_ref,
    decoded_ref,
    wq_ref,
    wkv_ref,
    state_ref,
    high_ref,
    low_ref,
    tok_ref,
    raw_ref,
    normed_ref,
    wdec_ref,
    wout_ref,
    sems,
):
    lon = place()[0]
    cols = tok_ref.shape[1]
    width = wq_ref.shape[0]
    keys, values = pl.ds(0, width), pl.ds(width, width)
    own_rows = pl.ds(HALF * lon, HALF)
    state_rows = pl.ds(pl.multiple_of(state_ref.shape[1] * lon, 8), state_ref.shape[1])
    copies = run_copies(
        sems,
        [
            (tok_hbm.at[own_rows], tok_ref),
            (wq_hbm, wq_ref),
            (wkv_hbm.at[:, keys], wkv_ref.at[:, keys]),
            (wkv_hbm.at[:, values], wkv_ref.at[:, values]),
            (wdec_hbm, wdec_ref),
            (wout_hbm, wout_ref),
            (state_hbm.at[:, state_rows, :], state_ref),
            (high_hbm, high_ref),
            (low_hbm, low_ref),
        ],
    )

    def load(pair, r):
        at = pair * 2 * WIN
        if at + 2 * WIN < cols:
            after = tok_ref[r, at + 2 * WIN : at + 3 * WIN, :]
        else:
            after = edge_ref[HALF * lon + r, :WIN, :]
        return window_columns(tok_ref[r, at : at + 2 * WIN, :], after)

    copies[0].wait()
    place_tokens(load, cols, gain_ref[...], raw_ref, normed_ref)
    project(normed_ref, wq_ref, wkv_ref, qkv_ref, copies[1:4])
    outs = wdec_ref.shape[1]
    band = outs // PATCH
    channels = band // PATCH
    row = lax.broadcasted_iota(jnp.int32, (outs, 1), 0)
    source = (row % channels) * PATCH * PATCH + (row % band // channels) * PATCH + row // band
    pick = (lax.broadcasted_iota(jnp.int32, (outs, outs), 1) == source).astype(F32).astype(BF16)
    copies[4].wait()
    wdec_t_ref[...] = dot_nt(pick, wdec_ref[...]).astype(BF16)
    decoded_ref[...] = dot_nt(wdec_t_ref[...], raw_ref[...])
    copies[5].wait()
    wmix_t_ref[...] = dot_nt(wdec_t_ref[...], wout_ref[...]).astype(BF16)
    for copy in copies[6:]:
        copy.wait()


def main_kernel(first, x_ref, *refs):
    gain_ref, qkv_own_ref, decoded_own_ref, wq_ref, wkv_ref, wmix_ref, wdec_ref, *refs = refs
    keep_ref, send_ref, raw_ref, normed_ref, qkv_ref, att_ref, decoded_ref = refs
    width = raw_ref.shape[1]
    head_size = width // HEADS
    half_cells = HALF * WIN
    cells = 2 * half_cells
    lanes = 4 * head_size
    quads = HEADS // 4
    cols = raw_ref.shape[0] // HALF
    base = first * HALF
    group_cols = GROUP * WIN
    group_half = GROUP * half_cells

    def load(pair, r):
        at = pair * 2 * WIN
        if len(x_ref.shape) == 2:
            return x_ref[r * cols + at : r * cols + at + 2 * WIN, :].astype(F32)
        return x_ref[r, at : at + 2 * WIN, :].astype(F32)

    def iota(shape, dim):
        return lax.broadcasted_iota(jnp.int32, shape, dim)

    blocks = (iota((lanes, lanes), 0) // head_size == iota((lanes, lanes), 1) // head_size).astype(F32).astype(BF16)
    split_rows = iota((cells, 2 * cells), 0) // half_cells != iota((cells, 2 * cells), 1) % cells // half_cells
    bias = jnp.where(split_rows & place()[1], -1e30, 0.0)
    first_head = iota((cells, 2 * cells), 1) < cells
    scale = 1.0 / (math.sqrt(head_size) * math.log(2.0))

    def project_quad(quad):
        normed = normed_ref[...]
        at = quad * lanes
        for offset, weights in (
            (0, wq_ref[:, at : at + lanes]),
            (width, wkv_ref[:, at : at + lanes]),
            (2 * width, wkv_ref[:, width + at : width + at + lanes]),
        ):
            qkv_ref[:, offset + at : offset + at + lanes] = dot(normed, weights).astype(BF16)

    def part(window, quad, offset):
        columns = slice(offset + quad * lanes, offset + (quad + 1) * lanes)
        got = slice(window * half_cells, (window + 1) * half_cells)
        own = slice(base + got.start, base + got.stop)
        return jnp.concatenate([qkv_own_ref[own, columns], qkv_ref[got, columns]], axis=0)

    def score(window, quad):
        keys = jnp.concatenate([part(window, quad, width)] * 4, axis=0) * blocks
        return dot_nt(part(window, quad, 0), keys)

    def weigh(scores):
        outs = []
        for side in range(2):
            two = scores[:, side * 2 * cells : (side + 1) * 2 * cells] + bias
            left = jnp.max(jnp.where(first_head, two, -jnp.inf), axis=-1, keepdims=True)
            right = jnp.max(jnp.where(first_head, -jnp.inf, two), axis=-1, keepdims=True)
            peak = jnp.where(first_head, left, right)
            outs.append(jnp.exp2((two - peak) * scale).astype(BF16))
        return jnp.concatenate(outs, axis=1)

    def mix(group, quad, weights):
        sums = dot(jnp.concatenate(weights, axis=0), blocks)
        mixed = []
        for i in range(GROUP):
            values = jnp.concatenate([part(group * GROUP + i, quad, 2 * width)] * 4, axis=0) * blocks
            mixed.append(dot(weights[i], values) / sums[i * cells : (i + 1) * cells])
        tiles = [mixed[i][at : at + WIN] for at in range(0, cells, WIN) for i in range(GROUP)]
        rows = slice(group * 2 * group_half, (group + 1) * 2 * group_half)
        att_ref[rows, quad * lanes : (quad + 1) * lanes] = jnp.concatenate(tiles, axis=0).astype(BF16)

    def decode(group):
        rows = slice(group * 2 * group_half, (group + 1) * 2 * group_half)
        decoded = dot_nt(wmix_ref[...], att_ref[rows, :])
        got = slice(group * group_half, (group + 1) * group_half)
        own = slice(base + got.start, base + got.stop)
        band = decoded.shape[0] // PATCH
        out_lanes = slice(group * group_cols * PATCH, (group + 1) * group_cols * PATCH)
        lane_part = iota((band, group_half), 1) // group_cols
        for half, more, out_ref in ((0, decoded_own_ref[:, own], keep_ref), (1, decoded_ref[:, got], send_ref)):
            total = decoded[:, half * group_half : (half + 1) * group_half] + more
            from_b = [total[b * band : (b + 1) * band] for b in range(PATCH)]
            for r in range(HALF):
                placed = None
                for b in range(PATCH):
                    moved = from_b[b]
                    if b != r:
                        moved = pltpu.roll(moved, (b - r) % PATCH * group_cols, axis=1)
                    placed = moved if placed is None else jnp.where(lane_part == b, moved, placed)
                out_ref[r * band : (r + 1) * band, out_lanes] = placed.astype(BF16)

    place_tokens(load, cols, gain_ref[...], raw_ref, normed_ref)
    project_quad(0)
    units = [(group, quad) for group in range(cols // group_cols) for quad in range(quads)]
    weights = None
    for i in range(len(units) + 1):
        if i < len(units):
            group, quad = units[i]
            scores = [score(group * GROUP + w, quad) for w in range(GROUP)]
            if group == 0 and quad + 1 < quads:
                project_quad(quad + 1)
            if i == quads - 1:
                decoded_ref[...] = dot_nt(wdec_ref[...], raw_ref[...])
        if i > 0:
            mix(*units[i - 1], weights)
            if units[i - 1][1] == quads - 1:
                decode(units[i - 1][0])
        if i < len(units):
            weights = [weigh(x) for x in scores]

    lon = place()[0]
    total_rows = keep_ref.shape[0]
    edge = send_ref.shape[0] - total_rows
    near = pl.ds(pl.multiple_of(lon * (total_rows - edge), edge), edge)
    send_ref[total_rows:, :] = keep_ref[near, :]


def unfiltered(field, high_ref, low_ref, strength):
    high = field.astype(BF16)
    low = (field - high.astype(F32)).astype(BF16)
    smooth = dot(high, high_ref[...]) + (dot(high, low_ref[...]) + dot(low, high_ref[...]))
    return field - strength * smooth


def edge_kernel(state_ref, got_ref, nudge_ref, high_ref, low_ref, edge_ref, whole_ref):
    lon = place()[0]
    channels, own_rows, cols = got_ref.shape
    depth = edge_ref.shape[0] // channels
    own_lanes = pl.ds(pl.multiple_of(lon * cols, 128), cols)
    got_lanes = pl.ds(pl.multiple_of((1 - lon) * cols, 128), cols)
    near = pl.ds(pl.multiple_of(lon * (own_rows - 8), 8), 8)
    for ch in range(0, channels, 8):
        own = jnp.swapaxes(state_ref[ch : ch + 8, near, :], 0, 1)
        got = jnp.swapaxes(got_ref[ch : ch + 8, near, :], 0, 1)
        for i in range(depth):
            rows = slice(i * channels + ch, i * channels + ch + 8)
            whole_ref[rows, own_lanes] = jnp.where(lon == 0, own[i], own[8 - depth + i])
            whole_ref[rows, got_lanes] = jnp.where(lon == 0, got[i], got[8 - depth + i])
    strength = nudge_column(nudge_ref, depth * channels)
    edge_ref[...] = unfiltered(whole_ref[...], high_ref, low_ref, strength).astype(BF16)


def state_kernel(first, state_ref, got_ref, nudge_ref, high_ref, low_ref, out_ref, whole_ref):
    lon = place()[0]
    channels, own_rows, cols = got_ref.shape
    own_lanes = pl.ds(pl.multiple_of(lon * cols, 128), cols)
    got_lanes = pl.ds(pl.multiple_of((1 - lon) * cols, 128), cols)
    for y in range(0, out_ref.shape[0] // channels, 8):
        part = slice(first + y, first + y + 8)
        for ch in range(0, channels, 8):
            own = jnp.swapaxes(state_ref[ch : ch + 8, part, :], 0, 1)
            got = jnp.swapaxes(got_ref[ch : ch + 8, part, :], 0, 1)
            for i in range(8):
                rows = slice((y + i) * channels + ch, (y + i) * channels + ch + 8)
                whole_ref[rows, own_lanes] = own[i]
                whole_ref[rows, got_lanes] = got[i]
    step = PATCH * channels
    strength = nudge_column(nudge_ref, step)
    for at in range(0, out_ref.shape[0], step):
        out_ref[at : at + step, :] = unfiltered(whole_ref[at : at + step, :], high_ref, low_ref, strength)


def filter_rows(dec, first, high_ref, low_ref):
    rows = pl.ds(pl.multiple_of(first, 128), dec.shape[1])
    return dot(dec, high_ref[rows, :]) + dot(dec, low_ref[rows, :])


def early_kernel(upper_ref, lower_ref, piece_ref, nudge_ref, high_ref, low_ref, *refs):
    *refs, out_ref = refs
    keep_refs, send_refs = refs[: len(refs) // 2], refs[len(refs) // 2 :]
    lon = place()[0]
    half = upper_ref.shape[0]
    total = half + lower_ref.shape[0]
    edge = out_ref.shape[0] - total
    far = pl.ds(pl.multiple_of((1 - lon) * (total - edge), edge), edge)
    own = [jnp.concatenate([keep[...], send[far, :]], axis=0) for keep, send in zip(keep_refs, send_refs)]
    decoded = jnp.concatenate(own, axis=1)
    smooth = filter_rows(decoded, lon * (high_ref.shape[0] // 3), high_ref, low_ref)
    step = PATCH * nudge_ref.shape[1]
    strength = nudge_column(nudge_ref, step)
    for at in range(0, total, step):
        base_ref, begin = (upper_ref, at) if at < half else (lower_ref, at - half)
        out_ref[at : at + step, :] = base_ref[begin : begin + step, :] + strength * smooth[at : at + step]
    length, width = out_ref.shape[1], piece_ref.shape[1]
    first = piece_ref.shape[0] - edge * length // width
    for (rows, lanes), (at_rows, at_lanes) in edge_blocks(edge, (length, width)):
        base_edge = piece_ref[first + at_rows.start : first + at_rows.stop, at_lanes].astype(F32)
        term = strength[rows] * smooth[total + rows.start : total + rows.stop, lanes]
        out_ref[total + rows.start : total + rows.stop, lanes] = base_edge + term


def add_kernel(skip, early_ref, got_ref, nudge_ref, high_ref, low_ref, out_ref):
    smooth = filter_rows(got_ref[...], place()[0] * (high_ref.shape[0] // 3) + high_ref.shape[0] // 3 + skip, high_ref, low_ref)
    step = PATCH * nudge_ref.shape[1]
    strength = nudge_column(nudge_ref, step)
    for at in range(0, out_ref.shape[0], step):
        rows = slice(at, min(at + step, out_ref.shape[0]))
        out_ref[rows, :] = early_ref[rows, :] + strength[: rows.stop - at] * smooth[rows]


def last_rows(high_ref, got_ref):
    part = high_ref.shape[0] // 3
    return place()[0] * part + 2 * part - got_ref.shape[1]


def near_kernel(early_ref, got_ref, nudge_ref, high_ref, low_ref, near_ref):
    lon = place()[0]
    edge = near_ref.shape[0]
    total = early_ref.shape[0] - edge
    far = pl.ds(pl.multiple_of((1 - lon) * (total - edge), edge), edge)
    smooth = filter_rows(got_ref[far, :], last_rows(high_ref, got_ref), high_ref, low_ref)
    near_ref[...] = (early_ref[far, :] + nudge_column(nudge_ref, edge) * smooth).astype(BF16)


def row_tile(ref, row, var):
    at = row * (VARS * LEV) + var * LEV
    return pl.ds(at if isinstance(at, int) else pl.multiple_of(at, LEV), LEV)


def tendency_row(south, centre, north, use, only=range(VARS)):
    push_u, push_v = (0.5 * time_step) * centre(0), (0.5 * time_step) * centre(1)
    calm = diffusion * time_step
    to_east, to_west, to_north, to_south = calm - push_u, calm + push_u, calm - push_v, calm + push_v
    for var in only:
        field = centre(var)
        length = field.shape[1]
        step = to_east * pltpu.roll(field, length - 1, axis=1) + to_west * pltpu.roll(field, 1, axis=1)
        step = step + (to_north * north(var) + to_south * south(var))
        use(var, field, step - (4.0 * calm) * field)


def inner_kernel(early_ref, got_ref, nudge_ref, high_ref, low_ref, field_ref, lat_ref, first_ref, last_ref):
    total = field_ref.shape[0]
    edge = lat_ref.shape[0]
    rows = total // (VARS * LEV)
    smooth = filter_rows(got_ref[...], last_rows(high_ref, got_ref), high_ref, low_ref)
    step = PATCH * nudge_ref.shape[1]
    strength = nudge_column(nudge_ref, step)
    for at in range(0, total, step):
        field_ref[at : at + step, :] = early_ref[at : at + step, :] + strength * smooth[at : at + step]
    lat_ref[...] = early_ref[total:, :] + strength[:edge] * smooth[total:]

    def reader(ref, row):
        return lambda var: ref[row_tile(ref, row, var), :]

    def section(ref, row, use):
        tendency_row(reader(ref, row - 1), reader(ref, row), reader(ref, row + 1), use)

    for row in range(1, rows - 1):

        def put_first(var, field, step):
            first_ref[row_tile(first_ref, row, var), :] = field + step

        section(field_ref, row, put_first)
    for row in range(2, rows - 2):

        def put_last(var, field, step):
            nudged = field_ref[row_tile(field_ref, row, var), :]
            last_ref[row_tile(last_ref, row, var), :] = 0.5 * (nudged + field + step)

        section(first_ref, row, put_last)


def outer_kernel(field_ref, first_ref, last_ref, lon_ref, lat_ref, out_hbm, ext_ref, edge_ref, out_ref, sems):
    channels, rows, length = out_ref.shape
    lon, pole = place()
    is_top = lon == 0
    from_lon = lon_ref[...].astype(F32)
    from_lat = jnp.where(pole, 0.0, lat_ref[...])
    edge = from_lon.shape[0]
    ext_ref[:edge, :] = jnp.where(is_top, from_lat, from_lon)
    ext_ref[edge:, :] = jnp.where(is_top, from_lon, from_lat)

    def field(row):
        def read(var):
            if row < 0:
                return ext_ref[row_tile(ext_ref, row + 2, var), :]
            if row >= rows:
                return ext_ref[row_tile(ext_ref, row - rows + 2, var), :]
            return field_ref[row_tile(field_ref, row, var), :]

        return read

    def first(row):
        def read(var):
            if row < 1:
                return edge_ref[row_tile(edge_ref, row + 1, var), :]
            if row >= rows - 1:
                return edge_ref[row_tile(edge_ref, row - rows + 3, var), :]
            return first_ref[row_tile(first_ref, row, var), :]

        return read

    outside = jnp.where(pole, 0.0, 1.0)
    for row in (-1, 0, rows - 1, rows):
        keep = None
        if row < 0:
            keep = jnp.where(is_top, outside, 1.0)
        if row >= rows:
            keep = jnp.where(is_top, 1.0, outside)

        def put(var, value, step):
            total = value + step
            at = row + 1 if row < 1 else row - rows + 3
            edge_ref[row_tile(edge_ref, at, var), :] = total if keep is None else total * keep

        tendency_row(field(row - 1), field(row), field(row + 1), put)
    copies = []
    for var in range(VARS):
        levels = slice(var * LEV, (var + 1) * LEV)
        outer = {}
        for row in (0, 1, rows - 2, rows - 1):

            def put(var, value, step):
                outer[row, var] = 0.5 * (field(row)(var) + value + step)

            tendency_row(first(row - 1), first(row), first(row + 1), put, [var])
        for y in range(0, rows, 8):
            block = []
            for row in range(y, y + 8):
                tile = outer[row, var] if (row, var) in outer else last_ref[row_tile(last_ref, row, var), :]
                block.append(tile[None])
            out_ref[levels, y : y + 8, :] = jnp.swapaxes(jnp.concatenate(block, axis=0), 0, 1)
        part = pl.ds(var * LEV, LEV)
        copies.append(pltpu.make_async_copy(out_ref.at[part], out_hbm.at[part], sems.at[var]))
        copies[-1].start()
    for copy in copies:
        copy.wait()


def work(micros):
    return pl.CostEstimate(flops=int(micros * 1e9), bytes_accessed=int(micros * 1e6), transcendentals=0)


def call(kernel, out_shape, n_in, scratch=(), vmem=24, micros=1.0):
    vmem_spec = pl.BlockSpec(memory_space=pltpu.VMEM)
    many = isinstance(out_shape, (tuple, list))
    return pl.pallas_call(
        kernel,
        out_shape=out_shape,
        in_specs=[vmem_spec] * n_in,
        out_specs=[vmem_spec] * len(out_shape) if many else vmem_spec,
        scratch_shapes=list(scratch),
        cost_estimate=work(micros),
        compiler_params=pltpu.CompilerParams(vmem_limit_bytes=vmem * MIB),
    )


def body(tokens, ln_gain, w_query, w_keyval, w_out, w_dec, nudge, state):
    tok_rows, tok_cols, width = tokens.shape
    channels, state_rows, state_cols = state.shape
    n_lat, n_lon = lax.axis_size("lat"), lax.axis_size("lon")
    lon = lax.axis_index("lon")
    total_cols = tok_cols * n_lon
    length = state_cols * n_lon
    band_rows = state_rows // n_lon
    both = ("lat", "lon")
    tokens_half = tok_cols * HALF
    band = band_rows * channels


    def at(row, col):
        return row * n_lon + col

    last = n_lat - 1
    swap = [(0, 1), (1, 0)]
    shift = [(at(i, 0), at(i + 1, 0)) for i in range(last)] + [(at(last, 0), at(last, 1))]
    shift += [(at(i, 1), at(i - 1, 1)) for i in range(1, n_lat)] + [(at(0, 1), at(0, 0))]
    meet = [(at(i, 1), at(i + 1, 0)) for i in range(last)] + [(at(i + 1, 0), at(i, 1)) for i in range(last)]
    meet_all = meet + [(at(0, 0), at(0, 0)), (at(last, 1), at(last, 1))]

    step = GROUP * WIN
    split = tok_cols - step
    chunks = [(0, split), (split, step)]

    hbm, vmem = pl.BlockSpec(memory_space=pltpu.HBM), pl.BlockSpec(memory_space=pltpu.VMEM)
    in_hbm = functools.partial(pltpu.with_memory_space_constraint, memory_space=pltpu.HBM)
    give, more, give_edge, give_state = pl.pallas_call(
        pack_kernel,
        out_shape=[
            pltpu.VMEM((HALF, split, width), BF16),
            pltpu.VMEM((HALF, step, width), BF16),
            pltpu.VMEM((tok_rows, 2 * WIN, width), BF16),
            pltpu.VMEM((channels, band_rows, state_cols), F32),
        ],
        in_specs=[hbm, hbm],
        out_specs=[vmem] * 4,
        scratch_shapes=[
            pltpu.VMEM((HALF, split + 2 * WIN, width), BF16),
            pltpu.SemaphoreType.DMA((4,)),
        ],
        compiler_params=pltpu.CompilerParams(vmem_limit_bytes=12 * MIB),
    )(in_hbm(tokens), in_hbm(state))
    got_tokens = [lax.ppermute(give, both, shift)]
    edge_tokens = lax.ppermute(give_edge, "lon", swap)
    got_state = lax.ppermute(give_state, "lon", swap)

    gain = ln_gain[None, :]
    nudge_row = nudge[None, :]
    matrix = zonal_filter(length, KEEP)
    high, low = (jnp.asarray(m) for m in split_high_low(matrix))
    order = decoded_order(total_cols, n_lon)
    order = np.concatenate([order[0], order[1], order[0]])
    dec_high, dec_low = (jnp.asarray(m) for m in split_high_low(matrix[order]))

    n_out = w_dec.shape[1]
    qkv_own, w_dec_t, w_mix_t, decoded_own, *weights, own_state, high, low = pl.pallas_call(
        own_kernel,
        out_shape=[
            pltpu.VMEM((tokens_half, 3 * width), BF16),
            pltpu.VMEM((n_out, width), BF16),
            pltpu.VMEM((n_out, width), BF16),
            pltpu.VMEM((n_out, tokens_half), F32),
            pltpu.VMEM(w_query.shape, BF16),
            pltpu.VMEM(w_keyval.shape, BF16),
            pltpu.VMEM((channels, band_rows, state_cols), F32),
            pltpu.VMEM((length, length), BF16),
            pltpu.VMEM((length, length), BF16),
        ],
        in_specs=[hbm, vmem, vmem] + [hbm] * 7,
        out_specs=[vmem] * 9,
        scratch_shapes=[
            pltpu.VMEM((HALF, tok_cols, width), BF16),
            pltpu.VMEM((tokens_half, width), BF16),
            pltpu.VMEM((tokens_half, width), BF16),
            pltpu.VMEM(w_dec.shape, BF16),
            pltpu.VMEM(w_out.shape, BF16),
            pltpu.SemaphoreType.DMA((9,)),
        ],
        cost_estimate=work(7.5),
        compiler_params=pltpu.CompilerParams(vmem_limit_bytes=32 * MIB),
    )(in_hbm(tokens), edge_tokens, gain, in_hbm(w_query), in_hbm(w_keyval), in_hbm(w_out), in_hbm(w_dec), in_hbm(state), in_hbm(high), in_hbm(low))

    edge_rows = 2 * channels
    got_state, qkv_own = lax.optimization_barrier((got_state, qkv_own))
    base_edge = call(
        edge_kernel,
        pltpu.VMEM((edge_rows, length), BF16),
        5,
        [pltpu.VMEM((edge_rows, length), F32)],
    )(own_state, got_state, nudge_row, high, low)
    their_base_edge = lax.ppermute(base_edge, "lon", swap)

    def state_half(first, rows):
        half = pltpu.VMEM((band // 2, length), F32)
        kernel = functools.partial(state_kernel, first)
        return call(kernel, half, 5, [half], micros=1.4)(rows, got_state, nudge_row, high, low)

    own_state, base_edge = lax.optimization_barrier((own_state, base_edge))
    upper = state_half(0, own_state)
    more, upper = lax.optimization_barrier((more, upper))
    last_rows = HALF * step + edge_rows * length // width
    last_piece = call(last_piece_kernel, pltpu.VMEM((last_rows, width), BF16), 3, vmem=12)(
        more, edge_tokens, their_base_edge
    )
    got_tokens.append(lax.ppermute(last_piece, both, shift))
    gain, last_piece = lax.optimization_barrier((gain, last_piece))

    keep, send, got = [], [], []
    for i, (first, cols) in enumerate(chunks):
        kept, sent = call(
            functools.partial(main_kernel, first),
            (pltpu.VMEM((band, cols * PATCH), BF16), pltpu.VMEM((band + edge_rows, cols * PATCH), BF16)),
            8,
            [
                pltpu.VMEM((cols * HALF, width), BF16),
                pltpu.VMEM((cols * HALF, width), BF16),
                pltpu.VMEM((cols * HALF, 3 * width), BF16),
                pltpu.VMEM((cols * WIN, width), BF16),
                pltpu.VMEM((n_out, cols * HALF), F32),
            ],
            micros=3.0 * (cols // step),
        )(got_tokens[i], gain, qkv_own, decoded_own, *weights, w_mix_t, w_dec_t)
        gain, kept, own_state = lax.optimization_barrier((gain, kept, own_state))
        keep.append(kept)
        send.append(sent)
        got.append(lax.ppermute(sent, both, meet_all))

    lower = state_half(band_rows // 2, own_state)
    sums = pltpu.VMEM((band + edge_rows, length), F32)
    early = call(early_kernel, sums, 6 + 2 * len(chunks), micros=1.2)(
        upper, lower, got_tokens[-1], nudge_row, dec_high, dec_low, *keep, *send
    )
    skip = 0
    for part in got[:-1]:
        early = call(functools.partial(add_kernel, skip), sums, 5)(early, part, nudge_row, dec_high, dec_low)
        skip += part.shape[1]
    late = (early, got[-1], nudge_row, dec_high, dec_low)
    to_lon = call(near_kernel, pltpu.VMEM((edge_rows, length), BF16), 5)(*late)
    from_lon = lax.ppermute(to_lon, "lon", swap)

    field = pltpu.VMEM((band, length), F32)
    edge = pltpu.VMEM((edge_rows, length), F32)
    nudged, from_lat, first, last_inner = call(inner_kernel, (field, edge, field, field), 5, micros=2.0)(*late)
    result = (channels, band_rows, length)
    return pl.pallas_call(
        outer_kernel,
        out_shape=jax.ShapeDtypeStruct(result, F32),
        in_specs=[vmem] * 5,
        out_specs=hbm,
        scratch_shapes=[
            pltpu.VMEM((2 * edge_rows, length), F32),
            pltpu.VMEM((2 * edge_rows, length), F32),
            pltpu.VMEM(result, F32),
            pltpu.SemaphoreType.DMA((VARS,)),
        ],
        cost_estimate=work(1.5),
        compiler_params=pltpu.CompilerParams(vmem_limit_bytes=24 * MIB),
    )(nudged, first, last_inner, from_lon, from_lat)


def solution(mesh):
    in_specs = (
        P(("member", "lat"), "lon", None),
        P(),
        P(),
        P(),
        P(),
        P(),
        P(),
        P(None, ("member", "lat"), "lon"),
    )
    out_specs = P(None, ("member", "lat", "lon"), None)
    return jax.shard_map(body, mesh=mesh, in_specs=in_specs, out_specs=out_specs, check_vma=False)
```

```python
import functools
import math

import jax
import jax.numpy as jnp
import ml_dtypes
import numpy as np
from jax import lax
from jax.experimental import pallas as pl
from jax.experimental.pallas import tpu as pltpu
from jax.sharding import PartitionSpec as P

HEADS = 16
WIN = 8
PATCH = 4
VARS = 4
LEV = 8
KEEP = 256

time_step = 0.1
diffusion = 0.5
epsilon = 1e-05
HALF = WIN // 2
GROUP = 4
MIB = 1 << 20
F32 = jnp.float32
BF16 = jnp.bfloat16


def zonal_filter(length, kept_waves):
    lag = np.arange(length, dtype=np.float64)
    waves = np.arange(1, kept_waves, dtype=np.float64)
    kernel = 1.0 + 2.0 * np.cos(2.0 * np.pi / length * lag[:, None] * waves[None, :]).sum(1)
    at = (np.arange(length)[:, None] - np.arange(length)[None, :]) % length
    return (kernel / length)[at]


def split_high_low(matrix):
    high = matrix.astype(ml_dtypes.bfloat16)
    low = (matrix - high.astype(np.float64)).astype(ml_dtypes.bfloat16)
    return high, low


def decoded_order(total_cols, parts):
    cols = total_cols // parts
    group_cols = GROUP * WIN
    rows = []
    for part in range(parts):
        lanes = []
        for group in range(cols // group_cols):
            for b in range(PATCH):
                for place in range(group_cols):
                    col = part * cols + group * group_cols + place
                    if place % WIN < HALF:
                        col += WIN
                    lanes.append((col % total_cols) * PATCH + b)
        rows.append(lanes)
    return np.array(rows)


def place():
    lat, lon = lax.axis_index("lat"), lax.axis_index("lon")
    return lon, ((lat == 0) & (lon == 0)) | ((lat == lax.axis_size("lat") - 1) & (lon == 1))


def nudge_column(nudge_ref, rows):
    channels = nudge_ref.shape[1]
    picked = lax.broadcasted_iota(jnp.int32, (rows, channels), 0) % channels == lax.broadcasted_iota(
        jnp.int32, (rows, channels), 1
    )
    return jnp.sum(jnp.where(picked, nudge_ref[...], 0.0), axis=1, keepdims=True)


def dot(a, b):
    return lax.dot_general(a, b, (((1,), (0,)), ((), ())), preferred_element_type=F32)


def dot_nt(a, b):
    return lax.dot_general(a, b, (((1,), (1,)), ((), ())), preferred_element_type=F32)


def window_columns(here, after):
    lead = lax.broadcasted_iota(jnp.int32, (2 * WIN, 1), 0) % WIN < HALF
    here, after = here.astype(F32), after.astype(F32)
    return jnp.where(lead, jnp.concatenate([here[WIN:], after], axis=0), here)


def normalise(block, gain):
    centred = block - jnp.mean(block, axis=-1, keepdims=True)
    variance = jnp.mean(centred * centred, axis=-1, keepdims=True)
    return centred * lax.rsqrt(variance + epsilon) * gain


def place_tokens(load, cols, gain, raw_ref, normed_ref):
    held = {}

    def emit(pair, r, block):
        group, inside = divmod(pair * 2, GROUP)
        at = (group * HALF + r) * GROUP * WIN + inside * WIN
        raw_ref[at : at + 2 * WIN, :] = block.astype(BF16)
        held[r % 2] = normalise(block, gain)
        if r % 2:
            for side in range(2):
                part = slice(side * WIN, (side + 1) * WIN)
                at = (2 * pair + side) * WIN * HALF + (r - 1) * WIN
                both = jnp.concatenate([held[0][part], held[1][part]], axis=0)
                normed_ref[at : at + 2 * WIN, :] = both.astype(BF16)

    for pair in range(cols // (2 * WIN)):
        for r in range(HALF):
            emit(pair, r, load(pair, r))


def project(normed_ref, wq_ref, wkv_ref, qkv_ref, copies=()):
    width = wq_ref.shape[0]
    normed = normed_ref[...]
    for i in range(3):
        if copies:
            copies[i].wait()
        weights = wq_ref[...] if i == 0 else wkv_ref[:, (i - 1) * width : i * width]
        qkv_ref[:, i * width : (i + 1) * width] = dot(normed, weights).astype(BF16)


def run_copies(sems, pairs):
    copies = [pltpu.make_async_copy(source, target, sems.at[i]) for i, (source, target) in enumerate(pairs)]
    for copy in copies:
        copy.start()
    return copies


def pack_kernel(tok_ref, state_ref, give_ref, more_ref, edge_ref, give_state_ref, whole_ref, sems):
    lon = place()[0]
    rows = give_state_ref.shape[1]
    give_rows = pl.ds(HALF * (1 - lon), HALF)
    more = more_ref.shape[1]
    pairs = [
        (tok_ref.at[give_rows, pl.ds(0, whole_ref.shape[1]), :], whole_ref),
        (tok_ref.at[give_rows, pl.ds(tok_ref.shape[1] - more, more), :], more_ref),
        (tok_ref.at[:, pl.ds(0, edge_ref.shape[1]), :], edge_ref),
        (state_ref.at[:, pl.ds(pl.multiple_of(rows * (1 - lon), 8), rows), :], give_state_ref),
    ]
    copies = run_copies(sems, pairs)
    copies[0].wait()
    for r in range(HALF):
        for at in range(0, give_ref.shape[1], 2 * WIN):
            after = whole_ref[r, at + 2 * WIN : at + 3 * WIN, :]
            columns = window_columns(whole_ref[r, at : at + 2 * WIN, :], after)
            give_ref[r, at : at + 2 * WIN, :] = columns.astype(BF16)
    for copy in copies[1:]:
        copy.wait()


def edge_blocks(rows, width):
    places = []
    for block in range(rows * width[0] // (16 * 128)):
        lane, row = divmod(block, rows // 16)
        to_row, to_lane = divmod(block, width[1] // 128)
        places.append(
            (
                (slice(row * 16, row * 16 + 16), slice(lane * 128, lane * 128 + 128)),
                (slice(to_row * 16, to_row * 16 + 16), slice(to_lane * 128, to_lane * 128 + 128)),
            )
        )
    return places


def last_piece_kernel(more_ref, edge_ref, base_edge_ref, out_ref):
    lon = place()[0]
    cols = more_ref.shape[1]
    for r in range(HALF):
        for at in range(0, cols, 2 * WIN):
            if at + 2 * WIN < cols:
                after = more_ref[r, at + 2 * WIN : at + 3 * WIN, :]
            else:
                after = edge_ref[HALF * (1 - lon) + r, :WIN, :]
            columns = window_columns(more_ref[r, at : at + 2 * WIN, :], after)
            out_ref[r * cols + at : r * cols + at + 2 * WIN, :] = columns.astype(BF16)
    widths = (base_edge_ref.shape[1], out_ref.shape[1])
    for (rows, lanes), (to_rows, to_lanes) in edge_blocks(base_edge_ref.shape[0], widths):
        at = slice(HALF * cols + to_rows.start, HALF * cols + to_rows.stop)
        out_ref[at, to_lanes] = base_edge_ref[rows, lanes]


def own_kernel(
    tok_hbm,
    edge_ref,
    gain_ref,
    wq_hbm,
    wkv_hbm,
    wout_hbm,
    wdec_hbm,
    state_hbm,
    high_hbm,
    low_hbm,
    qkv_ref,
    wdec_t_ref,
    wmix_t_ref,
    decoded_ref,
    wq_ref,
    wkv_ref,
    state_ref,
    high_ref,
    low_ref,
    tok_ref,
    raw_ref,
    normed_ref,
    wdec_ref,
    wout_ref,
    sems,
):
    lon = place()[0]
    cols = tok_ref.shape[1]
    width = wq_ref.shape[0]
    keys, values = pl.ds(0, width), pl.ds(width, width)
    own_rows = pl.ds(HALF * lon, HALF)
    state_rows = pl.ds(pl.multiple_of(state_ref.shape[1] * lon, 8), state_ref.shape[1])
    copies = run_copies(
        sems,
        [
            (tok_hbm.at[own_rows], tok_ref),
            (wq_hbm, wq_ref),
            (wkv_hbm.at[:, keys], wkv_ref.at[:, keys]),
            (wkv_hbm.at[:, values], wkv_ref.at[:, values]),
            (wdec_hbm, wdec_ref),
            (wout_hbm, wout_ref),
            (state_hbm.at[:, state_rows, :], state_ref),
            (high_hbm, high_ref),
            (low_hbm, low_ref),
        ],
    )

    def load(pair, r):
        at = pair * 2 * WIN
        if at + 2 * WIN < cols:
            after = tok_ref[r, at + 2 * WIN : at + 3 * WIN, :]
        else:
            after = edge_ref[HALF * lon + r, :WIN, :]
        return window_columns(tok_ref[r, at : at + 2 * WIN, :], after)

    copies[0].wait()
    place_tokens(load, cols, gain_ref[...], raw_ref, normed_ref)
    project(normed_ref, wq_ref, wkv_ref, qkv_ref, copies[1:4])
    outs = wdec_ref.shape[1]
    band = outs // PATCH
    channels = band // PATCH
    row = lax.broadcasted_iota(jnp.int32, (outs, 1), 0)
    source = (row % channels) * PATCH * PATCH + (row % band // channels) * PATCH + row // band
    pick = (lax.broadcasted_iota(jnp.int32, (outs, outs), 1) == source).astype(F32).astype(BF16)
    copies[4].wait()
    wdec_t_ref[...] = dot_nt(pick, wdec_ref[...]).astype(BF16)
    decoded_ref[...] = dot_nt(wdec_t_ref[...], raw_ref[...])
    copies[5].wait()
    wmix_t_ref[...] = dot_nt(wdec_t_ref[...], wout_ref[...]).astype(BF16)
    for copy in copies[6:]:
        copy.wait()


def main_kernel(first, x_ref, *refs):
    gain_ref, qkv_own_ref, decoded_own_ref, wq_ref, wkv_ref, wmix_ref, wdec_ref, *refs = refs
    keep_ref, send_ref, raw_ref, normed_ref, qkv_ref, att_ref, decoded_ref = refs
    width = raw_ref.shape[1]
    head_size = width // HEADS
    half_cells = HALF * WIN
    cells = 2 * half_cells
    lanes = 4 * head_size
    quads = HEADS // 4
    cols = raw_ref.shape[0] // HALF
    base = first * HALF
    group_cols = GROUP * WIN
    group_half = GROUP * half_cells

    def load(pair, r):
        at = pair * 2 * WIN
        if len(x_ref.shape) == 2:
            return x_ref[r * cols + at : r * cols + at + 2 * WIN, :].astype(F32)
        return x_ref[r, at : at + 2 * WIN, :].astype(F32)

    def iota(shape, dim):
        return lax.broadcasted_iota(jnp.int32, shape, dim)

    blocks = (iota((lanes, lanes), 0) // head_size == iota((lanes, lanes), 1) // head_size).astype(F32).astype(BF16)
    split_rows = iota((cells, 2 * cells), 0) // half_cells != iota((cells, 2 * cells), 1) % cells // half_cells
    bias = jnp.where(split_rows & place()[1], -1e30, 0.0)
    first_head = iota((cells, 2 * cells), 1) < cells
    scale = 1.0 / (math.sqrt(head_size) * math.log(2.0))

    def project_quad(quad):
        normed = normed_ref[...]
        at = quad * lanes
        for offset, weights in (
            (0, wq_ref[:, at : at + lanes]),
            (width, wkv_ref[:, at : at + lanes]),
            (2 * width, wkv_ref[:, width + at : width + at + lanes]),
        ):
            qkv_ref[:, offset + at : offset + at + lanes] = dot(normed, weights).astype(BF16)

    def part(window, quad, offset):
        columns = slice(offset + quad * lanes, offset + (quad + 1) * lanes)
        got = slice(window * half_cells, (window + 1) * half_cells)
        own = slice(base + got.start, base + got.stop)
        return jnp.concatenate([qkv_own_ref[own, columns], qkv_ref[got, columns]], axis=0)

    def score(window, quad):
        keys = jnp.concatenate([part(window, quad, width)] * 4, axis=0) * blocks
        return dot_nt(part(window, quad, 0), keys)

    def weigh(scores):
        outs = []
        for side in range(2):
            two = scores[:, side * 2 * cells : (side + 1) * 2 * cells] + bias
            left = jnp.max(jnp.where(first_head, two, -jnp.inf), axis=-1, keepdims=True)
            right = jnp.max(jnp.where(first_head, -jnp.inf, two), axis=-1, keepdims=True)
            peak = jnp.where(first_head, left, right)
            outs.append(jnp.exp2((two - peak) * scale).astype(BF16))
        return jnp.concatenate(outs, axis=1)

    def mix(group, quad, weights):
        sums = dot(jnp.concatenate(weights, axis=0), blocks)
        mixed = []
        for i in range(GROUP):
            values = jnp.concatenate([part(group * GROUP + i, quad, 2 * width)] * 4, axis=0) * blocks
            mixed.append(dot(weights[i], values) / sums[i * cells : (i + 1) * cells])
        tiles = [mixed[i][at : at + WIN] for at in range(0, cells, WIN) for i in range(GROUP)]
        rows = slice(group * 2 * group_half, (group + 1) * 2 * group_half)
        att_ref[rows, quad * lanes : (quad + 1) * lanes] = jnp.concatenate(tiles, axis=0).astype(BF16)

    def decode(group):
        rows = slice(group * 2 * group_half, (group + 1) * 2 * group_half)
        decoded = dot_nt(wmix_ref[...], att_ref[rows, :])
        got = slice(group * group_half, (group + 1) * group_half)
        own = slice(base + got.start, base + got.stop)
        band = decoded.shape[0] // PATCH
        out_lanes = slice(group * group_cols * PATCH, (group + 1) * group_cols * PATCH)
        lane_part = iota((band, group_half), 1) // group_cols
        for half, more, out_ref in ((0, decoded_own_ref[:, own], keep_ref), (1, decoded_ref[:, got], send_ref)):
            total = decoded[:, half * group_half : (half + 1) * group_half] + more
            from_b = [total[b * band : (b + 1) * band] for b in range(PATCH)]
            for r in range(HALF):
                placed = None
                for b in range(PATCH):
                    moved = from_b[b]
                    if b != r:
                        moved = pltpu.roll(moved, (b - r) % PATCH * group_cols, axis=1)
                    placed = moved if placed is None else jnp.where(lane_part == b, moved, placed)
                out_ref[r * band : (r + 1) * band, out_lanes] = placed.astype(BF16)

    place_tokens(load, cols, gain_ref[...], raw_ref, normed_ref)
    project_quad(0)
    units = [(group, quad) for group in range(cols // group_cols) for quad in range(quads)]
    weights = None
    for i in range(len(units) + 1):
        held = weights
        if i < len(units):
            group, quad = units[i]
            weights = []
            for w in range(GROUP):
                scores = score(group * GROUP + w, quad)
                if w == 1 and group == 0 and quad + 1 < quads:
                    project_quad(quad + 1)
                weights.append(weigh(scores))
            if i == 0:
                decoded_ref[...] = dot_nt(wdec_ref[...], raw_ref[...])
        if i > 0:
            mix(*units[i - 1], held)
            if units[i - 1][1] == quads - 1:
                decode(units[i - 1][0])

    lon = place()[0]
    total_rows = keep_ref.shape[0]
    edge = send_ref.shape[0] - total_rows
    near = pl.ds(pl.multiple_of(lon * (total_rows - edge), edge), edge)
    send_ref[total_rows:, :] = keep_ref[near, :]


def unfiltered(field, high_ref, low_ref, strength):
    high = field.astype(BF16)
    low = (field - high.astype(F32)).astype(BF16)
    smooth = dot(high, high_ref[...]) + (dot(high, low_ref[...]) + dot(low, high_ref[...]))
    return field - strength * smooth


def edge_kernel(state_ref, got_ref, nudge_ref, high_ref, low_ref, edge_ref, whole_ref):
    lon = place()[0]
    channels, own_rows, cols = got_ref.shape
    depth = edge_ref.shape[0] // channels
    own_lanes = pl.ds(pl.multiple_of(lon * cols, 128), cols)
    got_lanes = pl.ds(pl.multiple_of((1 - lon) * cols, 128), cols)
    near = pl.ds(pl.multiple_of(lon * (own_rows - 8), 8), 8)
    for ch in range(0, channels, 8):
        own = jnp.swapaxes(state_ref[ch : ch + 8, near, :], 0, 1)
        got = jnp.swapaxes(got_ref[ch : ch + 8, near, :], 0, 1)
        for i in range(depth):
            rows = slice(i * channels + ch, i * channels + ch + 8)
            whole_ref[rows, own_lanes] = jnp.where(lon == 0, own[i], own[8 - depth + i])
            whole_ref[rows, got_lanes] = jnp.where(lon == 0, got[i], got[8 - depth + i])
    strength = nudge_column(nudge_ref, depth * channels)
    edge_ref[...] = unfiltered(whole_ref[...], high_ref, low_ref, strength).astype(BF16)


def state_kernel(first, state_ref, got_ref, nudge_ref, high_ref, low_ref, out_ref, whole_ref):
    lon = place()[0]
    channels, own_rows, cols = got_ref.shape
    own_lanes = pl.ds(pl.multiple_of(lon * cols, 128), cols)
    got_lanes = pl.ds(pl.multiple_of((1 - lon) * cols, 128), cols)
    for y in range(0, out_ref.shape[0] // channels, 8):
        part = slice(first + y, first + y + 8)
        for ch in range(0, channels, 8):
            own = jnp.swapaxes(state_ref[ch : ch + 8, part, :], 0, 1)
            got = jnp.swapaxes(got_ref[ch : ch + 8, part, :], 0, 1)
            for i in range(8):
                rows = slice((y + i) * channels + ch, (y + i) * channels + ch + 8)
                whole_ref[rows, own_lanes] = own[i]
                whole_ref[rows, got_lanes] = got[i]
    step = PATCH * channels
    strength = nudge_column(nudge_ref, step)
    for at in range(0, out_ref.shape[0], step):
        out_ref[at : at + step, :] = unfiltered(whole_ref[at : at + step, :], high_ref, low_ref, strength)


def filter_rows(dec, first, high_ref, low_ref):
    rows = pl.ds(pl.multiple_of(first, 128), dec.shape[1])
    return dot(dec, high_ref[rows, :]) + dot(dec, low_ref[rows, :])


def early_kernel(upper_ref, lower_ref, piece_ref, nudge_ref, high_ref, low_ref, *refs):
    *refs, out_ref = refs
    keep_refs, send_refs = refs[: len(refs) // 2], refs[len(refs) // 2 :]
    lon = place()[0]
    half = upper_ref.shape[0]
    total = half + lower_ref.shape[0]
    edge = out_ref.shape[0] - total
    far = pl.ds(pl.multiple_of((1 - lon) * (total - edge), edge), edge)
    own = [jnp.concatenate([keep[...], send[far, :]], axis=0) for keep, send in zip(keep_refs, send_refs)]
    decoded = jnp.concatenate(own, axis=1)
    smooth = filter_rows(decoded, lon * (high_ref.shape[0] // 3), high_ref, low_ref)
    step = PATCH * nudge_ref.shape[1]
    strength = nudge_column(nudge_ref, step)
    for at in range(0, total, step):
        base_ref, begin = (upper_ref, at) if at < half else (lower_ref, at - half)
        out_ref[at : at + step, :] = base_ref[begin : begin + step, :] + strength * smooth[at : at + step]
    length, width = out_ref.shape[1], piece_ref.shape[1]
    first = piece_ref.shape[0] - edge * length // width
    for (rows, lanes), (at_rows, at_lanes) in edge_blocks(edge, (length, width)):
        base_edge = piece_ref[first + at_rows.start : first + at_rows.stop, at_lanes].astype(F32)
        term = strength[rows] * smooth[total + rows.start : total + rows.stop, lanes]
        out_ref[total + rows.start : total + rows.stop, lanes] = base_edge + term


def add_kernel(skip, early_ref, got_ref, nudge_ref, high_ref, low_ref, out_ref):
    smooth = filter_rows(got_ref[...], place()[0] * (high_ref.shape[0] // 3) + high_ref.shape[0] // 3 + skip, high_ref, low_ref)
    step = PATCH * nudge_ref.shape[1]
    strength = nudge_column(nudge_ref, step)
    for at in range(0, out_ref.shape[0], step):
        rows = slice(at, min(at + step, out_ref.shape[0]))
        out_ref[rows, :] = early_ref[rows, :] + strength[: rows.stop - at] * smooth[rows]


def last_rows(high_ref, got_ref):
    part = high_ref.shape[0] // 3
    return place()[0] * part + 2 * part - got_ref.shape[1]


def near_kernel(early_ref, got_ref, nudge_ref, high_ref, low_ref, near_ref):
    lon = place()[0]
    edge = near_ref.shape[0]
    total = early_ref.shape[0] - edge
    far = pl.ds(pl.multiple_of((1 - lon) * (total - edge), edge), edge)
    smooth = filter_rows(got_ref[far, :], last_rows(high_ref, got_ref), high_ref, low_ref)
    near_ref[...] = (early_ref[far, :] + nudge_column(nudge_ref, edge) * smooth).astype(BF16)


def row_tile(ref, row, var):
    at = row * (VARS * LEV) + var * LEV
    return pl.ds(at if isinstance(at, int) else pl.multiple_of(at, LEV), LEV)


def tendency_row(south, centre, north, use, only=range(VARS)):
    push_u, push_v = (0.5 * time_step) * centre(0), (0.5 * time_step) * centre(1)
    calm = diffusion * time_step
    to_east, to_west, to_north, to_south = calm - push_u, calm + push_u, calm - push_v, calm + push_v
    for var in only:
        field = centre(var)
        length = field.shape[1]
        step = to_east * pltpu.roll(field, length - 1, axis=1) + to_west * pltpu.roll(field, 1, axis=1)
        step = step + (to_north * north(var) + to_south * south(var))
        use(var, field, step - (4.0 * calm) * field)


def inner_kernel(early_ref, got_ref, nudge_ref, high_ref, low_ref, field_ref, lat_ref, first_ref, last_ref):
    total = field_ref.shape[0]
    edge = lat_ref.shape[0]
    rows = total // (VARS * LEV)
    step = PATCH * nudge_ref.shape[1]
    strength = nudge_column(nudge_ref, step)
    first_lane = last_rows(high_ref, got_ref)

    def smooth_rows(at, size):
        return filter_rows(got_ref[at : at + size, :], first_lane, high_ref, low_ref)

    def reader(ref, row):
        return lambda var: ref[row_tile(ref, row, var), :]

    def section(ref, row, use):
        tendency_row(reader(ref, row - 1), reader(ref, row), reader(ref, row + 1), use)

    def first_row(row):
        def put(var, field, step):
            first_ref[row_tile(first_ref, row, var), :] = field + step

        section(field_ref, row, put)

    def last_row(row):
        def put(var, field, step):
            nudged = field_ref[row_tile(field_ref, row, var), :]
            last_ref[row_tile(last_ref, row, var), :] = 0.5 * (nudged + field + step)

        section(first_ref, row, put)

    smooth = smooth_rows(0, step)
    next_first, next_last = 1, 2
    for at in range(0, total, step):
        field_ref[at : at + step, :] = early_ref[at : at + step, :] + strength * smooth
        if at + step < total:
            smooth = smooth_rows(at + step, step)
        else:
            smooth = smooth_rows(total, edge)
        ready = (at + step) // (VARS * LEV)
        while next_first <= min(rows - 2, ready - 2):
            first_row(next_first)
            next_first += 1
        while next_last <= min(rows - 3, next_first - 2):
            last_row(next_last)
            next_last += 1
    lat_ref[...] = early_ref[total:, :] + strength[:edge] * smooth


def outer_kernel(field_ref, first_ref, last_ref, lon_ref, lat_ref, out_hbm, ext_ref, edge_ref, out_ref, sems):
    channels, rows, length = out_ref.shape
    lon, pole = place()
    is_top = lon == 0
    from_lon = lon_ref[...].astype(F32)
    from_lat = jnp.where(pole, 0.0, lat_ref[...])
    edge = from_lon.shape[0]
    ext_ref[:edge, :] = jnp.where(is_top, from_lat, from_lon)
    ext_ref[edge:, :] = jnp.where(is_top, from_lon, from_lat)

    def field(row):
        def read(var):
            if row < 0:
                return ext_ref[row_tile(ext_ref, row + 2, var), :]
            if row >= rows:
                return ext_ref[row_tile(ext_ref, row - rows + 2, var), :]
            return field_ref[row_tile(field_ref, row, var), :]

        return read

    def first(row):
        def read(var):
            if row < 1:
                return edge_ref[row_tile(edge_ref, row + 1, var), :]
            if row >= rows - 1:
                return edge_ref[row_tile(edge_ref, row - rows + 3, var), :]
            return first_ref[row_tile(first_ref, row, var), :]

        return read

    outside = jnp.where(pole, 0.0, 1.0)
    for row in (-1, 0, rows - 1, rows):
        keep = None
        if row < 0:
            keep = jnp.where(is_top, outside, 1.0)
        if row >= rows:
            keep = jnp.where(is_top, 1.0, outside)

        def put(var, value, step):
            total = value + step
            at = row + 1 if row < 1 else row - rows + 3
            edge_ref[row_tile(edge_ref, at, var), :] = total if keep is None else total * keep

        tendency_row(field(row - 1), field(row), field(row + 1), put)
    copies = []
    for var in range(VARS):
        levels = slice(var * LEV, (var + 1) * LEV)
        outer = {}
        for row in (0, 1, rows - 2, rows - 1):

            def put(var, value, step):
                outer[row, var] = 0.5 * (field(row)(var) + value + step)

            tendency_row(first(row - 1), first(row), first(row + 1), put, [var])
        for y in range(0, rows, 8):
            block = []
            for row in range(y, y + 8):
                tile = outer[row, var] if (row, var) in outer else last_ref[row_tile(last_ref, row, var), :]
                block.append(tile[None])
            out_ref[levels, y : y + 8, :] = jnp.swapaxes(jnp.concatenate(block, axis=0), 0, 1)
        part = pl.ds(var * LEV, LEV)
        copies.append(pltpu.make_async_copy(out_ref.at[part], out_hbm.at[part], sems.at[var]))
        copies[-1].start()
    for copy in copies:
        copy.wait()


def work(micros):
    return pl.CostEstimate(flops=int(micros * 1e9), bytes_accessed=int(micros * 1e6), transcendentals=0)


def call(kernel, out_shape, n_in, scratch=(), vmem=24, micros=1.0):
    vmem_spec = pl.BlockSpec(memory_space=pltpu.VMEM)
    many = isinstance(out_shape, (tuple, list))
    return pl.pallas_call(
        kernel,
        out_shape=out_shape,
        in_specs=[vmem_spec] * n_in,
        out_specs=[vmem_spec] * len(out_shape) if many else vmem_spec,
        scratch_shapes=list(scratch),
        cost_estimate=work(micros),
        compiler_params=pltpu.CompilerParams(vmem_limit_bytes=vmem * MIB),
    )


def body(tokens, ln_gain, w_query, w_keyval, w_out, w_dec, nudge, state):
    tok_rows, tok_cols, width = tokens.shape
    channels, state_rows, state_cols = state.shape
    n_lat, n_lon = lax.axis_size("lat"), lax.axis_size("lon")
    lon = lax.axis_index("lon")
    total_cols = tok_cols * n_lon
    length = state_cols * n_lon
    band_rows = state_rows // n_lon
    both = ("lat", "lon")
    tokens_half = tok_cols * HALF
    band = band_rows * channels


    def at(row, col):
        return row * n_lon + col

    last = n_lat - 1
    swap = [(0, 1), (1, 0)]
    shift = [(at(i, 0), at(i + 1, 0)) for i in range(last)] + [(at(last, 0), at(last, 1))]
    shift += [(at(i, 1), at(i - 1, 1)) for i in range(1, n_lat)] + [(at(0, 1), at(0, 0))]
    meet = [(at(i, 1), at(i + 1, 0)) for i in range(last)] + [(at(i + 1, 0), at(i, 1)) for i in range(last)]
    meet_all = meet + [(at(0, 0), at(0, 0)), (at(last, 1), at(last, 1))]

    step = GROUP * WIN
    split = tok_cols - step
    chunks = [(0, split), (split, step)]

    hbm, vmem = pl.BlockSpec(memory_space=pltpu.HBM), pl.BlockSpec(memory_space=pltpu.VMEM)
    in_hbm = functools.partial(pltpu.with_memory_space_constraint, memory_space=pltpu.HBM)
    give, more, give_edge, give_state = pl.pallas_call(
        pack_kernel,
        out_shape=[
            pltpu.VMEM((HALF, split, width), BF16),
            pltpu.VMEM((HALF, step, width), BF16),
            pltpu.VMEM((tok_rows, 2 * WIN, width), BF16),
            pltpu.VMEM((channels, band_rows, state_cols), F32),
        ],
        in_specs=[hbm, hbm],
        out_specs=[vmem] * 4,
        scratch_shapes=[
            pltpu.VMEM((HALF, split + 2 * WIN, width), BF16),
            pltpu.SemaphoreType.DMA((4,)),
        ],
        compiler_params=pltpu.CompilerParams(vmem_limit_bytes=12 * MIB),
    )(in_hbm(tokens), in_hbm(state))
    got_tokens = [lax.ppermute(give, both, shift)]
    edge_tokens = lax.ppermute(give_edge, "lon", swap)
    got_state = lax.ppermute(give_state, "lon", swap)

    gain = ln_gain[None, :]
    nudge_row = nudge[None, :]
    matrix = zonal_filter(length, KEEP)
    high, low = (jnp.asarray(m) for m in split_high_low(matrix))
    order = decoded_order(total_cols, n_lon)
    order = np.concatenate([order[0], order[1], order[0]])
    dec_high, dec_low = (jnp.asarray(m) for m in split_high_low(matrix[order]))

    n_out = w_dec.shape[1]
    qkv_own, w_dec_t, w_mix_t, decoded_own, *weights, own_state, high, low = pl.pallas_call(
        own_kernel,
        out_shape=[
            pltpu.VMEM((tokens_half, 3 * width), BF16),
            pltpu.VMEM((n_out, width), BF16),
            pltpu.VMEM((n_out, width), BF16),
            pltpu.VMEM((n_out, tokens_half), F32),
            pltpu.VMEM(w_query.shape, BF16),
            pltpu.VMEM(w_keyval.shape, BF16),
            pltpu.VMEM((channels, band_rows, state_cols), F32),
            pltpu.VMEM((length, length), BF16),
            pltpu.VMEM((length, length), BF16),
        ],
        in_specs=[hbm, vmem, vmem] + [hbm] * 7,
        out_specs=[vmem] * 9,
        scratch_shapes=[
            pltpu.VMEM((HALF, tok_cols, width), BF16),
            pltpu.VMEM((tokens_half, width), BF16),
            pltpu.VMEM((tokens_half, width), BF16),
            pltpu.VMEM(w_dec.shape, BF16),
            pltpu.VMEM(w_out.shape, BF16),
            pltpu.SemaphoreType.DMA((9,)),
        ],
        cost_estimate=work(7.5),
        compiler_params=pltpu.CompilerParams(vmem_limit_bytes=32 * MIB),
    )(in_hbm(tokens), edge_tokens, gain, in_hbm(w_query), in_hbm(w_keyval), in_hbm(w_out), in_hbm(w_dec), in_hbm(state), in_hbm(high), in_hbm(low))

    edge_rows = 2 * channels
    got_state, qkv_own = lax.optimization_barrier((got_state, qkv_own))
    base_edge = call(
        edge_kernel,
        pltpu.VMEM((edge_rows, length), BF16),
        5,
        [pltpu.VMEM((edge_rows, length), F32)],
    )(own_state, got_state, nudge_row, high, low)
    their_base_edge = lax.ppermute(base_edge, "lon", swap)

    def state_half(first, rows):
        half = pltpu.VMEM((band // 2, length), F32)
        kernel = functools.partial(state_kernel, first)
        return call(kernel, half, 5, [half], micros=1.4)(rows, got_state, nudge_row, high, low)

    own_state, base_edge = lax.optimization_barrier((own_state, base_edge))
    upper = state_half(0, own_state)
    more, upper = lax.optimization_barrier((more, upper))
    last_rows = HALF * step + edge_rows * length // width
    last_piece = call(last_piece_kernel, pltpu.VMEM((last_rows, width), BF16), 3, vmem=12)(
        more, edge_tokens, their_base_edge
    )
    got_tokens.append(lax.ppermute(last_piece, both, shift))
    gain, last_piece = lax.optimization_barrier((gain, last_piece))

    keep, send, got = [], [], []
    for i, (first, cols) in enumerate(chunks):
        kept, sent = call(
            functools.partial(main_kernel, first),
            (pltpu.VMEM((band, cols * PATCH), BF16), pltpu.VMEM((band + edge_rows, cols * PATCH), BF16)),
            8,
            [
                pltpu.VMEM((cols * HALF, width), BF16),
                pltpu.VMEM((cols * HALF, width), BF16),
                pltpu.VMEM((cols * HALF, 3 * width), BF16),
                pltpu.VMEM((cols * WIN, width), BF16),
                pltpu.VMEM((n_out, cols * HALF), F32),
            ],
            micros=3.0 * (cols // step),
        )(got_tokens[i], gain, qkv_own, decoded_own, *weights, w_mix_t, w_dec_t)
        gain, kept, own_state = lax.optimization_barrier((gain, kept, own_state))
        keep.append(kept)
        send.append(sent)
        got.append(lax.ppermute(sent, both, meet_all))

    lower = state_half(band_rows // 2, own_state)
    sums = pltpu.VMEM((band + edge_rows, length), F32)
    early = call(early_kernel, sums, 6 + 2 * len(chunks), micros=1.2)(
        upper, lower, got_tokens[-1], nudge_row, dec_high, dec_low, *keep, *send
    )
    skip = 0
    for part in got[:-1]:
        early = call(functools.partial(add_kernel, skip), sums, 5)(early, part, nudge_row, dec_high, dec_low)
        skip += part.shape[1]
    late = (early, got[-1], nudge_row, dec_high, dec_low)
    to_lon = call(near_kernel, pltpu.VMEM((edge_rows, length), BF16), 5)(*late)
    from_lon = lax.ppermute(to_lon, "lon", swap)

    field = pltpu.VMEM((band, length), F32)
    edge = pltpu.VMEM((edge_rows, length), F32)
    nudged, from_lat, first, last_inner = call(inner_kernel, (field, edge, field, field), 5, micros=2.0)(*late)
    result = (channels, band_rows, length)
    return pl.pallas_call(
        outer_kernel,
        out_shape=jax.ShapeDtypeStruct(result, F32),
        in_specs=[vmem] * 5,
        out_specs=hbm,
        scratch_shapes=[
            pltpu.VMEM((2 * edge_rows, length), F32),
            pltpu.VMEM((2 * edge_rows, length), F32),
            pltpu.VMEM(result, F32),
            pltpu.SemaphoreType.DMA((VARS,)),
        ],
        cost_estimate=work(1.5),
        compiler_params=pltpu.CompilerParams(vmem_limit_bytes=24 * MIB),
    )(nudged, first, last_inner, from_lon, from_lat)


def solution(mesh):
    in_specs = (
        P(("member", "lat"), "lon", None),
        P(),
        P(),
        P(),
        P(),
        P(),
        P(),
        P(None, ("member", "lat"), "lon"),
    )
    out_specs = P(None, ("member", "lat", "lon"), None)
    return jax.shard_map(body, mesh=mesh, in_specs=in_specs, out_specs=out_specs, check_vma=False)
```

```python
import functools
import math

import jax
import jax.numpy as jnp
import ml_dtypes
import numpy as np
from jax import lax
from jax.experimental import pallas as pl
from jax.experimental.pallas import tpu as pltpu
from jax.sharding import PartitionSpec as P

HEADS = 16
WIN = 8
PATCH = 4
VARS = 4
LEV = 8
KEEP = 256

time_step = 0.1
diffusion = 0.5
epsilon = 1e-05
HALF = WIN // 2
GROUP = 4
MIB = 1 << 20
F32 = jnp.float32
BF16 = jnp.bfloat16


def zonal_filter(length, kept_waves):
    lag = np.arange(length, dtype=np.float64)
    waves = np.arange(1, kept_waves, dtype=np.float64)
    kernel = 1.0 + 2.0 * np.cos(2.0 * np.pi / length * lag[:, None] * waves[None, :]).sum(1)
    at = (np.arange(length)[:, None] - np.arange(length)[None, :]) % length
    return (kernel / length)[at]


def split_high_low(matrix):
    high = matrix.astype(ml_dtypes.bfloat16)
    low = (matrix - high.astype(np.float64)).astype(ml_dtypes.bfloat16)
    return high, low


def decoded_order(total_cols, parts):
    cols = total_cols // parts
    group_cols = GROUP * WIN
    rows = []
    for part in range(parts):
        lanes = []
        for group in range(cols // group_cols):
            for b in range(PATCH):
                for place in range(group_cols):
                    col = part * cols + group * group_cols + place
                    if place % WIN < HALF:
                        col += WIN
                    lanes.append((col % total_cols) * PATCH + b)
        rows.append(lanes)
    return np.array(rows)


def place():
    lat, lon = lax.axis_index("lat"), lax.axis_index("lon")
    return lon, ((lat == 0) & (lon == 0)) | ((lat == lax.axis_size("lat") - 1) & (lon == 1))


def nudge_column(nudge_ref, rows):
    channels = nudge_ref.shape[1]
    picked = lax.broadcasted_iota(jnp.int32, (rows, channels), 0) % channels == lax.broadcasted_iota(
        jnp.int32, (rows, channels), 1
    )
    return jnp.sum(jnp.where(picked, nudge_ref[...], 0.0), axis=1, keepdims=True)


def dot(a, b):
    return lax.dot_general(a, b, (((1,), (0,)), ((), ())), preferred_element_type=F32)


def dot_nt(a, b):
    return lax.dot_general(a, b, (((1,), (1,)), ((), ())), preferred_element_type=F32)


def window_columns(here, after):
    lead = lax.broadcasted_iota(jnp.int32, (2 * WIN, 1), 0) % WIN < HALF
    here, after = here.astype(F32), after.astype(F32)
    return jnp.where(lead, jnp.concatenate([here[WIN:], after], axis=0), here)


def normalise(block, gain):
    centred = block - jnp.mean(block, axis=-1, keepdims=True)
    variance = jnp.mean(centred * centred, axis=-1, keepdims=True)
    return centred * lax.rsqrt(variance + epsilon) * gain


def place_tokens(load, cols, gain, raw_ref, normed_ref):
    held = {}

    def emit(pair, r, block):
        group, inside = divmod(pair * 2, GROUP)
        at = (group * HALF + r) * GROUP * WIN + inside * WIN
        raw_ref[at : at + 2 * WIN, :] = block.astype(BF16)
        held[r % 2] = normalise(block, gain)
        if r % 2:
            for side in range(2):
                part = slice(side * WIN, (side + 1) * WIN)
                at = (2 * pair + side) * WIN * HALF + (r - 1) * WIN
                both = jnp.concatenate([held[0][part], held[1][part]], axis=0)
                normed_ref[at : at + 2 * WIN, :] = both.astype(BF16)

    for pair in range(cols // (2 * WIN)):
        for r in range(HALF):
            emit(pair, r, load(pair, r))


def project(normed_ref, wq_ref, wkv_ref, qkv_ref, copies=()):
    width = wq_ref.shape[0]
    normed = normed_ref[...]
    for i in range(3):
        if copies:
            copies[i].wait()
        weights = wq_ref[...] if i == 0 else wkv_ref[:, (i - 1) * width : i * width]
        qkv_ref[:, i * width : (i + 1) * width] = dot(normed, weights).astype(BF16)


def run_copies(sems, pairs):
    copies = [pltpu.make_async_copy(source, target, sems.at[i]) for i, (source, target) in enumerate(pairs)]
    for copy in copies:
        copy.start()
    return copies


def pack_kernel(tok_ref, state_ref, give_ref, edge_ref, give_state_ref, whole_ref, sems):
    lon = place()[0]
    rows = give_state_ref.shape[1]
    give_rows = pl.ds(HALF * (1 - lon), HALF)
    pairs = [
        (tok_ref.at[give_rows, pl.ds(0, whole_ref.shape[1]), :], whole_ref),
        (tok_ref.at[:, pl.ds(0, edge_ref.shape[1]), :], edge_ref),
        (state_ref.at[:, pl.ds(pl.multiple_of(rows * (1 - lon), 8), rows), :], give_state_ref),
    ]
    copies = run_copies(sems, pairs)
    copies[0].wait()
    for r in range(HALF):
        for at in range(0, give_ref.shape[1], 2 * WIN):
            after = whole_ref[r, at + 2 * WIN : at + 3 * WIN, :]
            columns = window_columns(whole_ref[r, at : at + 2 * WIN, :], after)
            give_ref[r, at : at + 2 * WIN, :] = columns.astype(BF16)
    for copy in copies[1:]:
        copy.wait()


def edge_blocks(rows, width):
    places = []
    for block in range(rows * width[0] // (16 * 128)):
        lane, row = divmod(block, rows // 16)
        to_row, to_lane = divmod(block, width[1] // 128)
        places.append(
            (
                (slice(row * 16, row * 16 + 16), slice(lane * 128, lane * 128 + 128)),
                (slice(to_row * 16, to_row * 16 + 16), slice(to_lane * 128, to_lane * 128 + 128)),
            )
        )
    return places


def last_piece_kernel(more_ref, edge_ref, base_edge_ref, out_ref):
    lon = place()[0]
    cols = more_ref.shape[1]
    for r in range(HALF):
        for at in range(0, cols, 2 * WIN):
            if at + 2 * WIN < cols:
                after = more_ref[r, at + 2 * WIN : at + 3 * WIN, :]
            else:
                after = edge_ref[HALF * (1 - lon) + r, :WIN, :]
            columns = window_columns(more_ref[r, at : at + 2 * WIN, :], after)
            out_ref[r * cols + at : r * cols + at + 2 * WIN, :] = columns.astype(BF16)
    widths = (base_edge_ref.shape[1], out_ref.shape[1])
    for (rows, lanes), (to_rows, to_lanes) in edge_blocks(base_edge_ref.shape[0], widths):
        at = slice(HALF * cols + to_rows.start, HALF * cols + to_rows.stop)
        out_ref[at, to_lanes] = base_edge_ref[rows, lanes]


def own_kernel(
    tok_hbm,
    edge_ref,
    gain_ref,
    wq_hbm,
    wkv_hbm,
    wout_hbm,
    wdec_hbm,
    state_hbm,
    high_hbm,
    low_hbm,
    qkv_ref,
    wdec_t_ref,
    wmix_t_ref,
    decoded_ref,
    wq_ref,
    wkv_ref,
    state_ref,
    high_ref,
    low_ref,
    more_ref,
    tok_ref,
    raw_ref,
    normed_ref,
    wdec_ref,
    wout_ref,
    sems,
):
    lon = place()[0]
    cols = tok_ref.shape[1]
    width = wq_ref.shape[0]
    keys, values = pl.ds(0, width), pl.ds(width, width)
    own_rows, give_rows = pl.ds(HALF * lon, HALF), pl.ds(HALF * (1 - lon), HALF)
    more = more_ref.shape[1]
    state_rows = pl.ds(pl.multiple_of(state_ref.shape[1] * lon, 8), state_ref.shape[1])
    copies = run_copies(
        sems,
        [
            (tok_hbm.at[own_rows], tok_ref),
            (wq_hbm, wq_ref),
            (wkv_hbm.at[:, keys], wkv_ref.at[:, keys]),
            (wkv_hbm.at[:, values], wkv_ref.at[:, values]),
            (wdec_hbm, wdec_ref),
            (wout_hbm, wout_ref),
            (state_hbm.at[:, state_rows, :], state_ref),
            (high_hbm, high_ref),
            (low_hbm, low_ref),
            (tok_hbm.at[give_rows, pl.ds(cols - more, more), :], more_ref),
        ],
    )

    def load(pair, r):
        at = pair * 2 * WIN
        if at + 2 * WIN < cols:
            after = tok_ref[r, at + 2 * WIN : at + 3 * WIN, :]
        else:
            after = edge_ref[HALF * lon + r, :WIN, :]
        return window_columns(tok_ref[r, at : at + 2 * WIN, :], after)

    copies[0].wait()
    place_tokens(load, cols, gain_ref[...], raw_ref, normed_ref)
    project(normed_ref, wq_ref, wkv_ref, qkv_ref, copies[1:4])
    outs = wdec_ref.shape[1]
    band = outs // PATCH
    channels = band // PATCH
    row = lax.broadcasted_iota(jnp.int32, (outs, 1), 0)
    source = (row % channels) * PATCH * PATCH + (row % band // channels) * PATCH + row // band
    pick = (lax.broadcasted_iota(jnp.int32, (outs, outs), 1) == source).astype(F32).astype(BF16)
    copies[4].wait()
    wdec_t_ref[...] = dot_nt(pick, wdec_ref[...]).astype(BF16)
    decoded_ref[...] = dot_nt(wdec_t_ref[...], raw_ref[...])
    copies[5].wait()
    wmix_t_ref[...] = dot_nt(wdec_t_ref[...], wout_ref[...]).astype(BF16)
    for copy in copies[6:]:
        copy.wait()


def main_kernel(first, x_ref, *refs):
    gain_ref, qkv_own_ref, decoded_own_ref, wq_ref, wkv_ref, wmix_ref, wdec_ref, *refs = refs
    keep_ref, send_ref, raw_ref, normed_ref, qkv_ref, att_ref, decoded_ref = refs
    width = raw_ref.shape[1]
    head_size = width // HEADS
    half_cells = HALF * WIN
    cells = 2 * half_cells
    lanes = 4 * head_size
    quads = HEADS // 4
    cols = raw_ref.shape[0] // HALF
    base = first * HALF
    group_cols = GROUP * WIN
    group_half = GROUP * half_cells

    def load(pair, r):
        at = pair * 2 * WIN
        if len(x_ref.shape) == 2:
            return x_ref[r * cols + at : r * cols + at + 2 * WIN, :].astype(F32)
        return x_ref[r, at : at + 2 * WIN, :].astype(F32)

    def iota(shape, dim):
        return lax.broadcasted_iota(jnp.int32, shape, dim)

    blocks = (iota((lanes, lanes), 0) // head_size == iota((lanes, lanes), 1) // head_size).astype(F32).astype(BF16)
    split_rows = iota((cells, 2 * cells), 0) // half_cells != iota((cells, 2 * cells), 1) % cells // half_cells
    bias = jnp.where(split_rows & place()[1], -1e30, 0.0)
    first_head = iota((cells, 2 * cells), 1) < cells
    scale = 1.0 / (math.sqrt(head_size) * math.log(2.0))

    def project_quad(quad):
        normed = normed_ref[...]
        at = quad * lanes
        for offset, weights in (
            (0, wq_ref[:, at : at + lanes]),
            (width, wkv_ref[:, at : at + lanes]),
            (2 * width, wkv_ref[:, width + at : width + at + lanes]),
        ):
            qkv_ref[:, offset + at : offset + at + lanes] = dot(normed, weights).astype(BF16)

    def part(window, quad, offset):
        columns = slice(offset + quad * lanes, offset + (quad + 1) * lanes)
        got = slice(window * half_cells, (window + 1) * half_cells)
        own = slice(base + got.start, base + got.stop)
        return jnp.concatenate([qkv_own_ref[own, columns], qkv_ref[got, columns]], axis=0)

    def score(window, quad):
        keys = jnp.concatenate([part(window, quad, width)] * 4, axis=0) * blocks
        return dot_nt(part(window, quad, 0), keys)

    def weigh(scores):
        outs = []
        for side in range(2):
            two = scores[:, side * 2 * cells : (side + 1) * 2 * cells] + bias
            left = jnp.max(jnp.where(first_head, two, -jnp.inf), axis=-1, keepdims=True)
            right = jnp.max(jnp.where(first_head, -jnp.inf, two), axis=-1, keepdims=True)
            peak = jnp.where(first_head, left, right)
            outs.append(jnp.exp2((two - peak) * scale).astype(BF16))
        return jnp.concatenate(outs, axis=1)

    def mix(group, quad, weights):
        sums = dot(jnp.concatenate(weights, axis=0), blocks)
        mixed = []
        for i in range(GROUP):
            values = jnp.concatenate([part(group * GROUP + i, quad, 2 * width)] * 4, axis=0) * blocks
            mixed.append(dot(weights[i], values) / sums[i * cells : (i + 1) * cells])
        tiles = [mixed[i][at : at + WIN] for at in range(0, cells, WIN) for i in range(GROUP)]
        rows = slice(group * 2 * group_half, (group + 1) * 2 * group_half)
        att_ref[rows, quad * lanes : (quad + 1) * lanes] = jnp.concatenate(tiles, axis=0).astype(BF16)

    def decode(group):
        rows = slice(group * 2 * group_half, (group + 1) * 2 * group_half)
        decoded = dot_nt(wmix_ref[...], att_ref[rows, :])
        got = slice(group * group_half, (group + 1) * group_half)
        own = slice(base + got.start, base + got.stop)
        band = decoded.shape[0] // PATCH
        out_lanes = slice(group * group_cols * PATCH, (group + 1) * group_cols * PATCH)
        lane_part = iota((band, group_half), 1) // group_cols
        for half, more, out_ref in ((0, decoded_own_ref[:, own], keep_ref), (1, decoded_ref[:, got], send_ref)):
            total = decoded[:, half * group_half : (half + 1) * group_half] + more
            from_b = [total[b * band : (b + 1) * band] for b in range(PATCH)]
            for r in range(HALF):
                placed = None
                for b in range(PATCH):
                    moved = from_b[b]
                    if b != r:
                        moved = pltpu.roll(moved, (b - r) % PATCH * group_cols, axis=1)
                    placed = moved if placed is None else jnp.where(lane_part == b, moved, placed)
                out_ref[r * band : (r + 1) * band, out_lanes] = placed.astype(BF16)

    place_tokens(load, cols, gain_ref[...], raw_ref, normed_ref)
    project_quad(0)
    units = [(group, quad) for group in range(cols // group_cols) for quad in range(quads)]
    weights = None
    for i in range(len(units) + 1):
        held = weights
        if i < len(units):
            group, quad = units[i]
            weights = []
            for w in range(GROUP):
                scores = score(group * GROUP + w, quad)
                if w == 1 and group == 0 and quad + 1 < quads:
                    project_quad(quad + 1)
                weights.append(weigh(scores))
            if i == 0:
                decoded_ref[...] = dot_nt(wdec_ref[...], raw_ref[...])
        if i > 0:
            mix(*units[i - 1], held)
            if units[i - 1][1] == quads - 1:
                decode(units[i - 1][0])

    lon = place()[0]
    total_rows = keep_ref.shape[0]
    edge = send_ref.shape[0] - total_rows
    near = pl.ds(pl.multiple_of(lon * (total_rows - edge), edge), edge)
    send_ref[total_rows:, :] = keep_ref[near, :]


def unfiltered(field, high_ref, low_ref, strength):
    high = field.astype(BF16)
    low = (field - high.astype(F32)).astype(BF16)
    smooth = dot(high, high_ref[...]) + (dot(high, low_ref[...]) + dot(low, high_ref[...]))
    return field - strength * smooth


def edge_kernel(state_ref, got_ref, nudge_ref, high_ref, low_ref, edge_ref, whole_ref):
    lon = place()[0]
    channels, own_rows, cols = got_ref.shape
    depth = edge_ref.shape[0] // channels
    own_lanes = pl.ds(pl.multiple_of(lon * cols, 128), cols)
    got_lanes = pl.ds(pl.multiple_of((1 - lon) * cols, 128), cols)
    near = pl.ds(pl.multiple_of(lon * (own_rows - 8), 8), 8)
    for ch in range(0, channels, 8):
        own = jnp.swapaxes(state_ref[ch : ch + 8, near, :], 0, 1)
        got = jnp.swapaxes(got_ref[ch : ch + 8, near, :], 0, 1)
        for i in range(depth):
            rows = slice(i * channels + ch, i * channels + ch + 8)
            whole_ref[rows, own_lanes] = jnp.where(lon == 0, own[i], own[8 - depth + i])
            whole_ref[rows, got_lanes] = jnp.where(lon == 0, got[i], got[8 - depth + i])
    strength = nudge_column(nudge_ref, depth * channels)
    edge_ref[...] = unfiltered(whole_ref[...], high_ref, low_ref, strength).astype(BF16)


def state_kernel(first, state_ref, got_ref, nudge_ref, high_ref, low_ref, out_ref, whole_ref):
    lon = place()[0]
    channels, own_rows, cols = got_ref.shape
    own_lanes = pl.ds(pl.multiple_of(lon * cols, 128), cols)
    got_lanes = pl.ds(pl.multiple_of((1 - lon) * cols, 128), cols)
    for y in range(0, out_ref.shape[0] // channels, 8):
        part = slice(first + y, first + y + 8)
        for ch in range(0, channels, 8):
            own = jnp.swapaxes(state_ref[ch : ch + 8, part, :], 0, 1)
            got = jnp.swapaxes(got_ref[ch : ch + 8, part, :], 0, 1)
            for i in range(8):
                rows = slice((y + i) * channels + ch, (y + i) * channels + ch + 8)
                whole_ref[rows, own_lanes] = own[i]
                whole_ref[rows, got_lanes] = got[i]
    step = PATCH * channels
    strength = nudge_column(nudge_ref, step)
    for at in range(0, out_ref.shape[0], step):
        out_ref[at : at + step, :] = unfiltered(whole_ref[at : at + step, :], high_ref, low_ref, strength)


def filter_rows(dec, first, high_ref, low_ref):
    rows = pl.ds(pl.multiple_of(first, 128), dec.shape[1])
    return dot(dec, high_ref[rows, :]) + dot(dec, low_ref[rows, :])


def early_kernel(upper_ref, lower_ref, piece_ref, nudge_ref, high_ref, low_ref, *refs):
    *refs, out_ref = refs
    keep_refs, send_refs = refs[: len(refs) // 2], refs[len(refs) // 2 :]
    lon = place()[0]
    half = upper_ref.shape[0]
    total = half + lower_ref.shape[0]
    edge = out_ref.shape[0] - total
    far = pl.ds(pl.multiple_of((1 - lon) * (total - edge), edge), edge)
    own = [jnp.concatenate([keep[...], send[far, :]], axis=0) for keep, send in zip(keep_refs, send_refs)]
    decoded = jnp.concatenate(own, axis=1)
    smooth = filter_rows(decoded, lon * (high_ref.shape[0] // 3), high_ref, low_ref)
    step = PATCH * nudge_ref.shape[1]
    strength = nudge_column(nudge_ref, step)
    for at in range(0, total, step):
        base_ref, begin = (upper_ref, at) if at < half else (lower_ref, at - half)
        out_ref[at : at + step, :] = base_ref[begin : begin + step, :] + strength * smooth[at : at + step]
    length, width = out_ref.shape[1], piece_ref.shape[1]
    first = piece_ref.shape[0] - edge * length // width
    for (rows, lanes), (at_rows, at_lanes) in edge_blocks(edge, (length, width)):
        base_edge = piece_ref[first + at_rows.start : first + at_rows.stop, at_lanes].astype(F32)
        term = strength[rows] * smooth[total + rows.start : total + rows.stop, lanes]
        out_ref[total + rows.start : total + rows.stop, lanes] = base_edge + term


def add_kernel(skip, early_ref, got_ref, nudge_ref, high_ref, low_ref, out_ref):
    smooth = filter_rows(got_ref[...], place()[0] * (high_ref.shape[0] // 3) + high_ref.shape[0] // 3 + skip, high_ref, low_ref)
    step = PATCH * nudge_ref.shape[1]
    strength = nudge_column(nudge_ref, step)
    for at in range(0, out_ref.shape[0], step):
        rows = slice(at, min(at + step, out_ref.shape[0]))
        out_ref[rows, :] = early_ref[rows, :] + strength[: rows.stop - at] * smooth[rows]


def last_rows(high_ref, got_ref):
    part = high_ref.shape[0] // 3
    return place()[0] * part + 2 * part - got_ref.shape[1]


def near_kernel(early_ref, got_ref, nudge_ref, high_ref, low_ref, near_ref):
    lon = place()[0]
    edge = near_ref.shape[0]
    total = early_ref.shape[0] - edge
    far = pl.ds(pl.multiple_of((1 - lon) * (total - edge), edge), edge)
    smooth = filter_rows(got_ref[far, :], last_rows(high_ref, got_ref), high_ref, low_ref)
    near_ref[...] = (early_ref[far, :] + nudge_column(nudge_ref, edge) * smooth).astype(BF16)


def row_tile(ref, row, var):
    at = row * (VARS * LEV) + var * LEV
    return pl.ds(at if isinstance(at, int) else pl.multiple_of(at, LEV), LEV)


def tendency_row(south, centre, north, use, only=range(VARS)):
    push_u, push_v = (0.5 * time_step) * centre(0), (0.5 * time_step) * centre(1)
    calm = diffusion * time_step
    to_east, to_west, to_north, to_south = calm - push_u, calm + push_u, calm - push_v, calm + push_v
    for var in only:
        field = centre(var)
        length = field.shape[1]
        step = to_east * pltpu.roll(field, length - 1, axis=1) + to_west * pltpu.roll(field, 1, axis=1)
        step = step + (to_north * north(var) + to_south * south(var))
        use(var, field, step - (4.0 * calm) * field)


def inner_kernel(early_ref, got_ref, nudge_ref, high_ref, low_ref, field_ref, lat_ref, first_ref, last_ref):
    total = field_ref.shape[0]
    edge = lat_ref.shape[0]
    rows = total // (VARS * LEV)
    step = PATCH * nudge_ref.shape[1]
    strength = nudge_column(nudge_ref, step)
    first_lane = last_rows(high_ref, got_ref)

    def smooth_rows(at, size):
        return filter_rows(got_ref[at : at + size, :], first_lane, high_ref, low_ref)

    def reader(ref, row):
        return lambda var: ref[row_tile(ref, row, var), :]

    def section(ref, row, use):
        tendency_row(reader(ref, row - 1), reader(ref, row), reader(ref, row + 1), use)

    def first_row(row):
        def put(var, field, step):
            first_ref[row_tile(first_ref, row, var), :] = field + step

        section(field_ref, row, put)

    def last_row(row):
        def put(var, field, step):
            nudged = field_ref[row_tile(field_ref, row, var), :]
            last_ref[row_tile(last_ref, row, var), :] = 0.5 * (nudged + field + step)

        section(first_ref, row, put)

    smooth = smooth_rows(0, step)
    next_first, next_last = 1, 2
    for at in range(0, total, step):
        field_ref[at : at + step, :] = early_ref[at : at + step, :] + strength * smooth
        if at + step < total:
            smooth = smooth_rows(at + step, step)
        else:
            smooth = smooth_rows(total, edge)
        ready = (at + step) // (VARS * LEV)
        while next_first <= min(rows - 2, ready - 2):
            first_row(next_first)
            next_first += 1
        while next_last <= min(rows - 3, next_first - 2):
            last_row(next_last)
            next_last += 1
    lat_ref[...] = early_ref[total:, :] + strength[:edge] * smooth


def outer_kernel(field_ref, first_ref, last_ref, lon_ref, lat_ref, out_hbm, ext_ref, edge_ref, out_ref, sems):
    channels, rows, length = out_ref.shape
    lon, pole = place()
    is_top = lon == 0
    from_lon = lon_ref[...].astype(F32)
    from_lat = jnp.where(pole, 0.0, lat_ref[...])
    edge = from_lon.shape[0]
    ext_ref[:edge, :] = jnp.where(is_top, from_lat, from_lon)
    ext_ref[edge:, :] = jnp.where(is_top, from_lon, from_lat)

    def field(row):
        def read(var):
            if row < 0:
                return ext_ref[row_tile(ext_ref, row + 2, var), :]
            if row >= rows:
                return ext_ref[row_tile(ext_ref, row - rows + 2, var), :]
            return field_ref[row_tile(field_ref, row, var), :]

        return read

    def first(row):
        def read(var):
            if row < 1:
                return edge_ref[row_tile(edge_ref, row + 1, var), :]
            if row >= rows - 1:
                return edge_ref[row_tile(edge_ref, row - rows + 3, var), :]
            return first_ref[row_tile(first_ref, row, var), :]

        return read

    outside = jnp.where(pole, 0.0, 1.0)
    for row in (-1, 0, rows - 1, rows):
        keep = None
        if row < 0:
            keep = jnp.where(is_top, outside, 1.0)
        if row >= rows:
            keep = jnp.where(is_top, 1.0, outside)

        def put(var, value, step):
            total = value + step
            at = row + 1 if row < 1 else row - rows + 3
            edge_ref[row_tile(edge_ref, at, var), :] = total if keep is None else total * keep

        tendency_row(field(row - 1), field(row), field(row + 1), put)
    copies = []
    for var in range(VARS):
        levels = slice(var * LEV, (var + 1) * LEV)
        outer = {}
        for row in (0, 1, rows - 2, rows - 1):

            def put(var, value, step):
                outer[row, var] = 0.5 * (field(row)(var) + value + step)

            tendency_row(first(row - 1), first(row), first(row + 1), put, [var])
        for y in range(0, rows, 8):
            block = []
            for row in range(y, y + 8):
                tile = outer[row, var] if (row, var) in outer else last_ref[row_tile(last_ref, row, var), :]
                block.append(tile[None])
            out_ref[levels, y : y + 8, :] = jnp.swapaxes(jnp.concatenate(block, axis=0), 0, 1)
        part = pl.ds(var * LEV, LEV)
        copies.append(pltpu.make_async_copy(out_ref.at[part], out_hbm.at[part], sems.at[var]))
        copies[-1].start()
    for copy in copies:
        copy.wait()


def work(micros):
    return pl.CostEstimate(flops=int(micros * 1e9), bytes_accessed=int(micros * 1e6), transcendentals=0)


def call(kernel, out_shape, n_in, scratch=(), vmem=24, micros=1.0):
    vmem_spec = pl.BlockSpec(memory_space=pltpu.VMEM)
    many = isinstance(out_shape, (tuple, list))
    return pl.pallas_call(
        kernel,
        out_shape=out_shape,
        in_specs=[vmem_spec] * n_in,
        out_specs=[vmem_spec] * len(out_shape) if many else vmem_spec,
        scratch_shapes=list(scratch),
        cost_estimate=work(micros),
        compiler_params=pltpu.CompilerParams(vmem_limit_bytes=vmem * MIB),
    )


def body(tokens, ln_gain, w_query, w_keyval, w_out, w_dec, nudge, state):
    tok_rows, tok_cols, width = tokens.shape
    channels, state_rows, state_cols = state.shape
    n_lat, n_lon = lax.axis_size("lat"), lax.axis_size("lon")
    lon = lax.axis_index("lon")
    total_cols = tok_cols * n_lon
    length = state_cols * n_lon
    band_rows = state_rows // n_lon
    both = ("lat", "lon")
    tokens_half = tok_cols * HALF
    band = band_rows * channels


    def at(row, col):
        return row * n_lon + col

    last = n_lat - 1
    swap = [(0, 1), (1, 0)]
    shift = [(at(i, 0), at(i + 1, 0)) for i in range(last)] + [(at(last, 0), at(last, 1))]
    shift += [(at(i, 1), at(i - 1, 1)) for i in range(1, n_lat)] + [(at(0, 1), at(0, 0))]
    meet = [(at(i, 1), at(i + 1, 0)) for i in range(last)] + [(at(i + 1, 0), at(i, 1)) for i in range(last)]
    meet_all = meet + [(at(0, 0), at(0, 0)), (at(last, 1), at(last, 1))]

    step = GROUP * WIN
    split = tok_cols - step
    chunks = [(0, split), (split, step)]

    hbm, vmem = pl.BlockSpec(memory_space=pltpu.HBM), pl.BlockSpec(memory_space=pltpu.VMEM)
    in_hbm = functools.partial(pltpu.with_memory_space_constraint, memory_space=pltpu.HBM)
    give, give_edge, give_state = pl.pallas_call(
        pack_kernel,
        out_shape=[
            pltpu.VMEM((HALF, split, width), BF16),
            pltpu.VMEM((tok_rows, 2 * WIN, width), BF16),
            pltpu.VMEM((channels, band_rows, state_cols), F32),
        ],
        in_specs=[hbm, hbm],
        out_specs=[vmem] * 3,
        scratch_shapes=[
            pltpu.VMEM((HALF, split + 2 * WIN, width), BF16),
            pltpu.SemaphoreType.DMA((3,)),
        ],
        compiler_params=pltpu.CompilerParams(vmem_limit_bytes=12 * MIB),
    )(in_hbm(tokens), in_hbm(state))
    got_tokens = [lax.ppermute(give, both, shift)]
    edge_tokens = lax.ppermute(give_edge, "lon", swap)
    got_state = lax.ppermute(give_state, "lon", swap)

    gain = ln_gain[None, :]
    nudge_row = nudge[None, :]
    matrix = zonal_filter(length, KEEP)
    high, low = (jnp.asarray(m) for m in split_high_low(matrix))
    order = decoded_order(total_cols, n_lon)
    order = np.concatenate([order[0], order[1], order[0]])
    dec_high, dec_low = (jnp.asarray(m) for m in split_high_low(matrix[order]))

    n_out = w_dec.shape[1]
    qkv_own, w_dec_t, w_mix_t, decoded_own, *weights, own_state, high, low, more = pl.pallas_call(
        own_kernel,
        out_shape=[
            pltpu.VMEM((tokens_half, 3 * width), BF16),
            pltpu.VMEM((n_out, width), BF16),
            pltpu.VMEM((n_out, width), BF16),
            pltpu.VMEM((n_out, tokens_half), F32),
            pltpu.VMEM(w_query.shape, BF16),
            pltpu.VMEM(w_keyval.shape, BF16),
            pltpu.VMEM((channels, band_rows, state_cols), F32),
            pltpu.VMEM((length, length), BF16),
            pltpu.VMEM((length, length), BF16),
            pltpu.VMEM((HALF, step, width), BF16),
        ],
        in_specs=[hbm, vmem, vmem] + [hbm] * 7,
        out_specs=[vmem] * 10,
        scratch_shapes=[
            pltpu.VMEM((HALF, tok_cols, width), BF16),
            pltpu.VMEM((tokens_half, width), BF16),
            pltpu.VMEM((tokens_half, width), BF16),
            pltpu.VMEM(w_dec.shape, BF16),
            pltpu.VMEM(w_out.shape, BF16),
            pltpu.SemaphoreType.DMA((10,)),
        ],
        cost_estimate=work(7.5),
        compiler_params=pltpu.CompilerParams(vmem_limit_bytes=32 * MIB),
    )(in_hbm(tokens), edge_tokens, gain, in_hbm(w_query), in_hbm(w_keyval), in_hbm(w_out), in_hbm(w_dec), in_hbm(state), in_hbm(high), in_hbm(low))

    edge_rows = 2 * channels
    got_state, qkv_own = lax.optimization_barrier((got_state, qkv_own))
    base_edge = call(
        edge_kernel,
        pltpu.VMEM((edge_rows, length), BF16),
        5,
        [pltpu.VMEM((edge_rows, length), F32)],
    )(own_state, got_state, nudge_row, high, low)
    their_base_edge = lax.ppermute(base_edge, "lon", swap)

    def state_half(first, rows):
        half = pltpu.VMEM((band // 2, length), F32)
        kernel = functools.partial(state_kernel, first)
        return call(kernel, half, 5, [half], micros=1.4)(rows, got_state, nudge_row, high, low)

    own_state, base_edge = lax.optimization_barrier((own_state, base_edge))
    upper = state_half(0, own_state)
    more, upper = lax.optimization_barrier((more, upper))
    last_rows = HALF * step + edge_rows * length // width
    last_piece = call(last_piece_kernel, pltpu.VMEM((last_rows, width), BF16), 3, vmem=12)(
        more, edge_tokens, their_base_edge
    )
    got_tokens.append(lax.ppermute(last_piece, both, shift))
    gain, last_piece = lax.optimization_barrier((gain, last_piece))

    keep, send, got = [], [], []
    for i, (first, cols) in enumerate(chunks):
        kept, sent = call(
            functools.partial(main_kernel, first),
            (pltpu.VMEM((band, cols * PATCH), BF16), pltpu.VMEM((band + edge_rows, cols * PATCH), BF16)),
            8,
            [
                pltpu.VMEM((cols * HALF, width), BF16),
                pltpu.VMEM((cols * HALF, width), BF16),
                pltpu.VMEM((cols * HALF, 3 * width), BF16),
                pltpu.VMEM((cols * WIN, width), BF16),
                pltpu.VMEM((n_out, cols * HALF), F32),
            ],
            micros=3.0 * (cols // step),
        )(got_tokens[i], gain, qkv_own, decoded_own, *weights, w_mix_t, w_dec_t)
        gain, kept, own_state = lax.optimization_barrier((gain, kept, own_state))
        keep.append(kept)
        send.append(sent)
        got.append(lax.ppermute(sent, both, meet_all))

    lower = state_half(band_rows // 2, own_state)
    sums = pltpu.VMEM((band + edge_rows, length), F32)
    early = call(early_kernel, sums, 6 + 2 * len(chunks), micros=1.2)(
        upper, lower, got_tokens[-1], nudge_row, dec_high, dec_low, *keep, *send
    )
    skip = 0
    for part in got[:-1]:
        early = call(functools.partial(add_kernel, skip), sums, 5)(early, part, nudge_row, dec_high, dec_low)
        skip += part.shape[1]
    late = (early, got[-1], nudge_row, dec_high, dec_low)
    to_lon = call(near_kernel, pltpu.VMEM((edge_rows, length), BF16), 5)(*late)
    from_lon = lax.ppermute(to_lon, "lon", swap)

    field = pltpu.VMEM((band, length), F32)
    edge = pltpu.VMEM((edge_rows, length), F32)
    nudged, from_lat, first, last_inner = call(inner_kernel, (field, edge, field, field), 5, micros=2.0)(*late)
    result = (channels, band_rows, length)
    return pl.pallas_call(
        outer_kernel,
        out_shape=jax.ShapeDtypeStruct(result, F32),
        in_specs=[vmem] * 5,
        out_specs=hbm,
        scratch_shapes=[
            pltpu.VMEM((2 * edge_rows, length), F32),
            pltpu.VMEM((2 * edge_rows, length), F32),
            pltpu.VMEM(result, F32),
            pltpu.SemaphoreType.DMA((VARS,)),
        ],
        cost_estimate=work(1.5),
        compiler_params=pltpu.CompilerParams(vmem_limit_bytes=24 * MIB),
    )(nudged, first, last_inner, from_lon, from_lat)


def solution(mesh):
    in_specs = (
        P(("member", "lat"), "lon", None),
        P(),
        P(),
        P(),
        P(),
        P(),
        P(),
        P(None, ("member", "lat"), "lon"),
    )
    out_specs = P(None, ("member", "lat", "lon"), None)
    return jax.shard_map(body, mesh=mesh, in_specs=in_specs, out_specs=out_specs, check_vma=False)
```
